512 devices in a mesh: lat: 128 (over x, z_lo, y), lon: 4 (over z_hi, core).
Axes of the slice: x: 4, y: 4, z: 16 (z_hi: 2, z_lo: 8; z = z_hi * 8 + z_lo), core: 2. Of those that a mesh axis runs over, the one named last changes fastest.
Arguments:
- tokens: bfloat16 [2, 768, 96, 192], P(None, 'lat', 'lon'), may hold values from -6 to 6
- mask_ids: int32 [2, 768, 96], P(None, 'lat', 'lon'), may hold values from 0 to 2
- pos_index: int32 [144, 144], replicated, may hold values from 0 to 3311
- norm_gain: float32 [192], replicated, may hold values from 0.1 to 1.9
- w_qkv: bfloat16 [192, 576], replicated, may hold values from -0.4375 to 0.4375
- w_proj: bfloat16 [192, 192], replicated, may hold values from -0.4375 to 0.4375
- earth_bias: float32 [128, 6, 3312], P('lat'), may hold values from -300 to 300, as said below
- d_out: bfloat16 [2, 768, 96, 192], P(None, 'lat', 'lon'), may hold values from -6 to 6
Outputs:
- updated: bfloat16 [2, 768, 96, 192], P(None, 'lat', 'lon')
- d_tokens: bfloat16 [2, 768, 96, 192], P(None, 'lat', 'lon')
- grad_qkv: float32 [192, 576], replicated
- grad_proj: float32 [192, 192], replicated
- grad_gain: float32 [192], replicated
- grad_bias: float32 [128, 6, 3312], P('lat')
The draws below stay inside these ranges and needn't reach their ends.
Inputs may be any that keep to these rules, and one draw needn't show every extreme that they name: `earth_bias`: the 2 levels form a single pressure window, so the bias is indexed by latitude window only.
All inputs are finite; a program needn't handle non-finite values.
Results may differ from the reference program's by a relative error of at most 0.019.
Values may be sent and summed in bfloat16 or wider, within the bound.
No kernel may reach another device: no remote copies, remote signals or barrier semaphores. Data moves between devices by JAX's collectives and lax.ppermute only.
A program may use at most 64 MiB of HBM per device.

```python
import jax
import jax.numpy as jnp
from jax import lax

C = 192
HEADS = 6
WPL = 2
WLAT = 6
WLON = 12
PL = 2
NLON = 96
NLAT = 768
NTYPES = 128
WIN = 144
NPOS = 3312
TOKENS = 147456


def draw_earth_bias(key, part):
    key = jax.random.fold_in(key, 7)
    key_base = jax.random.fold_in(key, 0)
    shape = (NTYPES, HEADS, NPOS)
    base = jnp.clip(jax.random.normal(key_base, shape, jnp.float32), -6.0, 6.0)
    return base


def touch_ends(array, own_key, least, high):
    dims = array.shape
    index_at = [jax.random.randint(jax.random.fold_in(own_key, axis), (), 0, dims[axis]) for axis in range(len(dims))]
    array = array.at[tuple(index_at)].set(least)
    longest = dims.index(max(dims))
    index_at[longest] = (index_at[longest] + 1) % dims[longest]
    return array.at[tuple(index_at)].set(high)


def shard_levels(rng, dims, pieces, least, top_value):
    gain, own = 1.0, jax.random.fold_in(rng, 6)
    for axis_at, blocks in pieces:
        heights = jnp.exp(jax.random.uniform(jax.random.fold_in(own, axis_at), (blocks,), jnp.float32, least / len(pieces), top_value / len(pieces)))
        gain = gain * jnp.repeat(heights, dims[axis_at] // blocks).reshape([-1 if axis == axis_at else 1 for axis in range(len(dims))])
    return gain


def scatter_about(rng, dims, width, limit, shards=(), held_as=jnp.bfloat16):
    array = jax.random.normal(rng, dims, jnp.float32) * width
    if len(shards) > 0:
        array = shard_levels(rng, dims, shards, -0.22, 0.18) * array
    return jnp.clip(array, min=-limit, max=limit).astype(held_as)


def setup_inputs(seed: int = 0) -> dict:
    keys = jax.random.split(jax.random.key(seed), 9)
    return {
        "tokens": scatter_about(keys[0], (PL, NLAT, NLON, C), 1.0, 6.0, ((1, 128), (2, 4))),
        "mask_ids": touch_ends(jax.random.randint(keys[1], (PL, NLAT, NLON), 0, 3), jax.random.fold_in(keys[1], 1), 0, 2).astype(jnp.int32),
        "pos_index": touch_ends(jax.random.randint(keys[2], (WIN, WIN), 0, NPOS), jax.random.fold_in(keys[2], 1), 0, NPOS - 1).astype(jnp.int32),
        "norm_gain": jnp.clip(1.0 + 0.18 * jax.random.normal(keys[3], (C,), jnp.float32), 0.1, 1.9),
        "w_qkv": scatter_about(keys[4], (C, 3 * C), C ** -0.5, 0.4375),
        "w_proj": scatter_about(keys[5], (C, C), C ** -0.5, 0.4375),
        "earth_bias": draw_earth_bias(jax.random.fold_in(keys[8], 71), 0),
        "d_out": scatter_about(keys[7], (PL, NLAT, NLON, C), 1.0, 6.0, ((1, 128), (2, 4))),
    }


epsilon = 1e-05

def normalize(field, norm_gain):
    values = field.astype(jnp.float32)
    center = lax.optimization_barrier(jnp.mean(values, axis=-1, keepdims=True))
    spread = lax.optimization_barrier(jnp.mean((values - center) ** 2, axis=-1, keepdims=True))
    return ((values - center) * lax.rsqrt(spread + epsilon) * norm_gain).astype(jnp.bfloat16)

def windowed(field):
    levels, row_count, col_count, channels = field.shape
    blocked = field.reshape(levels, row_count // WLAT, WLAT, col_count // WLON, WLON, channels)
    blocked = blocked.transpose(1, 3, 0, 2, 4, 5)
    return blocked.reshape(row_count // WLAT, col_count // WLON, levels * WLAT * WLON, channels)

def unwindow(blocked, levels):
    lat_win, lon_win, entries, channels = blocked.shape
    field = blocked.reshape(lat_win, lon_win, levels, WLAT, WLON, channels)
    return field.transpose(2, 0, 3, 1, 4, 5).reshape(levels, lat_win * WLAT, lon_win * WLON, channels)

def attend(packed, region, table, pos_index):
    levels = packed.shape[0]
    channels = packed.shape[3] // 3
    head_count = table.shape[1]
    head_size = channels // head_count
    blocks = windowed(packed)
    lat_win, lon_win, entries, packed_width = blocks.shape
    split = blocks.reshape(lat_win, lon_win, entries, 3, head_count, head_size)
    queries = split[:, :, :, 0].astype(jnp.float32)
    keyset = split[:, :, :, 1].astype(jnp.float32)
    values = split[:, :, :, 2].astype(jnp.float32)
    scores = jnp.einsum('abqhd,abkhd->abhqk', queries, keyset) * head_size ** (-0.5)
    scores = scores + table[:, :, pos_index][:, None]
    labels = windowed(region[..., None])[..., 0]
    same = labels[:, :, None, :, None] == labels[:, :, None, None, :]
    scores = jnp.where(same, scores, -1000000000.0)
    largest = lax.stop_gradient(lax.optimization_barrier(jnp.max(scores, axis=-1, keepdims=True)))
    expo = jnp.exp(scores - largest)
    weights = (expo / lax.optimization_barrier(jnp.sum(expo, axis=-1, keepdims=True))).astype(jnp.bfloat16)
    mixed = jnp.einsum('abhqk,abkhd->abqhd', weights.astype(jnp.float32), values).astype(jnp.bfloat16)
    return unwindow(mixed.reshape(lat_win, lon_win, entries, channels), levels)

def reference(tokens, mask_ids, pos_index, norm_gain, w_qkv, w_proj, earth_bias, d_out):
    forward_shift = (-(WPL // 2), -(WLAT // 2), -(WLON // 2))
    back_shift = (WPL // 2, WLAT // 2, WLON // 2)
    rolled = jnp.roll(tokens, forward_shift, (0, 1, 2))
    d_rolled_in = jnp.roll(d_out, forward_shift, (0, 1, 2))
    channels = tokens.shape[3]

    def band_step(totals, band_index):
        row_start = band_index * WLAT
        part_x = lax.dynamic_slice_in_dim(rolled, row_start, WLAT, 1)
        part_region = lax.dynamic_slice_in_dim(mask_ids, row_start, WLAT, 1)
        part_dout = lax.dynamic_slice_in_dim(d_rolled_in, row_start, WLAT, 1)
        part_bias = lax.dynamic_slice_in_dim(earth_bias, band_index, 1, 0)
        normed, norm_back = jax.vjp(normalize, part_x, norm_gain)
        flat_normed = normed.reshape(-1, channels)
        packed = jnp.dot(flat_normed, w_qkv, preferred_element_type=jnp.float32).astype(jnp.bfloat16)
        packed = packed.reshape(normed.shape[:3] + (3 * channels,))
        mixed, attend_back = jax.vjp(lambda first, second: attend(first, part_region, second, pos_index), packed, part_bias)
        flat_mixed = mixed.reshape(-1, channels)
        proj = jnp.dot(flat_mixed, w_proj, preferred_element_type=jnp.float32).astype(jnp.bfloat16)
        flat_dproj = part_dout.reshape(-1, channels)
        grad_proj = jnp.dot(flat_mixed.T, flat_dproj, preferred_element_type=jnp.float32)
        d_mixed = jnp.dot(flat_dproj, w_proj.T, preferred_element_type=jnp.float32).astype(jnp.bfloat16)
        d_packed, d_table = attend_back(d_mixed.reshape(mixed.shape))
        flat_dpacked = d_packed.reshape(-1, 3 * channels)
        grad_qkv = jnp.dot(flat_normed.T, flat_dpacked, preferred_element_type=jnp.float32)
        d_normed = jnp.dot(flat_dpacked, w_qkv.T, preferred_element_type=jnp.float32).astype(jnp.bfloat16)
        d_rolled, d_gain = norm_back(d_normed.reshape(normed.shape))
        new_totals = (totals[0] + grad_qkv, totals[1] + grad_proj, totals[2] + d_gain)
        return (new_totals, (proj.reshape(part_x.shape), d_rolled, d_table[0]))
    start_totals = (jnp.zeros((channels, 3 * channels), jnp.float32), jnp.zeros((channels, channels), jnp.float32), jnp.zeros((channels,), jnp.float32))
    totals, stacked = lax.scan(band_step, start_totals, jnp.arange(NTYPES, dtype=jnp.int32))
    proj_all = stacked[0].transpose(1, 0, 2, 3, 4).reshape(tokens.shape)
    d_rolled_all = stacked[1].transpose(1, 0, 2, 3, 4).reshape(tokens.shape)
    updated = (tokens.astype(jnp.float32) + jnp.roll(proj_all, back_shift, (0, 1, 2)).astype(jnp.float32)).astype(jnp.bfloat16)
    d_tokens = (d_out.astype(jnp.float32) + jnp.roll(d_rolled_all, back_shift, (0, 1, 2)).astype(jnp.float32)).astype(jnp.bfloat16)
    scale = float(TOKENS) ** (-0.5)
    return (updated, d_tokens, totals[0] * scale, totals[1] * scale, totals[2] * scale, stacked[2])
```

```python
import jax
import jax.numpy as jnp
import numpy as np
from jax import lax
from jax.experimental import pallas as pl
from jax.experimental.pallas import tpu as pltpu
from jax.sharding import PartitionSpec as P

BF = jnp.bfloat16
F32 = jnp.float32

WPL, WLAT, WLON = 2, 6, 12
HALF_LAT, HALF_LON = WLAT // 2, WLON // 2
ROWS, COLS = 6, 24
C = 192
HEADS = 6
HEAD = C // HEADS
WIN = WPL * WLAT * WLON
WINDOWS = COLS // WLON
NPOS = 3312
HI = -(-NPOS // 128)
HIP = 32
EDGE = 8
N_OWN = WPL * ROWS * COLS
N_LAT = WPL * HALF_LAT * COLS
N_EDGE = WPL * HALF_LAT * EDGE
N_ALL = N_OWN + N_LAT + 2 * N_EDGE
MAIN = 128
REST = WIN - MAIN
PAIRS = HEADS * MAIN + 128
EPS = 1e-05
SCALE = HEAD**-0.5
NEG = -1000000000.0
G_ROWS = 1280
VMEM_LIMIT = 48 * 1024 * 1024

SPLIT = (4, 8, 4, 2, 2)
AXES = ("x", "zl", "y", "zh", "c")
LAT_AXES = ("x", "zl", "y")
LON_AXES = ("zh", "c")
PLANE = ("x", "y", "c")
LINE = ("zh", "zl")


def source_rows():
    at = np.zeros((WINDOWS, WIN), np.int32)
    for level in range(WPL):
        for row in range(ROWS):
            for col in range(COLS):
                from_level = (level + WPL // 2) % WPL
                r, c = row + HALF_LAT, col + HALF_LON
                if r < ROWS and c < COLS:
                    src = from_level * ROWS * COLS + r * COLS + c
                elif c < COLS:
                    src = N_OWN + from_level * HALF_LAT * COLS + (r - ROWS) * COLS + c
                elif r < ROWS:
                    src = N_OWN + N_LAT + from_level * HALF_LAT * EDGE + (r - HALF_LAT) * EDGE + c - COLS
                else:
                    src = N_OWN + N_LAT + N_EDGE + from_level * HALF_LAT * EDGE + (r - ROWS) * EDGE + c - COLS
                at[col // WLON, level * WLAT * WLON + row * WLON + col % WLON] = src
    return at


def constants():
    at = source_rows()
    pick = np.zeros((WINDOWS, WIN, N_ALL), np.float32)
    for w in range(WINDOWS):
        pick[w, np.arange(WIN), at[w]] = 1.0
    back = pick.transpose(0, 2, 1)
    spread = np.zeros((256, WIN), np.float32)
    for lane in range(MAIN):
        spread[lane, lane] = 1.0
    for lane in range(HEADS * REST):
        spread[MAIN + lane, MAIN + lane % REST] = 1.0
    return pick.astype(BF), back.astype(BF), spread.astype(BF)


def dot(a, b, dims):
    return lax.dot_general(a, b, ((dims[:1], dims[1:]), ((), ())), preferred_element_type=F32)


def nn(a, b):
    return dot(a, b, (1, 0))


def nt(a, b):
    return dot(a, b, (1, 1))


def eye(n):
    return (lax.broadcasted_iota(jnp.int32, (n, n), 0) == lax.broadcasted_iota(jnp.int32, (n, n), 1)).astype(F32).astype(BF)


def cut_kernel(tokens, d_out, lat, lon, diag):
    for i, ref in enumerate((tokens, d_out)):
        top = ref[:, :HALF_LAT]
        lat[i] = top
        diag[i] = top[:, :, :EDGE]
        lon[i] = ref[:, HALF_LAT:, :, :][:, :, :EDGE]


def tables_kernel(pos, table, spread, w_qkv, w_proj, mask, bias, hi_out, lo_out, w3, w3t, wpt, blocked, lo_scr):
    one = eye(WIN)
    idx = pos[...]
    hi = lax.shift_right_logical(idx, 7)
    lo = lax.bitwise_and(idx, 127)
    sp = spread[...]
    hi2 = nt(nt(one, hi.astype(F32).astype(BF)).astype(BF), sp)
    lo2 = nt(nt(one, lo.astype(F32).astype(BF)).astype(BF), sp)
    hi2 = hi2.astype(jnp.int32)
    lo2 = lo2.astype(jnp.int32)
    hi_out[...] = hi2
    lo_out[...] = lo2

    def step(block, carry):
        rows = pl.ds(pl.multiple_of(block * 8, 8), 8)
        lane = lax.broadcasted_iota(jnp.int32, (8, 128), 1)
        for tile in range(2):
            cols = pl.ds(tile * 128, 128)
            h_idx = hi_out[rows, cols]
            l_idx = lo_out[rows, cols]
            if tile == 0:
                acc = [jnp.zeros((8, 128), F32) for _ in range(HEADS)]
            else:
                acc = [jnp.zeros((8, 128), F32)]
            for part in range(HI):
                width = min(128, NPOS - part * 128)
                hit = h_idx == part
                for head in range(HEADS):
                    row = jnp.broadcast_to(lo_scr[head : head + 1, pl.ds(part * 128, 128)], (8, 128))
                    got = jnp.take_along_axis(row, l_idx, axis=1, mode="promise_in_bounds")
                    if tile == 0:
                        acc[head] = jnp.where(hit, got, acc[head])
                    else:
                        mine = hit & (lax.shift_right_logical(lane, 4) == head)
                        acc[0] = jnp.where(mine, got, acc[0])
            if tile == 0:
                for head in range(HEADS):
                    bias[rows, pl.ds(head * MAIN, 128)] = acc[head]
            else:
                bias[rows, pl.ds(HEADS * MAIN, 128)] = acc[0]
        return carry

    lo_scr[:, : HI * 128] = jnp.zeros((HEADS, HI * 128), F32)
    lo_scr[:, :NPOS] = table[0]
    lax.fori_loop(0, WIN // 8, step, 0)

    one = eye(C)
    for i in range(3):
        w = w_qkv[:, C * i : C * (i + 1)]
        w3[i] = w
        w3t[i] = nt(one, w).astype(BF)
    wpt[...] = nt(one, w_proj[...]).astype(BF)

    lab = mask[...].astype(F32).reshape(WPL * ROWS, COLS).astype(BF)
    for w in range(WINDOWS):
        lane = lax.broadcasted_iota(jnp.int32, (COLS, WIN), 1)
        col = lax.broadcasted_iota(jnp.int32, (COLS, WIN), 0)
        across = (lax.rem(lane, WLON) + w * WLON == col).astype(F32).astype(BF)
        wide = nn(lab, across)
        r = lax.broadcasted_iota(jnp.int32, (WPL * ROWS, WIN), 0)
        a = lax.broadcasted_iota(jnp.int32, (WPL * ROWS, WIN), 1)
        row = jnp.sum(jnp.where(lax.div(a, WLON) == r, wide, 0.0), axis=0, keepdims=True)
        row = jnp.broadcast_to(row, (WIN, WIN)).astype(BF)
        down = nt(eye(WIN), row)
        over = nt(row, sp)
        blocked[w] = jnp.where(over == jnp.broadcast_to(down[:, :1], (WIN, 256)), 0.0, NEG)


def by_head(x):
    lane = lax.broadcasted_iota(jnp.int32, (1, C), 1)
    keep = [((lane >= HEAD * h) & (lane < HEAD * (h + 1))).astype(F32).astype(BF) for h in range(HEADS)]
    parts = [x[:MAIN] * keep[h] for h in range(HEADS)]
    parts += [x[MAIN:] * keep[h] for h in range(HEADS)]
    parts.append(jnp.zeros((PAIRS - HEADS * WIN, C), BF))
    return jnp.concatenate(parts, axis=0)


def heads_apart(left, right, scale):
    main = [
        nn(left[HEAD * h : HEAD * (h + 1)], right[:, MAIN * h : MAIN * (h + 1)]) for h in range(HEADS)
    ]
    main = (jnp.concatenate(main, axis=0) * scale).astype(BF)
    rest = nn(left, right[:, HEADS * MAIN :]) * scale
    row = lax.broadcasted_iota(jnp.int32, (C, 128), 0)
    lane = lax.broadcasted_iota(jnp.int32, (C, 128), 1)
    rest = jnp.where(lax.div(row, HEAD) == lax.div(lane, REST), rest, 0.0).astype(BF)
    fold_l = lax.broadcasted_iota(jnp.int32, (128, REST), 0)
    fold_a = lax.broadcasted_iota(jnp.int32, (128, REST), 1)
    fold = (lax.rem(fold_l, REST) == fold_a).astype(F32).astype(BF)
    rest = nn(rest, fold).astype(BF)
    return jnp.concatenate([main, rest], axis=1)


def block_kernel(
    own_x, own_d, lat, lon, diag, pick, back, gain, w3, w3t, wp, wpt, bias, blocked,
    base_x, base_d, out_lat, out_lon, out_diag, grads, d_bias,
):
    x_all = jnp.concatenate([own_x[...], lat[0], lon[0], diag[0]], axis=0)
    d_all = jnp.concatenate([own_d[...], lat[1], lon[1], diag[1]], axis=0)
    eye_c = eye(C)
    eye_w = eye(WIN)
    g = gain[...]
    sums = [jnp.zeros((C, C), F32) for _ in range(4)]
    d_gain = jnp.zeros((C, 1), F32)
    x_back = jnp.zeros((N_ALL, C), F32)
    d_back = jnp.zeros((N_ALL, C), F32)
    for w in range(WINDOWS):
        x = nn(pick[w], x_all).astype(BF)
        d_proj = nn(pick[w], d_all).astype(BF)
        xt = nt(eye_c, x)
        mean = jnp.sum(xt, axis=0, keepdims=True) * (1.0 / C)
        centered = xt - mean
        var = jnp.sum(centered * centered, axis=0, keepdims=True) * (1.0 / C)
        rstd = lax.rsqrt(var + EPS)
        xhat = centered * rstd
        nt_w = (xhat * g).astype(BF)
        n_w = nt(eye_w, nt_w).astype(BF)
        q = nn(n_w, w3[0]).astype(BF)
        k = nn(n_w, w3[1]).astype(BF)
        v = nn(n_w, w3[2]).astype(BF)
        kt = nn(w3t[1], nt_w).astype(BF)
        vt = nn(w3t[2], nt_w).astype(BF)
        qm = by_head(q)
        dm = by_head(nt(d_proj, wp[...]).astype(BF))
        far = jnp.concatenate([blocked[w, :, :MAIN]] * HEADS + [blocked[w, :, MAIN:]], axis=1)
        s = nt(k, qm) * SCALE + bias[...] + far
        e = jnp.exp(s - jnp.max(s, axis=0, keepdims=True))
        p = e * (1.0 / jnp.sum(e, axis=0, keepdims=True))
        attn = p.astype(BF)
        d_attn = nt(v, dm)
        pd = p * d_attn
        ds = pd - p * jnp.sum(pd, axis=0, keepdims=True)
        dsb = ds.astype(BF)
        if w == 0:
            d_bias[...] = ds
        else:
            d_bias[...] += ds
        mixed_t = heads_apart(vt, attn, 1.0)
        dq_t = heads_apart(kt, dsb, SCALE)
        dk = (nn(dsb, qm) * SCALE).astype(BF)
        dv = nn(attn, dm).astype(BF)
        proj_t = nn(wpt[...], mixed_t).astype(BF)
        x_back = x_back + nt(back[w], proj_t)
        sums[0] = sums[0] + nt(nt_w, dq_t)
        sums[1] = sums[1] + nn(nt_w, dk)
        sums[2] = sums[2] + nn(nt_w, dv)
        sums[3] = sums[3] + nn(mixed_t, d_proj)
        dn = nn(w3[0], dq_t) + nt(w3[1], dk) + nt(w3[2], dv)
        dn = dn.astype(BF).astype(F32)
        d_gain = d_gain + jnp.sum(dn * xhat, axis=1, keepdims=True)
        dy = dn * g
        m1 = jnp.sum(dy, axis=0, keepdims=True) * (1.0 / C)
        m2 = jnp.sum(dy * xhat, axis=0, keepdims=True) * (1.0 / C)
        dx = (rstd * (dy - m1 - xhat * m2)).astype(BF)
        d_back = d_back + nt(back[w], dx)
    for i in range(4):
        grads[C * i : C * (i + 1), :] = sums[i][:, :128].astype(BF)
    for i in range(2):
        pair = jnp.concatenate([sums[2 * i][:, 128:], sums[2 * i + 1][:, 128:]], axis=1)
        grads[C * (4 + i) : C * (5 + i), :] = pair.astype(BF)
    lane = lax.broadcasted_iota(jnp.int32, (128, 128), 1)
    tail = jnp.concatenate([d_gain[128:], jnp.zeros((256 - C, 1), F32)], axis=0)
    both = jnp.where(lane == 0, d_gain[:128], jnp.where(lane == 1, tail, 0.0))
    grads[6 * C :, :] = both.astype(BF)
    for i, (total, own, base) in enumerate(((x_back, own_x, base_x), (d_back, own_d, base_d))):
        base[...] = (own[...].astype(F32) + total[:N_OWN]).astype(BF)
        out_lat[i] = total[N_OWN : N_OWN + N_LAT].astype(BF)
        out_lon[i] = total[N_OWN + N_LAT : N_OWN + N_LAT + N_EDGE].astype(BF)
        out_diag[i] = total[N_OWN + N_LAT + N_EDGE :].astype(BF)


def scatter_kernel(d_bias, hi, lo, out, acc):
    acc[...] = jnp.zeros_like(acc)

    def step(block, carry):
        rows = pl.ds(pl.multiple_of(block * 8, 8), 8)
        h_all = hi[rows, :]
        l_all = lo[rows, :]
        d_all = d_bias[rows, :]
        part = lax.broadcasted_iota(jnp.int32, (HIP, 256), 0)
        group = lax.shift_right_logical(lax.broadcasted_iota(jnp.int32, (HIP, 128), 1), 4)
        place = lax.broadcasted_iota(jnp.int32, (128, 256), 0)
        total = acc[...]
        for i in range(8):
            hit = jnp.broadcast_to(h_all[i : i + 1], (HIP, 256)) == part
            rest = jnp.broadcast_to(d_all[i : i + 1, HEADS * MAIN :], (HIP, 128))
            rest = jnp.where(hit[:, 128:], rest, 0.0)
            many = []
            for head in range(HEADS):
                main = jnp.broadcast_to(d_all[i : i + 1, MAIN * head : MAIN * (head + 1)], (HIP, 128))
                main = jnp.where(hit[:, :128], main, 0.0)
                many.append(jnp.concatenate([main, jnp.where(group == head, rest, 0.0)], axis=1))
            many = jnp.concatenate(many, axis=0).astype(BF)
            spot = (jnp.broadcast_to(l_all[i : i + 1], (128, 256)) == place).astype(F32).astype(BF)
            total = total + nt(many, spot)
        acc[...] = total
        return carry

    lax.fori_loop(0, WIN // 8, step, 0)
    out[...] = acc[...].astype(BF)


def finish_kernel(base_x, base_d, lat, lon, diag, tabs, out_x, out_d, out_t):
    for i, (base, out) in enumerate(((base_x, out_x), (base_d, out_d))):
        a = base[...].astype(F32)
        edge = jnp.concatenate([diag[i].astype(F32), lon[i].astype(F32)], axis=1)
        pad = jnp.zeros((WPL, ROWS, COLS - EDGE, C), F32)
        far = jnp.concatenate([lat[i].astype(F32), jnp.zeros((WPL, HALF_LAT, COLS, C), F32)], axis=1)
        out[...] = (a + jnp.concatenate([edge, pad], axis=2) + far).astype(BF)
    t = jnp.sum(tabs[...].astype(F32), axis=0)
    for part in range(HI):
        width = min(128, NPOS - part * 128)
        for head in range(HEADS):
            row = head * HIP + part
            out_t[0, head : head + 1, part * 128 : part * 128 + width] = t[row : row + 1, :width]


def unpack_kernel(g, scale, qkv, proj, gain):
    k = scale
    full = [g[C * i : C * (i + 1), :].astype(F32) * k for i in range(6)]
    qkv[:, 0:128] = full[0]
    qkv[:, 128:256] = jnp.concatenate([full[4][:, :64], full[1][:, :64]], axis=1)
    qkv[:, 256:384] = jnp.concatenate([full[1][:, 64:], full[4][:, 64:]], axis=1)
    qkv[:, 384:512] = full[2]
    qkv[:, 512:576] = full[5][:, :64]
    proj[:, 0:128] = full[3]
    proj[:, 128:192] = full[5][:, 64:]
    gain[...] = g[6 * C :, :].astype(F32) * k


def call(kernel, out_shape, *args, scratch=(), cost=(0, 0)):
    return pl.pallas_call(
        kernel,
        out_shape=out_shape,
        scratch_shapes=list(scratch),
        compiler_params=pltpu.CompilerParams(vmem_limit_bytes=VMEM_LIMIT),
        cost_estimate=pl.CostEstimate(flops=cost[0], bytes_accessed=cost[1], transcendentals=0),
    )(*args)


def sds(shape, dtype):
    return jax.ShapeDtypeStruct(shape, dtype)


def make(sizes):
    n_lat = sizes[0] * sizes[1] * sizes[2]
    n_lon = sizes[3] * sizes[4]
    n_plane = sizes[0] * sizes[2] * sizes[4]
    n_line = sizes[1] * sizes[3]
    piece = G_ROWS // n_plane

    def route(d_lat, d_lon):
        return [
            (a * n_lon + b, (a + d_lat) % n_lat * n_lon + (b + d_lon) % n_lon)
            for a in range(n_lat)
            for b in range(n_lon)
        ]

    def per_device(tokens, mask_ids, pos_index, norm_gain, w_qkv, w_proj, earth_bias, d_out):
        pick, back, spread = (jnp.asarray(c) for c in constants())
        lat, lon, diag = call(
            cut_kernel,
            (
                sds((2, WPL, HALF_LAT, COLS, C), BF),
                sds((2, WPL, HALF_LAT, EDGE, C), BF),
                sds((2, WPL, HALF_LAT, EDGE, C), BF),
            ),
            tokens,
            d_out,
        )
        lat = lax.ppermute(lat, AXES, route(-1, 0))
        lon = lax.ppermute(lon, AXES, route(0, -1))
        diag = lax.ppermute(diag, AXES, route(-1, -1))
        bias, hi, lo, w3, w3t, wpt, blocked = call(
            tables_kernel,
            (
                sds((WIN, PAIRS), F32),
                sds((WIN, 256), jnp.int32),
                sds((WIN, 256), jnp.int32),
                sds((3, C, C), BF),
                sds((3, C, C), BF),
                sds((C, C), BF),
                sds((WINDOWS, WIN, 256), F32),
            ),
            pos_index,
            earth_bias,
            spread,
            w_qkv,
            w_proj,
            mask_ids,
            scratch=[pltpu.VMEM((HEADS, HI * 128), F32)],
            cost=(10**9, 10**6),
        )
        base_x, base_d, out_lat, out_lon, out_diag, grads, d_bias = call(
            block_kernel,
            (
                sds((N_OWN, C), BF),
                sds((N_OWN, C), BF),
                sds((2, N_LAT, C), BF),
                sds((2, N_EDGE, C), BF),
                sds((2, N_EDGE, C), BF),
                sds((G_ROWS, 128), BF),
                sds((WIN, PAIRS), F32),
            ),
            tokens.reshape(N_OWN, C),
            d_out.reshape(N_OWN, C),
            lat.reshape(2, N_LAT, C),
            lon.reshape(2, N_EDGE, C),
            diag.reshape(2, N_EDGE, C),
            pick,
            back,
            norm_gain.reshape(C, 1),
            w3,
            w3t,
            w_proj,
            wpt,
            bias,
            blocked,
        )
        parts = lax.all_to_all(grads.reshape(n_plane, piece, 128), PLANE, 0, 0)
        part = jnp.sum(parts.astype(F32), axis=0).astype(BF)
        line = lax.all_gather(part, LINE)

        table = call(
            scatter_kernel,
            sds((HEADS * HIP, 128), BF),
            d_bias,
            hi,
            lo,
            scratch=[pltpu.VMEM((HEADS * HIP, 128), F32)],
        )
        tabs = lax.all_to_all(jnp.broadcast_to(table, (n_lon,) + table.shape), LON_AXES, 0, 0)
        out_lat = lax.ppermute(out_lat, AXES, route(1, 0))
        out_diag = lax.ppermute(out_diag, AXES, route(1, 1))
        out_lon = lax.ppermute(out_lon, AXES, route(0, 1))
        updated, d_tokens, d_table = call(
            finish_kernel,
            (
                sds((WPL, ROWS, COLS, C), BF),
                sds((WPL, ROWS, COLS, C), BF),
                sds((1, HEADS, NPOS), F32),
            ),
            base_x.reshape(WPL, ROWS, COLS, C),
            base_d.reshape(WPL, ROWS, COLS, C),
            out_lat.reshape(2, WPL, HALF_LAT, COLS, C),
            out_lon.reshape(2, WPL, HALF_LAT, EDGE, C),
            out_diag.reshape(2, WPL, HALF_LAT, EDGE, C),
            tabs,
        )
        total = jnp.sum(line.astype(F32), axis=0).astype(BF)
        whole = lax.all_to_all(jnp.broadcast_to(total, (n_plane,) + total.shape), PLANE, 0, 0)
        scale = float(n_lat * n_lon * N_OWN) ** -0.5
        qkv, proj, gain = call(
            lambda g, a, b, c: unpack_kernel(g, scale, a, b, c),
            (sds((C, 3 * C), F32), sds((C, C), F32), sds((128, 128), F32)),
            whole.reshape(G_ROWS, 128),
        )
        gain = jnp.concatenate([gain[:, 0], gain[: C - 128, 1]])
        return updated, d_tokens, qkv, proj, gain, d_table

    return per_device


def solution(mesh):
    fine = jax.sharding.Mesh(mesh.devices.reshape(SPLIT), AXES)
    placed = (
        P(None, LAT_AXES, LON_AXES, None),
        P(None, LAT_AXES, LON_AXES),
        P(),
        P(),
        P(),
        P(),
        P(LAT_AXES, None, None),
        P(None, LAT_AXES, LON_AXES, None),
    )
    return jax.shard_map(
        make(SPLIT),
        mesh=fine,
        in_specs=placed,
        out_specs=(
            P(None, LAT_AXES, LON_AXES, None),
            P(None, LAT_AXES, LON_AXES, None),
            P(),
            P(),
            P(),
            P(LAT_AXES, None, None),
        ),
        check_vma=False,
    )
```

```python
import jax
import jax.numpy as jnp
import numpy as np
from jax import lax
from jax.experimental import pallas as pl
from jax.experimental.pallas import tpu as pltpu
from jax.sharding import PartitionSpec as P

BF = jnp.bfloat16
F32 = jnp.float32

WPL, WLAT, WLON = 2, 6, 12
HALF_LAT, HALF_LON = WLAT // 2, WLON // 2
ROWS, COLS = 6, 24
C = 192
HEADS = 6
HEAD = C // HEADS
WIN = WPL * WLAT * WLON
WINDOWS = COLS // WLON
NPOS = 3312
HI = -(-NPOS // 128)
HIP = 32
EDGE = 8
N_OWN = WPL * ROWS * COLS
N_LAT = WPL * HALF_LAT * COLS
N_EDGE = WPL * HALF_LAT * EDGE
N_ALL = N_OWN + N_LAT + 2 * N_EDGE
MAIN = 128
REST = WIN - MAIN
PAIRS = HEADS * MAIN + 128
EPS = 1e-05
SCALE = HEAD**-0.5
NEG = -1000000000.0
G_ROWS = 1280
CUT = WPL * ROWS * HALF_LON
EDGE_ROWS = 3 * CUT
TAB_ROWS = 160
MSG = EDGE_ROWS + TAB_ROWS

SPLIT = (4, 8, 4, 2, 2)
AXES = ("x", "zl", "y", "zh", "c")
LAT_AXES = ("x", "zl", "y")
LON_AXES = ("zh", "c")
PLANE = ("x", "y", "c")
LINE = ("zh", "zl")


def source_rows():
    at = np.zeros((WINDOWS, WIN), np.int32)
    for level in range(WPL):
        for row in range(ROWS):
            for col in range(COLS):
                from_level = (level + WPL // 2) % WPL
                r, c = row + HALF_LAT, col + HALF_LON
                if r < ROWS and c < COLS:
                    src = from_level * ROWS * COLS + r * COLS + c
                elif c < COLS:
                    src = N_OWN + from_level * HALF_LAT * COLS + (r - ROWS) * COLS + c
                elif r < ROWS:
                    src = N_OWN + N_LAT + from_level * HALF_LAT * EDGE + (r - HALF_LAT) * EDGE + c - COLS
                else:
                    src = N_OWN + N_LAT + N_EDGE + from_level * HALF_LAT * EDGE + (r - ROWS) * EDGE + c - COLS
                at[col // WLON, level * WLAT * WLON + row * WLON + col % WLON] = src
    return at


def constants():
    at = source_rows()
    pick = np.zeros((WINDOWS, WIN, N_ALL), np.float32)
    for w in range(WINDOWS):
        pick[w, np.arange(WIN), at[w]] = 1.0
    back = np.zeros((WINDOWS, N_OWN + N_LAT + CUT, WIN), np.float32)
    back[:, : N_OWN + N_LAT] = pick.transpose(0, 2, 1)[:, : N_OWN + N_LAT]
    place = np.zeros((N_OWN + N_LAT, CUT), np.float32)
    for level in range(WPL):
        for row in range(ROWS):
            for col in range(HALF_LON):
                edge = N_OWN + N_LAT + level * HALF_LAT * EDGE + (row % HALF_LAT) * EDGE + col
                edge += 0 if row >= HALF_LAT else N_EDGE
                to = level * ROWS * HALF_LON + row * HALF_LON + col
                back[:, N_OWN + N_LAT + to] = pick[:, :, edge]
                if row >= HALF_LAT:
                    place[level * ROWS * COLS + row * COLS + col, to] = 1.0
                else:
                    place[N_OWN + level * HALF_LAT * COLS + row * COLS + col, to] = 1.0
    spread = np.zeros((256, WIN), np.float32)
    for lane in range(MAIN):
        spread[lane, lane] = 1.0
    for lane in range(HEADS * REST):
        spread[MAIN + lane, MAIN + lane % REST] = 1.0
    return pick.astype(BF), back.astype(BF), spread.astype(BF), place.astype(BF)


def dot(a, b, dims):
    return lax.dot_general(a, b, ((dims[:1], dims[1:]), ((), ())), preferred_element_type=F32)


def nn(a, b):
    return dot(a, b, (1, 0))


def nt(a, b):
    return dot(a, b, (1, 1))


def eye(n):
    return (lax.broadcasted_iota(jnp.int32, (n, n), 0) == lax.broadcasted_iota(jnp.int32, (n, n), 1)).astype(F32).astype(BF)


def cut_kernel(tokens, d_out, lat, lon, diag):
    for i, ref in enumerate((tokens, d_out)):
        top = ref[:, :HALF_LAT]
        lat[i] = top
        diag[i] = top[:, :, :EDGE]
        lon[i] = ref[:, HALF_LAT:, :, :][:, :, :EDGE]


def tables_kernel(pos, table, spread, w_qkv, w_proj, mask, gain, bias, hi_out, lo_out, w3, w3t, wpt, blocked, gain_out, scr):
    one = eye(WIN)
    idx = pos[...]
    hi = lax.shift_right_logical(idx, 7)
    lo = lax.bitwise_and(idx, 127)
    sp = spread[...]
    hi2 = nt(nt(one, hi.astype(F32).astype(BF)).astype(BF), sp)
    lo2 = nt(nt(one, lo.astype(F32).astype(BF)).astype(BF), sp)
    hi2 = hi2.astype(jnp.int32)
    lo2 = lo2.astype(jnp.int32)
    hi_out[...] = hi2
    lo_out[...] = lo2

    steps = []
    for pair in range(HEADS // 2):
        words = []
        for head in (2 * pair, 2 * pair + 1):
            row = table[head]
            unit = jnp.maximum(jnp.max(jnp.abs(row), axis=1, keepdims=True), 1e-20) * (1.0 / 32767.0)
            fixed = row * (1.0 / unit)
            fixed = jnp.floor(jnp.clip(fixed + 0.5, -32767.0, 32767.0)).astype(jnp.int32)
            steps.append(unit)
            words.append(fixed)
        scr[pair : pair + 1, :NPOS] = lax.shift_left(words[0], 16) | lax.bitwise_and(words[1], 65535)
    scr[:, NPOS:] = jnp.zeros((HEADS // 2, HI * 128 - NPOS), jnp.int32)

    def look(h_idx, l_idx):
        acc = [[jnp.zeros((8, 128), jnp.int32) for _ in h_idx] for _ in range(HEADS // 2)]
        for part in range(HI):
            hit = [h == part for h in h_idx]
            for pair in range(HEADS // 2):
                row = jnp.broadcast_to(scr[pair : pair + 1, part * 128 : part * 128 + 128], (8, 128))
                for i, l in enumerate(l_idx):
                    got = jnp.take_along_axis(row, l, axis=1, mode="promise_in_bounds")
                    acc[pair][i] = jnp.where(hit[i], got, acc[pair][i])
        out = []
        for pair in range(HEADS // 2):
            high = [lax.shift_right_arithmetic(v, 16) for v in acc[pair]]
            low = [lax.shift_right_arithmetic(lax.shift_left(v, 16), 16) for v in acc[pair]]
            out.append([v.astype(F32) * steps[2 * pair] for v in high])
            out.append([v.astype(F32) * steps[2 * pair + 1] for v in low])
        return out

    def step(block, carry):
        rows = [pl.ds(pl.multiple_of(block * 24 + 8 * i, 8), 8) for i in range(3)]
        acc = look([hi_out[r, :128] for r in rows], [lo_out[r, :128] for r in rows])
        for head in range(HEADS):
            for i, r in enumerate(rows):
                bias[r, MAIN * head : MAIN * (head + 1)] = acc[head][i]
        return carry

    lax.fori_loop(0, WIN // 24, step, 0)
    pad = jnp.zeros((REST, 256 - WIN), jnp.int32)
    h_rest = jnp.concatenate([hi[MAIN:], pad], axis=1)
    l_rest = jnp.concatenate([lo[MAIN:], pad], axis=1)
    tiles = [(slice(8 * i, 8 * i + 8), slice(128 * j, 128 * j + 128)) for i in range(2) for j in range(2)]
    acc = look([h_rest[t] for t in tiles], [l_rest[t] for t in tiles])
    rest = [jnp.concatenate([jnp.concatenate(a[2 * i : 2 * i + 2], axis=1) for i in range(2)], axis=0) for a in acc]
    rest = jnp.concatenate(rest + [jnp.zeros((128 - HEADS * REST, 256), F32)], axis=0)
    bias[:, HEADS * MAIN :] = rest.T[:WIN]

    one = eye(C)
    for i in range(3):
        w = w_qkv[:, C * i : C * (i + 1)]
        w3[i] = w
        w3t[i] = nt(one, w).astype(BF)
    wpt[...] = nt(one, w_proj[...]).astype(BF)
    gain_out[...] = jnp.sum(one.astype(F32) * gain[...], axis=1, keepdims=True)

    lab = [mask[row, level : level + 1, :].astype(F32) for level in range(WPL) for row in range(ROWS)]
    lab = jnp.concatenate(lab, axis=0).astype(BF)
    for w in range(WINDOWS):
        lane = lax.broadcasted_iota(jnp.int32, (COLS, WIN), 1)
        col = lax.broadcasted_iota(jnp.int32, (COLS, WIN), 0)
        across = (lax.rem(lane, WLON) + w * WLON == col).astype(F32).astype(BF)
        wide = nn(lab, across)
        r = lax.broadcasted_iota(jnp.int32, (WPL * ROWS, WIN), 0)
        a = lax.broadcasted_iota(jnp.int32, (WPL * ROWS, WIN), 1)
        row = jnp.sum(jnp.where(lax.div(a, WLON) == r, wide, 0.0), axis=0, keepdims=True)
        row = jnp.broadcast_to(row, (WIN, WIN)).astype(BF)
        down = nt(eye(WIN), row)
        over = nt(row, sp)
        blocked[w] = jnp.where(over == jnp.broadcast_to(down[:, :1], (WIN, 256)), 0.0, NEG)


def by_head(x):
    lane = lax.broadcasted_iota(jnp.int32, (1, C), 1)
    keep = [((lane >= HEAD * h) & (lane < HEAD * (h + 1))).astype(F32).astype(BF) for h in range(HEADS)]
    parts = [x[:MAIN] * keep[h] for h in range(HEADS)]
    parts += [x[MAIN:] * keep[h] for h in range(HEADS)]
    parts.append(jnp.zeros((PAIRS - HEADS * WIN, C), BF))
    return jnp.concatenate(parts, axis=0)


def heads_apart(left, right, scale):
    main = [
        nn(left[HEAD * h : HEAD * (h + 1)], right[:, MAIN * h : MAIN * (h + 1)]) for h in range(HEADS)
    ]
    main = (jnp.concatenate(main, axis=0) * scale).astype(BF)
    rest = nn(left, right[:, HEADS * MAIN :]) * scale
    row = lax.broadcasted_iota(jnp.int32, (C, 128), 0)
    lane = lax.broadcasted_iota(jnp.int32, (C, 128), 1)
    rest = jnp.where(lax.div(row, HEAD) == lax.div(lane, REST), rest, 0.0).astype(BF)
    fold_l = lax.broadcasted_iota(jnp.int32, (128, REST), 0)
    fold_a = lax.broadcasted_iota(jnp.int32, (128, REST), 1)
    fold = (lax.rem(fold_l, REST) == fold_a).astype(F32).astype(BF)
    rest = nn(rest, fold).astype(BF)
    return jnp.concatenate([main, rest], axis=1)


def block_kernel(
    own_x, own_d, lat, lon, diag, pick, back, gain, w3, w3t, wp, wpt, bias, blocked,
    base_x, base_d, out_lat, out_edge, grads, d_bias,
):
    x_all = jnp.concatenate([own_x[...], lat[0], lon[0], diag[0]], axis=0)
    d_all = jnp.concatenate([own_d[...], lat[1], lon[1], diag[1]], axis=0)
    eye_c = eye(C)
    eye_w = eye(WIN)
    g = gain[...]
    sums = [jnp.zeros((C, C), F32) for _ in range(4)]
    d_gain = jnp.zeros((C, 1), F32)
    x_back = jnp.zeros((N_OWN + N_LAT + CUT, C), F32)
    d_back = jnp.zeros((N_OWN + N_LAT + CUT, C), F32)
    for w in range(WINDOWS):
        x = nn(pick[w], x_all).astype(BF)
        d_proj = nn(pick[w], d_all).astype(BF)
        xt = nt(eye_c, x)
        mean = jnp.sum(xt, axis=0, keepdims=True) * (1.0 / C)
        centered = xt - mean
        var = jnp.sum(centered * centered, axis=0, keepdims=True) * (1.0 / C)
        rstd = lax.rsqrt(var + EPS)
        xhat = centered * rstd
        nt_w = (xhat * g).astype(BF)
        n_w = nt(eye_w, nt_w).astype(BF)
        q = nn(n_w, w3[0]).astype(BF)
        k = nn(n_w, w3[1]).astype(BF)
        v = nn(n_w, w3[2]).astype(BF)
        kt = nn(w3t[1], nt_w).astype(BF)
        vt = nn(w3t[2], nt_w).astype(BF)
        qm = by_head(q)
        dm = by_head(nt(d_proj, wp[...]).astype(BF))
        far = jnp.concatenate([blocked[w, :, :MAIN]] * HEADS + [blocked[w, :, MAIN:]], axis=1)
        s = nt(k, qm) * SCALE + bias[...] + far
        e = jnp.exp(s - jnp.max(s, axis=0, keepdims=True))
        p = e * (1.0 / jnp.sum(e, axis=0, keepdims=True))
        attn = p.astype(BF)
        d_attn = nt(v, dm)
        pd = p * d_attn
        ds = pd - p * jnp.sum(pd, axis=0, keepdims=True)
        dsb = ds.astype(BF)
        if w == 0:
            d_bias[...] = ds
        else:
            d_bias[...] += ds
        mixed_t = heads_apart(vt, attn, 1.0)
        dq_t = heads_apart(kt, dsb, SCALE)
        dk = (nn(dsb, qm) * SCALE).astype(BF)
        dv = nn(attn, dm).astype(BF)
        proj_t = nn(wpt[...], mixed_t).astype(BF)
        x_back = x_back + nt(back[w], proj_t)
        sums[0] = sums[0] + nt(nt_w, dq_t)
        sums[1] = sums[1] + nn(nt_w, dk)
        sums[2] = sums[2] + nn(nt_w, dv)
        sums[3] = sums[3] + nn(mixed_t, d_proj)
        dn = nn(w3[0], dq_t) + nt(w3[1], dk) + nt(w3[2], dv)
        dn = dn.astype(BF).astype(F32)
        d_gain = d_gain + jnp.sum(dn * xhat, axis=1, keepdims=True)
        dy = dn * g
        m1 = jnp.sum(dy, axis=0, keepdims=True) * (1.0 / C)
        m2 = jnp.sum(dy * xhat, axis=0, keepdims=True) * (1.0 / C)
        dx = (rstd * (dy - m1 - xhat * m2)).astype(BF)
        d_back = d_back + nt(back[w], dx)
    for i in range(4):
        grads[C * i : C * (i + 1), :] = sums[i][:, :128].astype(BF)
    for i in range(2):
        pair = jnp.concatenate([sums[2 * i][:, 128:], sums[2 * i + 1][:, 128:]], axis=1)
        grads[C * (4 + i) : C * (5 + i), :] = pair.astype(BF)
    row = jnp.sum(eye_c.astype(F32) * d_gain, axis=0, keepdims=True)
    tail = jnp.concatenate([row[:, 128:], jnp.zeros((1, 256 - C), F32)], axis=1)
    grads[6 * C :, :] = jnp.concatenate([row[:, :128], tail, jnp.zeros((126, 128), F32)], axis=0).astype(BF)
    for i, (total, own, base) in enumerate(((x_back, own_x, base_x), (d_back, own_d, base_d))):
        base[...] = (own[...].astype(F32) + total[:N_OWN]).astype(BF)
        out_lat[i] = total[N_OWN : N_OWN + N_LAT].astype(BF)
    edge = jnp.concatenate([x_back[N_OWN + N_LAT :], d_back[N_OWN + N_LAT :]], axis=0)
    out_edge[: 2 * CUT, :] = edge[:, :128].astype(BF)
    out_edge[2 * CUT :, :] = jnp.concatenate([edge[:CUT, 128:], edge[CUT:, 128:]], axis=1).astype(BF)


def scatter_kernel(d_bias, hi, lo, edge, out, acc):
    acc[...] = jnp.zeros_like(acc)

    def step(block, carry):
        rows = pl.ds(pl.multiple_of(block * 8, 8), 8)
        h_all = hi[rows, :]
        l_all = lo[rows, :]
        d_all = d_bias[rows, :]
        part = lax.broadcasted_iota(jnp.int32, (HIP, 256), 0)
        group = lax.shift_right_logical(lax.broadcasted_iota(jnp.int32, (HIP, 128), 1), 4)
        place = lax.broadcasted_iota(jnp.int32, (128, 256), 0)
        total = acc[...]
        for i in range(8):
            hit = jnp.broadcast_to(h_all[i : i + 1], (HIP, 256)) == part
            rest = jnp.broadcast_to(d_all[i : i + 1, HEADS * MAIN :], (HIP, 128))
            rest = jnp.where(hit[:, 128:], rest, 0.0)
            many = []
            for head in range(HEADS):
                main = jnp.broadcast_to(d_all[i : i + 1, MAIN * head : MAIN * (head + 1)], (HIP, 128))
                main = jnp.where(hit[:, :128], main, 0.0)
                many.append(jnp.concatenate([main, jnp.where(group == head, rest, 0.0)], axis=1))
            many = jnp.concatenate(many, axis=0).astype(BF)
            spot = (jnp.broadcast_to(l_all[i : i + 1], (128, 256)) == place).astype(F32).astype(BF)
            total = total + nt(many, spot)
        acc[...] = total
        return carry

    lax.fori_loop(0, WIN // 8, step, 0)
    out[:EDGE_ROWS, :] = edge[...].astype(F32).astype(BF)
    rows = [acc[HIP * h : HIP * h + HI] for h in range(HEADS)] + [jnp.zeros((TAB_ROWS - HEADS * HI, 128), F32)]
    out[EDGE_ROWS:, :] = jnp.concatenate(rows, axis=0).astype(BF)


def pair_kernel(own, near, out):
    out[...] = jnp.concatenate(
        [own[:EDGE_ROWS, :].astype(F32), own[EDGE_ROWS:, :].astype(F32) + near[EDGE_ROWS:, :].astype(F32)], axis=0
    ).astype(BF)


def middle_kernel(core, pair, near, far, base_x, base_d, lat, place, out_x, out_d, out_lat, out_t):
    from_near = jnp.broadcast_to(core[...], (EDGE_ROWS, 128)) == 1
    edge = jnp.where(from_near, near[:EDGE_ROWS, :].astype(F32), far[:EDGE_ROWS, :].astype(F32))
    for i, (base, out) in enumerate(((base_x, out_x), (base_d, out_d))):
        wide = jnp.concatenate([edge[CUT * i : CUT * (i + 1)], edge[2 * CUT :, 64 * i : 64 * (i + 1)]], axis=1)
        add = nn(place[...], wide.astype(BF))
        out[...] = (base[...].astype(F32) + add[:N_OWN]).astype(BF)
        out_lat[i] = (lat[i].astype(F32) + add[N_OWN:]).astype(BF)
    t = pair[EDGE_ROWS:, :].astype(F32) + far[EDGE_ROWS:, :].astype(F32)
    for part in range(HI):
        width = min(128, NPOS - part * 128)
        for head in range(HEADS):
            row = head * HI + part
            out_t[head, :, part * 128 : part * 128 + width] = t[row : row + 1, :width]


def finish_kernel(base_x, base_d, lat, out_x, out_d):
    for i, (base, out) in enumerate(((base_x, out_x), (base_d, out_d))):
        out[:, HALF_LAT:] = base[:, HALF_LAT:]
        out[:, :HALF_LAT] = (base[:, :HALF_LAT].astype(F32) + lat[i].astype(F32)).astype(BF)


def unpack_kernel(g, scale, qkv, proj, gain):
    k = scale
    full = [g[C * i : C * (i + 1), :].astype(F32) * k for i in range(6)]
    qkv[:, 0:128] = full[0]
    qkv[:, 128:256] = jnp.concatenate([full[4][:, :64], full[1][:, :64]], axis=1)
    qkv[:, 256:384] = jnp.concatenate([full[1][:, 64:], full[4][:, 64:]], axis=1)
    qkv[:, 384:512] = full[2]
    qkv[:, 512:576] = full[5][:, :64]
    proj[:, 0:128] = full[3]
    proj[:, 128:192] = full[5][:, 64:]
    tail = g[6 * C : 6 * C + 16, :].astype(F32) * k
    gain[:, :128] = tail[0:1]
    gain[:, 128:] = tail[1:2, : C - 128]


def call(kernel, out_shape, *args, scratch=(), cost=(0, 0), vmem=60):
    return pl.pallas_call(
        kernel,
        out_shape=out_shape,
        scratch_shapes=list(scratch),
        compiler_params=pltpu.CompilerParams(vmem_limit_bytes=vmem * 2**20),
        cost_estimate=pl.CostEstimate(flops=cost[0], bytes_accessed=cost[1], transcendentals=0),
    )(*args)


def sds(shape, dtype):
    return jax.ShapeDtypeStruct(shape, dtype)


def make(sizes):
    n_lat = sizes[0] * sizes[1] * sizes[2]
    n_lon = sizes[3] * sizes[4]
    n_plane = sizes[0] * sizes[2] * sizes[4]
    n_line = sizes[1] * sizes[3]
    piece = G_ROWS // n_plane

    def route(d_lat, d_lon):
        return [
            (a * n_lon + b, (a + d_lat) % n_lat * n_lon + (b + d_lon) % n_lon)
            for a in range(n_lat)
            for b in range(n_lon)
        ]

    def hop(to):
        return [
            (a * n_lon + zh * sizes[4] + c, a * n_lon + to(zh, c)[0] * sizes[4] + to(zh, c)[1])
            for a in range(n_lat)
            for zh in range(sizes[3])
            for c in range(sizes[4])
        ]

    def per_device(tokens, mask_ids, pos_index, norm_gain, w_qkv, w_proj, earth_bias, d_out):
        pick, back, spread, place = (jnp.asarray(c) for c in constants())
        lat, lon, diag = call(
            cut_kernel,
            (
                sds((2, WPL, HALF_LAT, COLS, C), BF),
                sds((2, WPL, HALF_LAT, EDGE, C), BF),
                sds((2, WPL, HALF_LAT, EDGE, C), BF),
            ),
            tokens,
            d_out,
        )
        lat = lax.ppermute(lat, AXES, route(-1, 0))
        lon = lax.ppermute(lon, AXES, route(0, -1))
        diag = lax.ppermute(diag, AXES, route(-1, -1))
        bias, hi, lo, w3, w3t, wpt, blocked, gain_col = call(
            tables_kernel,
            (
                sds((WIN, PAIRS), F32),
                sds((WIN, 256), jnp.int32),
                sds((WIN, 256), jnp.int32),
                sds((3, C, C), BF),
                sds((3, C, C), BF),
                sds((C, C), BF),
                sds((WINDOWS, WIN, 256), F32),
                sds((C, 1), F32),
            ),
            pos_index,
            earth_bias.transpose(1, 0, 2),
            spread,
            w_qkv,
            w_proj,
            mask_ids.transpose(1, 0, 2),
            norm_gain.reshape(1, C),
            scratch=[pltpu.VMEM((HEADS // 2, HI * 128), jnp.int32)],
            cost=(6 * 10**9, 10**6),
        )
        base_x, base_d, out_lat, out_edge, grads, d_bias = call(
            block_kernel,
            (
                sds((N_OWN, C), BF),
                sds((N_OWN, C), BF),
                sds((2, N_LAT, C), BF),
                sds((EDGE_ROWS, 128), BF),
                sds((G_ROWS, 128), BF),
                sds((WIN, PAIRS), F32),
            ),
            tokens.reshape(N_OWN, C),
            d_out.reshape(N_OWN, C),
            lat.reshape(2, N_LAT, C),
            lon.reshape(2, N_EDGE, C),
            diag.reshape(2, N_EDGE, C),
            pick,
            back,
            gain_col,
            w3,
            w3t,
            w_proj,
            wpt,
            bias,
            blocked,
            cost=(6 * 10**9, 10**6),
        )
        parts = lax.all_to_all(grads.reshape(n_plane, piece, 128), PLANE, 0, 0)
        own = call(
            scatter_kernel,
            sds((MSG, 128), BF),
            d_bias,
            hi,
            lo,
            out_edge,
            scratch=[pltpu.VMEM((HEADS * HIP, 128), F32)],
            cost=(8 * 10**9, 10**6),
        )
        parts, own = lax.optimization_barrier((parts, own))
        near = lax.ppermute(own, AXES, hop(lambda zh, c: (zh, 1 - c)))
        part = jnp.sum(parts.astype(F32), axis=0).astype(BF)
        line = lax.all_to_all(jnp.broadcast_to(part, (n_line,) + part.shape), LINE, 0, 0)
        pair = call(pair_kernel, sds((MSG, 128), BF), own, near)
        far = lax.ppermute(pair, AXES, hop(lambda zh, c: (1 - zh, 1 - c)))
        line, pair = lax.optimization_barrier((line, pair))
        total = jnp.sum(line.astype(F32), axis=0).astype(BF)
        whole = lax.all_to_all(jnp.broadcast_to(total, (n_plane,) + total.shape), PLANE, 0, 0)
        core = jnp.full((1, 128), lax.axis_index("c"), jnp.int32)
        base_x, base_d, out_lat, d_table = call(
            middle_kernel,
            (
                sds((N_OWN, C), BF),
                sds((N_OWN, C), BF),
                sds((2, N_LAT, C), BF),
                sds((HEADS, 1, NPOS), F32),
            ),
            core,
            pair,
            near,
            far,
            base_x,
            base_d,
            out_lat,
            place,
            cost=(20 * 10**9, 10**6),
        )
        out_lat = lax.ppermute(out_lat, AXES, route(1, 0))
        scale = float(n_lat * n_lon * N_OWN) ** -0.5
        qkv, proj, gain = call(
            lambda g, a, b, c: unpack_kernel(g, scale, a, b, c),
            (sds((C, 3 * C), F32), sds((C, C), F32), sds((1, C), F32)),
            whole.reshape(G_ROWS, 128),
        )
        base_x, qkv = lax.optimization_barrier((base_x, qkv))
        updated, d_tokens = call(
            finish_kernel,
            (sds((WPL, ROWS, COLS, C), BF), sds((WPL, ROWS, COLS, C), BF)),
            base_x.reshape(WPL, ROWS, COLS, C),
            base_d.reshape(WPL, ROWS, COLS, C),
            out_lat.reshape(2, WPL, HALF_LAT, COLS, C),
            cost=(20 * 10**9, 10**6),
        )
        return updated, d_tokens, qkv, proj, gain.reshape(C), d_table.transpose(1, 0, 2)

    return per_device


def solution(mesh):
    fine = jax.sharding.Mesh(mesh.devices.reshape(SPLIT), AXES)
    placed = (
        P(None, LAT_AXES, LON_AXES, None),
        P(None, LAT_AXES, LON_AXES),
        P(),
        P(),
        P(),
        P(),
        P(LAT_AXES, None, None),
        P(None, LAT_AXES, LON_AXES, None),
    )
    return jax.shard_map(
        make(SPLIT),
        mesh=fine,
        in_specs=placed,
        out_specs=(
            P(None, LAT_AXES, LON_AXES, None),
            P(None, LAT_AXES, LON_AXES, None),
            P(),
            P(),
            P(),
            P(LAT_AXES, None, None),
        ),
        check_vma=False,
    )
```

```python
import jax
import jax.numpy as jnp
import numpy as np
from jax import lax
from jax.experimental import pallas as pl
from jax.experimental.pallas import tpu as pltpu
from jax.sharding import PartitionSpec as P

BF = jnp.bfloat16
F32 = jnp.float32

WPL, WLAT, WLON = 2, 6, 12
HALF_LAT, HALF_LON = WLAT // 2, WLON // 2
ROWS, COLS = 6, 24
C = 192
HEADS = 6
HEAD = C // HEADS
WIN = WPL * WLAT * WLON
WINDOWS = COLS // WLON
NPOS = 3312
HI = -(-NPOS // 128)
HIP = 32
EDGE = 8
N_OWN = WPL * ROWS * COLS
N_LAT = WPL * HALF_LAT * COLS
N_EDGE = WPL * HALF_LAT * EDGE
N_ALL = N_OWN + N_LAT + 2 * N_EDGE
MAIN = 128
REST = WIN - MAIN
PAIRS = HEADS * MAIN + 128
EPS = 1e-05
SCALE = HEAD**-0.5
NEG = -1000000000.0
G_ROWS = 1280
CUT = WPL * ROWS * HALF_LON
EDGE_ROWS = 3 * CUT + 8
TAB_ROWS = 160
MSG = EDGE_ROWS + TAB_ROWS
LAT_ROWS = 3 * N_LAT
CORNER_ROWS = 3 * N_EDGE
SIDE_ROWS = 2 * CORNER_ROWS
LINE_ROWS = 2 * LAT_ROWS + CORNER_ROWS

SPLIT = (4, 8, 4, 2, 2)
AXES = ("x", "zl", "y", "zh", "c")
LAT_AXES = ("x", "zl", "y")
LON_AXES = ("zh", "c")
PLANE = ("x", "y", "c")
LINE = ("zh", "zl")


N_BACK = N_OWN + 2 * N_LAT + CUT


def source_rows():
    at = np.zeros((WINDOWS, WIN), np.int32)
    for level in range(WPL):
        for row in range(ROWS):
            for col in range(COLS):
                from_level = (level + WPL // 2) % WPL
                r, c = row + HALF_LAT, col + HALF_LON
                if r < ROWS and c < COLS:
                    src = from_level * ROWS * COLS + r * COLS + c
                elif c < COLS:
                    src = N_OWN + from_level * HALF_LAT * COLS + (r - ROWS) * COLS + c
                elif r < ROWS:
                    src = N_OWN + N_LAT + from_level * HALF_LAT * EDGE + (r - HALF_LAT) * EDGE + c - COLS
                else:
                    src = N_OWN + N_LAT + N_EDGE + from_level * HALF_LAT * EDGE + (r - ROWS) * EDGE + c - COLS
                at[col // WLON, level * WLAT * WLON + row * WLON + col % WLON] = src
    return at


def constants():
    at = source_rows()
    pick = np.zeros((WINDOWS, WIN, N_ALL), np.float32)
    for w in range(WINDOWS):
        pick[w, np.arange(WIN), at[w]] = 1.0
    back = np.zeros((WINDOWS, N_BACK, WIN), np.float32)
    back[:, : N_OWN + N_LAT] = pick.transpose(0, 2, 1)[:, : N_OWN + N_LAT]
    place = np.zeros((N_OWN + N_LAT, CUT), np.float32)
    for level in range(WPL):
        for row in range(ROWS):
            for col in range(HALF_LON):
                edge = N_OWN + N_LAT + level * HALF_LAT * EDGE + (row % HALF_LAT) * EDGE + col
                edge += 0 if row >= HALF_LAT else N_EDGE
                to = level * ROWS * HALF_LON + row * HALF_LON + col
                back[:, N_OWN + N_LAT + to] = pick[:, :, edge]
                if row >= HALF_LAT:
                    place[level * ROWS * COLS + row * COLS + col, to] = 1.0
                else:
                    at_lat = level * HALF_LAT * COLS + row * COLS + col
                    place[N_OWN + at_lat, to] = 1.0
                    back[:, N_OWN + N_LAT + CUT + at_lat] = pick[:, :, edge]
    return pick.astype(BF), back.astype(BF), place.astype(BF)


def dot(a, b, dims):
    return lax.dot_general(a, b, ((dims[:1], dims[1:]), ((), ())), preferred_element_type=F32)


def nn(a, b):
    return dot(a, b, (1, 0))


def nt(a, b):
    return dot(a, b, (1, 1))


def eye(n):
    return (lax.broadcasted_iota(jnp.int32, (n, n), 0) == lax.broadcasted_iota(jnp.int32, (n, n), 1)).astype(F32).astype(BF)


def spread():
    lane = lax.broadcasted_iota(jnp.int32, (256, WIN), 0)
    query = lax.broadcasted_iota(jnp.int32, (256, WIN), 1)
    held = jnp.where(lane < MAIN, lane, MAIN + lax.bitwise_and(lane, REST - 1))
    return ((held == query) & (lane < MAIN + HEADS * REST)).astype(F32).astype(BF)


def fold(a, b):
    return jnp.concatenate([a[:, :128], b[:, :128], jnp.concatenate([a[:, 128:], b[:, 128:]], axis=1)], axis=0)


def unfold(both, n):
    return [
        jnp.concatenate([both[n * i : n * (i + 1)], both[2 * n : 3 * n, 64 * i : 64 * (i + 1)]], axis=1) for i in range(2)
    ]


def core_is(core, rows):
    return lax.broadcasted_iota(jnp.int32, (rows, 128), 0) * 0 + lax.axis_index("c") == core


def band_is(first, rows):
    at = lax.axis_index("zl") * lax.axis_size("y") + lax.axis_index("y")
    want = 0 if first else lax.axis_size("zl") * lax.axis_size("y") - 1
    return lax.broadcasted_iota(jnp.int32, (rows, 128), 0) * 0 + at == want


def cut_kernel(tokens, d_out, to_core, lat, edge):
    both = (tokens[...].astype(F32), d_out[...].astype(F32))
    top = fold(*(a[:, :HALF_LAT].reshape(N_LAT, C) for a in both))
    corner = fold(*(a[:, :HALF_LAT, :EDGE].reshape(N_EDGE, C) for a in both))
    lon = fold(*(a[:, HALF_LAT:, :EDGE].reshape(N_EDGE, C) for a in both))
    side = jnp.concatenate([corner, lon], axis=0)
    lat[...] = top.astype(BF)
    edge[...] = side.astype(BF)
    spare = jnp.zeros((LAT_ROWS - SIDE_ROWS, 128), F32)
    to_core[...] = jnp.where(core_is(1, LAT_ROWS), jnp.concatenate([side, spare], axis=0), top).astype(BF)


def join_kernel(lat, edge, sibling, to_lon, to_lat, to_line):
    corner = edge[:CORNER_ROWS, :]
    to_lon[...] = edge[...]
    to_lat[:LAT_ROWS, :] = lat[...]
    theirs = sibling[:CORNER_ROWS, :].astype(F32)
    to_lat[LAT_ROWS:, :] = jnp.where(band_is(True, CORNER_ROWS), corner.astype(F32), theirs).astype(BF)
    to_line[:LAT_ROWS, :] = lat[...]
    to_line[LAT_ROWS : 2 * LAT_ROWS, :] = sibling[...]
    to_line[2 * LAT_ROWS :, :] = corner


def tables_kernel(pos, table, bias, hi_out, lo_out, scr):
    one = eye(WIN)
    idx = pos[...]
    hi = lax.shift_right_logical(idx, 7)
    lo = lax.bitwise_and(idx, 127)
    sp = spread()
    hi2 = nt(nt(one, hi.astype(F32).astype(BF)).astype(BF), sp)
    lo2 = nt(nt(one, lo.astype(F32).astype(BF)).astype(BF), sp)
    hi2 = hi2.astype(jnp.int32)
    lo2 = lo2.astype(jnp.int32)
    hi_out[...] = hi2
    lo_out[...] = lo2

    steps = []
    for pair in range(HEADS // 2):
        words = []
        for head in (2 * pair, 2 * pair + 1):
            row = table[head]
            unit = jnp.maximum(jnp.max(jnp.abs(row), axis=1, keepdims=True), 1e-20) * (1.0 / 32767.0)
            fixed = row * (1.0 / unit)
            fixed = jnp.floor(jnp.clip(fixed + 0.5, -32767.0, 32767.0)).astype(jnp.int32)
            steps.append(unit)
            words.append(fixed)
        scr[pair : pair + 1, :NPOS] = lax.shift_left(words[0], 16) | lax.bitwise_and(words[1], 65535)
    scr[:, NPOS:] = jnp.zeros((HEADS // 2, HI * 128 - NPOS), jnp.int32)

    def look(h_idx, l_idx):
        acc = [[jnp.zeros((8, 128), jnp.int32) for _ in h_idx] for _ in range(HEADS // 2)]
        for part in range(HI):
            hit = [h == part for h in h_idx]
            for pair in range(HEADS // 2):
                row = jnp.broadcast_to(scr[pair : pair + 1, part * 128 : part * 128 + 128], (8, 128))
                for i, l in enumerate(l_idx):
                    got = jnp.take_along_axis(row, l, axis=1, mode="promise_in_bounds")
                    acc[pair][i] = jnp.where(hit[i], got, acc[pair][i])
        out = []
        for pair in range(HEADS // 2):
            high = [lax.shift_right_arithmetic(v, 16) for v in acc[pair]]
            low = [lax.shift_right_arithmetic(lax.shift_left(v, 16), 16) for v in acc[pair]]
            out.append([v.astype(F32) * steps[2 * pair] for v in high])
            out.append([v.astype(F32) * steps[2 * pair + 1] for v in low])
        return out

    def step(block, carry):
        rows = [pl.ds(pl.multiple_of(block * 24 + 8 * i, 8), 8) for i in range(3)]
        acc = look([hi_out[r, :128] for r in rows], [lo_out[r, :128] for r in rows])
        for head in range(HEADS):
            for i, r in enumerate(rows):
                bias[r, MAIN * head : MAIN * (head + 1)] = acc[head][i]
        return carry

    lax.fori_loop(0, WIN // 24, step, 0)
    pad = jnp.zeros((REST, 256 - WIN), jnp.int32)
    h_rest = jnp.concatenate([hi[MAIN:], pad], axis=1)
    l_rest = jnp.concatenate([lo[MAIN:], pad], axis=1)
    tiles = [(slice(8 * i, 8 * i + 8), slice(128 * j, 128 * j + 128)) for i in range(2) for j in range(2)]
    acc = look([h_rest[t] for t in tiles], [l_rest[t] for t in tiles])
    rest = [jnp.concatenate([jnp.concatenate(a[2 * i : 2 * i + 2], axis=1) for i in range(2)], axis=0) for a in acc]
    rest = jnp.concatenate(rest + [jnp.zeros((128 - HEADS * REST, 256), F32)], axis=0)
    bias[:, HEADS * MAIN :] = rest.T[:WIN]


def by_head(x):
    lane = lax.broadcasted_iota(jnp.int32, (1, C), 1)
    keep = [((lane >= HEAD * h) & (lane < HEAD * (h + 1))).astype(F32).astype(BF) for h in range(HEADS)]
    parts = [x[:MAIN] * keep[h] for h in range(HEADS)]
    parts += [x[MAIN:] * keep[h] for h in range(HEADS)]
    parts.append(jnp.zeros((PAIRS - HEADS * WIN, C), BF))
    return jnp.concatenate(parts, axis=0)


def heads_apart(left, right, scale):
    main = [
        nn(left[HEAD * h : HEAD * (h + 1)], right[:, MAIN * h : MAIN * (h + 1)]) for h in range(HEADS)
    ]
    main = (jnp.concatenate(main, axis=0) * scale).astype(BF)
    rest = nn(left, right[:, HEADS * MAIN :]) * scale
    row = lax.broadcasted_iota(jnp.int32, (C, 128), 0)
    lane = lax.broadcasted_iota(jnp.int32, (C, 128), 1)
    rest = jnp.where(lax.div(row, HEAD) == lax.div(lane, REST), rest, 0.0).astype(BF)
    fold_l = lax.broadcasted_iota(jnp.int32, (128, REST), 0)
    fold_a = lax.broadcasted_iota(jnp.int32, (128, REST), 1)
    fold = (lax.rem(fold_l, REST) == fold_a).astype(F32).astype(BF)
    rest = nn(rest, fold).astype(BF)
    return jnp.concatenate([main, rest], axis=1)


def regions(mask):
    sp = spread()
    out = []
    lab = [mask[row, level : level + 1, :].astype(F32) for level in range(WPL) for row in range(ROWS)]
    lab = jnp.concatenate(lab, axis=0).astype(BF)
    for w in range(WINDOWS):
        lane = lax.broadcasted_iota(jnp.int32, (COLS, WIN), 1)
        col = lax.broadcasted_iota(jnp.int32, (COLS, WIN), 0)
        across = (lax.rem(lane, WLON) + w * WLON == col).astype(F32).astype(BF)
        wide = nn(lab, across)
        r = lax.broadcasted_iota(jnp.int32, (WPL * ROWS, WIN), 0)
        a = lax.broadcasted_iota(jnp.int32, (WPL * ROWS, WIN), 1)
        row = jnp.sum(jnp.where(lax.div(a, WLON) == r, wide, 0.0), axis=0, keepdims=True)
        row = jnp.broadcast_to(row, (WIN, WIN)).astype(BF)
        down = nt(eye(WIN), row)
        over = nt(row, sp)
        out.append(jnp.where(over == jnp.broadcast_to(down[:, :1], (WIN, 256)), 0.0, NEG))
    return out


def block_kernel(
    own_x, own_d, sibling, from_lon, from_lat, from_line, from_side, from_corner, pick, back, gain, w_qkv, wp, mask, bias,
    base_x, base_d, out_lat, out_corner, out_edge, grads, d_bias,
):
    f32 = lambda ref, start, size: ref[start : start + size, :].astype(F32)
    over = f32(from_line, 0, LAT_ROWS) + f32(from_side, LAT_ROWS, LAT_ROWS)
    lat = unfold(jnp.where(band_is(False, LAT_ROWS), over, f32(from_lat, 0, LAT_ROWS)), N_LAT)
    lon = f32(sibling, CORNER_ROWS, CORNER_ROWS), f32(from_lon, CORNER_ROWS, CORNER_ROWS)
    lon = unfold(jnp.where(core_is(0, CORNER_ROWS), *lon), N_EDGE)
    direct = core_is(0, CORNER_ROWS) != band_is(False, CORNER_ROWS)
    diag = f32(from_side, 2 * LAT_ROWS, CORNER_ROWS) + f32(from_corner, 0, CORNER_ROWS)
    diag = unfold(jnp.where(direct, f32(from_lat, LAT_ROWS, CORNER_ROWS), diag), N_EDGE)
    x_all, d_all = (
        jnp.concatenate([own[...], lat[i].astype(BF), lon[i].astype(BF), diag[i].astype(BF)], axis=0)
        for i, own in enumerate((own_x, own_d))
    )
    eye_c = eye(C)
    eye_w = eye(WIN)
    g = jnp.sum(eye_c.astype(F32) * gain[...], axis=1, keepdims=True)
    w3 = [w_qkv[:, C * i : C * (i + 1)] for i in range(3)]
    w3t = [None] + [nt(eye_c, w).astype(BF) for w in w3[1:]]
    wpt = nt(eye_c, wp[...]).astype(BF)
    blocked = regions(mask)
    sums = [jnp.zeros((C, C), F32) for _ in range(4)]
    d_gain = jnp.zeros((C, 1), F32)
    x_back = jnp.zeros((N_BACK, C), F32)
    d_back = jnp.zeros((N_BACK, C), F32)
    for w in range(WINDOWS):
        x = nn(pick[w], x_all).astype(BF)
        d_proj = nn(pick[w], d_all).astype(BF)
        xt = nt(eye_c, x)
        mean = jnp.sum(xt, axis=0, keepdims=True) * (1.0 / C)
        centered = xt - mean
        var = jnp.sum(centered * centered, axis=0, keepdims=True) * (1.0 / C)
        rstd = lax.rsqrt(var + EPS)
        xhat = centered * rstd
        nt_w = (xhat * g).astype(BF)
        n_w = nt(eye_w, nt_w).astype(BF)
        q = nn(n_w, w3[0]).astype(BF)
        k = nn(n_w, w3[1]).astype(BF)
        v = nn(n_w, w3[2]).astype(BF)
        kt = nn(w3t[1], nt_w).astype(BF)
        vt = nn(w3t[2], nt_w).astype(BF)
        qm = by_head(q)
        dm = by_head(nt(d_proj, wp[...]).astype(BF))
        far = jnp.concatenate([blocked[w][:, :MAIN]] * HEADS + [blocked[w][:, MAIN:]], axis=1)
        s = nt(k, qm) * SCALE + bias[...] + far
        e = jnp.exp(s - jnp.max(s, axis=0, keepdims=True))
        p = e * (1.0 / jnp.sum(e, axis=0, keepdims=True))
        attn = p.astype(BF)
        d_attn = nt(v, dm)
        pd = p * d_attn
        ds = pd - p * jnp.sum(pd, axis=0, keepdims=True)
        dsb = ds.astype(BF)
        if w == 0:
            d_bias[...] = ds
        else:
            d_bias[...] += ds
        mixed_t = heads_apart(vt, attn, 1.0)
        dq_t = heads_apart(kt, dsb, SCALE)
        dk = (nn(dsb, qm) * SCALE).astype(BF)
        dv = nn(attn, dm).astype(BF)
        proj_t = nn(wpt, mixed_t).astype(BF)
        x_back = x_back + nt(back[w], proj_t)
        sums[0] = sums[0] + nt(nt_w, dq_t)
        sums[1] = sums[1] + nn(nt_w, dk)
        sums[2] = sums[2] + nn(nt_w, dv)
        sums[3] = sums[3] + nn(mixed_t, d_proj)
        dn = nn(w3[0], dq_t) + nt(w3[1], dk) + nt(w3[2], dv)
        dn = dn.astype(BF).astype(F32)
        d_gain = d_gain + jnp.sum(dn * xhat, axis=1, keepdims=True)
        dy = dn * g
        m1 = jnp.sum(dy, axis=0, keepdims=True) * (1.0 / C)
        m2 = jnp.sum(dy * xhat, axis=0, keepdims=True) * (1.0 / C)
        dx = (rstd * (dy - m1 - xhat * m2)).astype(BF)
        d_back = d_back + nt(back[w], dx)
    for i in range(4):
        grads[C * i : C * (i + 1), :] = sums[i][:, :128].astype(BF)
    for i in range(2):
        pair = jnp.concatenate([sums[2 * i][:, 128:], sums[2 * i + 1][:, 128:]], axis=1)
        grads[C * (4 + i) : C * (5 + i), :] = pair.astype(BF)
    row = jnp.sum(eye_c.astype(F32) * d_gain, axis=0, keepdims=True)
    tail = jnp.concatenate([row[:, 128:], jnp.zeros((1, 256 - C), F32)], axis=1)
    grads[6 * C :, :] = jnp.concatenate([row[:, :128], tail, jnp.zeros((126, 128), F32)], axis=0).astype(BF)
    for i, (total, own, base) in enumerate(((x_back, own_x, base_x), (d_back, own_d, base_d))):
        base[...] = (own[...].astype(F32) + total[:N_OWN]).astype(BF)
    parts = ((out_lat, N_OWN, N_LAT), (out_edge, N_OWN + N_LAT, CUT), (out_corner, N_OWN + N_LAT + CUT, N_LAT))
    for out, start, size in parts:
        both = fold(x_back[start : start + size], d_back[start : start + size])
        spare = out.shape[0] - both.shape[0]
        if spare:
            both = jnp.concatenate([both, jnp.zeros((spare, 128), F32)], axis=0)
        out[...] = both.astype(BF)


def scatter_kernel(d_bias, hi, lo, edge, lat, out, acc):
    acc[...] = jnp.zeros_like(acc)

    def step(block, carry):
        rows = pl.ds(pl.multiple_of(block * 8, 8), 8)
        h_all = hi[rows, :]
        l_all = lo[rows, :]
        d_all = d_bias[rows, :]
        part = lax.broadcasted_iota(jnp.int32, (HIP, 256), 0)
        group = lax.shift_right_logical(lax.broadcasted_iota(jnp.int32, (HIP, 128), 1), 4)
        place = lax.broadcasted_iota(jnp.int32, (128, 256), 0)
        total = acc[...]
        for i in range(8):
            hit = jnp.broadcast_to(h_all[i : i + 1], (HIP, 256)) == part
            rest = jnp.broadcast_to(d_all[i : i + 1, HEADS * MAIN :], (HIP, 128))
            rest = jnp.where(hit[:, 128:], rest, 0.0)
            many = []
            for head in range(HEADS):
                main = jnp.broadcast_to(d_all[i : i + 1, MAIN * head : MAIN * (head + 1)], (HIP, 128))
                main = jnp.where(hit[:, :128], main, 0.0)
                many.append(jnp.concatenate([main, jnp.where(group == head, rest, 0.0)], axis=1))
            many = jnp.concatenate(many, axis=0).astype(BF)
            spot = (jnp.broadcast_to(l_all[i : i + 1], (128, 256)) == place).astype(F32).astype(BF)
            total = total + nt(many, spot)
        acc[...] = total
        return carry

    lax.fori_loop(0, WIN // 8, step, 0)
    out[:EDGE_ROWS, :] = edge[...]
    rows = [acc[HIP * h : HIP * h + HI] for h in range(HEADS)] + [jnp.zeros((TAB_ROWS - HEADS * HI, 128), F32)]
    out[EDGE_ROWS:MSG, :] = jnp.concatenate(rows, axis=0).astype(BF)
    out[MSG:, :] = lat[...]


def pair_kernel(own, near, lat, corner, out, across):
    out[:EDGE_ROWS, :] = own[:EDGE_ROWS, :]
    out[EDGE_ROWS:, :] = (own[EDGE_ROWS:MSG, :].astype(F32) + near[EDGE_ROWS:MSG, :].astype(F32)).astype(BF)
    across[:LAT_ROWS, :] = lat[...]
    across[LAT_ROWS:, :] = (near[MSG:, :].astype(F32) + corner[...].astype(F32)).astype(BF)


def total_kernel(parts, out):
    total = parts[0].astype(F32)
    for i in range(1, parts.shape[0]):
        total = total + parts[i].astype(F32)
    total = total.astype(BF)
    for i in range(out.shape[0]):
        out[i] = total


def middle_kernel(pair, near, far, base_x, base_d, lat, corner, across, place, out_x, out_d, out_lat, out_near):
    edge = jnp.where(core_is(1, 3 * CUT), near[: 3 * CUT, :].astype(F32), far[: 3 * CUT, :].astype(F32))
    adds = [nn(place[...], e.astype(BF)) for e in unfold(edge, CUT)]
    for add, base, out in ((adds[0], base_x, out_x), (adds[1], base_d, out_d)):
        out[...] = (base[...].astype(F32) + add[:N_OWN]).astype(BF)
    whole = lat[...].astype(F32) + fold(adds[0][N_OWN:], adds[1][N_OWN:])
    out_lat[...] = jnp.where(band_is(False, LAT_ROWS), corner[...].astype(F32), whole).astype(BF)
    out_near[:LAT_ROWS, :] = across[LAT_ROWS:, :]
    out_near[LAT_ROWS:, :] = (pair[EDGE_ROWS:, :].astype(F32) + far[EDGE_ROWS:, :].astype(F32)).astype(BF)


def finish_kernel(base_x, base_d, lat, across, near, own, out_x, out_d, out_t):
    got = lat[...].astype(F32) + across[:LAT_ROWS, :].astype(F32) + near[:LAT_ROWS, :].astype(F32)
    for add, base, out in zip(unfold(got, N_LAT), (base_x, base_d), (out_x, out_d)):
        out[:, HALF_LAT:] = base[:, HALF_LAT:]
        add = add.reshape(WPL, HALF_LAT, COLS, C)
        out[:, :HALF_LAT] = (base[:, :HALF_LAT].astype(F32) + add).astype(BF)
    t = jnp.where(core_is(1, TAB_ROWS), near[LAT_ROWS:, :].astype(F32), own[LAT_ROWS:, :].astype(F32))
    for part in range(HI):
        width = min(128, NPOS - part * 128)
        for head in range(HEADS):
            row = head * HI + part
            out_t[head, :, part * 128 : part * 128 + width] = t[row : row + 1, :width]


def unpack_kernel(g, scale, qkv, proj, gain):
    k = scale
    full = [g[C * i : C * (i + 1), :].astype(F32) * k for i in range(6)]
    qkv[:, 0:128] = full[0]
    qkv[:, 128:256] = jnp.concatenate([full[4][:, :64], full[1][:, :64]], axis=1)
    qkv[:, 256:384] = jnp.concatenate([full[1][:, 64:], full[4][:, 64:]], axis=1)
    qkv[:, 384:512] = full[2]
    qkv[:, 512:576] = full[5][:, :64]
    proj[:, 0:128] = full[3]
    proj[:, 128:192] = full[5][:, 64:]
    tail = g[6 * C : 6 * C + 16, :].astype(F32) * k
    gain[:, :128] = tail[0:1]
    gain[:, 128:] = tail[1:2, : C - 128]


def call(kernel, out_shape, *args, scratch=(), cost=(0, 0), vmem=8):
    return pl.pallas_call(
        kernel,
        out_shape=out_shape,
        scratch_shapes=list(scratch),
        compiler_params=pltpu.CompilerParams(vmem_limit_bytes=vmem * 2**20),
        cost_estimate=pl.CostEstimate(flops=cost[0], bytes_accessed=cost[1], transcendentals=0),
    )(*args)


def sds(shape, dtype):
    return jax.ShapeDtypeStruct(shape, dtype)


def make(sizes):
    n_lat = sizes[0] * sizes[1] * sizes[2]
    n_lon = sizes[3] * sizes[4]
    n_plane = sizes[0] * sizes[2] * sizes[4]
    n_line = sizes[1] * sizes[3]
    piece = G_ROWS // n_plane
    band = sizes[1] * sizes[2]

    def route(d_lat, d_lon):
        return [
            (a * n_lon + b, (a + d_lat) % n_lat * n_lon + (b + d_lon) % n_lon)
            for a in range(n_lat)
            for b in range(n_lon)
        ]

    def first(pair):
        return pair[0] // n_lon % band == 0

    def last(pair):
        return pair[0] // n_lon % band == band - 1

    def hop(to, cores):
        return [
            (a * n_lon + zh * sizes[4] + c, a * n_lon + to(zh, c)[0] * sizes[4] + to(zh, c)[1])
            for a in range(n_lat)
            for zh in range(sizes[3])
            for c in cores
        ]

    def per_device(tokens, mask_ids, pos_index, norm_gain, w_qkv, w_proj, earth_bias, d_out):
        pick, back, place = (jnp.asarray(c) for c in constants())
        to_core, lat, edge = call(
            cut_kernel,
            (sds((LAT_ROWS, 128), BF), sds((LAT_ROWS, 128), BF), sds((SIDE_ROWS, 128), BF)),
            tokens,
            d_out,
        )
        sibling = lax.ppermute(to_core, AXES, hop(lambda zh, c: (zh, 1 - c), (0, 1)))
        to_lon, to_lat, to_line = call(
            join_kernel,
            (sds((SIDE_ROWS, 128), BF), sds((LAT_ROWS + CORNER_ROWS, 128), BF), sds((LINE_ROWS, 128), BF)),
            lat,
            edge,
            sibling,
        )
        south = route(-1, 0)
        from_lon = lax.ppermute(to_lon, AXES, hop(lambda zh, c: (1 - zh, 1), (0,)))
        corners = [r for r in route(-1, -1) if first(r) and r[0] % sizes[4] == 0]
        from_lat = lax.ppermute(to_lat, AXES, [r for r in south if not first(r)] + corners)
        from_line = lax.ppermute(to_line, AXES, [r for r in south if first(r) and r[0] % sizes[4] == 1])
        bias, hi, lo = call(
            tables_kernel,
            (sds((WIN, PAIRS), F32), sds((WIN, 256), jnp.int32), sds((WIN, 256), jnp.int32)),
            pos_index,
            earth_bias.transpose(1, 0, 2),
            scratch=[pltpu.VMEM((HEADS // 2, HI * 128), jnp.int32)],
            cost=(6 * 10**9, 10**6),
        )
        from_lon, from_lat, bias = lax.optimization_barrier((from_lon, from_lat, bias))
        from_corner = lax.ppermute(from_lon, AXES, [r for r in south if not first(r) and r[0] % sizes[4] == 1])
        from_line, from_corner = lax.optimization_barrier((from_line, from_corner))
        from_side = lax.ppermute(from_line, AXES, [r for r in hop(lambda zh, c: (zh, 0), (1,)) if last(r)])
        base_x, base_d, out_lat, out_corner, out_edge, grads, d_bias = call(
            block_kernel,
            (
                sds((N_OWN, C), BF),
                sds((N_OWN, C), BF),
                sds((LAT_ROWS, 128), BF),
                sds((LAT_ROWS, 128), BF),
                sds((EDGE_ROWS, 128), BF),
                sds((G_ROWS, 128), BF),
                sds((WIN, PAIRS), F32),
            ),
            tokens.reshape(N_OWN, C),
            d_out.reshape(N_OWN, C),
            sibling,
            from_lon,
            from_lat,
            from_line,
            from_side,
            from_corner,
            pick,
            back,
            norm_gain.reshape(1, C),
            w_qkv,
            w_proj,
            mask_ids.transpose(1, 0, 2),
            bias,
            vmem=20,
            cost=(6 * 10**9, 10**6),
        )
        parts = lax.all_to_all(grads.reshape(n_plane, piece, 128), PLANE, 0, 0)
        own = call(
            scatter_kernel,
            sds((MSG + LAT_ROWS, 128), BF),
            d_bias,
            hi,
            lo,
            out_edge,
            out_lat,
            scratch=[pltpu.VMEM((HEADS * HIP, 128), F32)],
            cost=(8 * 10**9, 10**6),
        )
        parts, own = lax.optimization_barrier((parts, own))
        near = lax.ppermute(own, AXES, hop(lambda zh, c: (zh, 1 - c), (0, 1)))
        part = call(total_kernel, sds((n_line, piece, 128), BF), parts, cost=(10**9, 10**6))
        line = lax.all_to_all(part, LINE, 0, 0)
        pair, across = call(
            pair_kernel,
            (sds((MSG, 128), BF), sds((2 * LAT_ROWS, 128), BF)),
            own,
            near,
            out_lat,
            out_corner,
            cost=(10**9, 10**6),
        )
        far = lax.ppermute(pair, AXES, hop(lambda zh, c: (1 - zh, 0), (1,)))
        across = lax.ppermute(across, AXES, [r for r in route(1, 0) if last(r) and r[0] % sizes[4] == 0])
        line, pair = lax.optimization_barrier((line, pair))
        total = call(total_kernel, sds((n_plane, piece, 128), BF), line, cost=(10**9, 10**6))
        whole = lax.all_to_all(total, PLANE, 0, 0)
        base_x, base_d, to_lat, to_near = call(
            middle_kernel,
            (
                sds((N_OWN, C), BF),
                sds((N_OWN, C), BF),
                sds((LAT_ROWS, 128), BF),
                sds((LAT_ROWS + TAB_ROWS, 128), BF),
            ),
            pair,
            near,
            far,
            base_x,
            base_d,
            out_lat,
            out_corner,
            across,
            place,
            cost=(20 * 10**9, 10**6),
        )
        corners = [r for r in route(1, 1) if last(r) and r[0] % sizes[4] == 1]
        from_lat = lax.ppermute(to_lat, AXES, [r for r in route(1, 0) if not last(r)] + corners)
        from_near = lax.ppermute(to_near, AXES, hop(lambda zh, c: (zh, 1), (0,)))
        scale = float(n_lat * n_lon * N_OWN) ** -0.5
        qkv, proj, gain = call(
            lambda g, a, b, c: unpack_kernel(g, scale, a, b, c),
            (sds((C, 3 * C), F32), sds((C, C), F32), sds((1, C), F32)),
            whole.reshape(G_ROWS, 128),
        )
        base_x, qkv = lax.optimization_barrier((base_x, qkv))
        updated, d_tokens, d_table = call(
            finish_kernel,
            (
                sds((WPL, ROWS, COLS, C), BF),
                sds((WPL, ROWS, COLS, C), BF),
                sds((HEADS, 1, NPOS), F32),
            ),
            base_x.reshape(WPL, ROWS, COLS, C),
            base_d.reshape(WPL, ROWS, COLS, C),
            from_lat,
            across,
            from_near,
            to_near,
            cost=(20 * 10**9, 10**6),
        )
        return updated, d_tokens, qkv, proj, gain.reshape(C), d_table.transpose(1, 0, 2)

    return per_device


def solution(mesh):
    fine = jax.sharding.Mesh(mesh.devices.reshape(SPLIT), AXES)
    placed = (
        P(None, LAT_AXES, LON_AXES, None),
        P(None, LAT_AXES, LON_AXES),
        P(),
        P(),
        P(),
        P(),
        P(LAT_AXES, None, None),
        P(None, LAT_AXES, LON_AXES, None),
    )
    return jax.shard_map(
        make(SPLIT),
        mesh=fine,
        in_specs=placed,
        out_specs=(
            P(None, LAT_AXES, LON_AXES, None),
            P(None, LAT_AXES, LON_AXES, None),
            P(),
            P(),
            P(),
            P(LAT_AXES, None, None),
        ),
        check_vma=False,
    )
```

```python
import jax
import jax.numpy as jnp
import numpy as np
from jax import lax
from jax.experimental import pallas as pl
from jax.experimental.pallas import tpu as pltpu
from jax.sharding import PartitionSpec as P

BF = jnp.bfloat16
F32 = jnp.float32

WPL, WLAT, WLON = 2, 6, 12
HALF_LAT, HALF_LON = WLAT // 2, WLON // 2
ROWS, COLS = 6, 24
C = 192
HEADS = 6
HEAD = C // HEADS
WIN = WPL * WLAT * WLON
WINDOWS = COLS // WLON
NPOS = 3312
HI = -(-NPOS // 128)
HIP = 32
EDGE = 8
N_OWN = WPL * ROWS * COLS
N_LAT = WPL * HALF_LAT * COLS
N_EDGE = WPL * HALF_LAT * EDGE
N_ALL = N_OWN + N_LAT + 2 * N_EDGE
MAIN = 128
REST = WIN - MAIN
PAIRS = HEADS * MAIN + 128
EPS = 1e-05
SCALE = HEAD**-0.5
NEG = -1000000000.0
G_ROWS = 1280
CUT = WPL * ROWS * HALF_LON
EDGE_ROWS = 3 * CUT + 8
TAB_ROWS = 160
MSG = EDGE_ROWS + TAB_ROWS
LAT_ROWS = 3 * N_LAT
CORNER_ROWS = 3 * N_EDGE
SIDE_ROWS = 2 * CORNER_ROWS
LINE_ROWS = 2 * LAT_ROWS + CORNER_ROWS

SPLIT = (4, 8, 4, 2, 2)
AXES = ("x", "zl", "y", "zh", "c")
LAT_AXES = ("x", "zl", "y")
LON_AXES = ("zh", "c")
PLANE = ("x", "y", "c")
LINE = ("zh", "zl")


N_BACK = N_OWN + 2 * N_LAT + CUT


def source_rows():
    at = np.zeros((WINDOWS, WIN), np.int32)
    for level in range(WPL):
        for row in range(ROWS):
            for col in range(COLS):
                from_level = (level + WPL // 2) % WPL
                r, c = row + HALF_LAT, col + HALF_LON
                if r < ROWS and c < COLS:
                    src = from_level * ROWS * COLS + r * COLS + c
                elif c < COLS:
                    src = N_OWN + from_level * HALF_LAT * COLS + (r - ROWS) * COLS + c
                elif r < ROWS:
                    src = N_OWN + N_LAT + from_level * HALF_LAT * EDGE + (r - HALF_LAT) * EDGE + c - COLS
                else:
                    src = N_OWN + N_LAT + N_EDGE + from_level * HALF_LAT * EDGE + (r - ROWS) * EDGE + c - COLS
                at[col // WLON, level * WLAT * WLON + row * WLON + col % WLON] = src
    return at


def constants():
    at = source_rows()
    pick = np.zeros((WINDOWS, WIN, N_ALL), np.float32)
    for w in range(WINDOWS):
        pick[w, np.arange(WIN), at[w]] = 1.0
    back = np.zeros((WINDOWS, N_BACK, WIN), np.float32)
    back[:, : N_OWN + N_LAT] = pick.transpose(0, 2, 1)[:, : N_OWN + N_LAT]
    place = np.zeros((N_OWN + N_LAT, CUT), np.float32)
    for level in range(WPL):
        for row in range(ROWS):
            for col in range(HALF_LON):
                edge = N_OWN + N_LAT + level * HALF_LAT * EDGE + (row % HALF_LAT) * EDGE + col
                edge += 0 if row >= HALF_LAT else N_EDGE
                to = level * ROWS * HALF_LON + row * HALF_LON + col
                back[:, N_OWN + N_LAT + to] = pick[:, :, edge]
                if row >= HALF_LAT:
                    place[level * ROWS * COLS + row * COLS + col, to] = 1.0
                else:
                    at_lat = level * HALF_LAT * COLS + row * COLS + col
                    place[N_OWN + at_lat, to] = 1.0
                    back[:, N_OWN + N_LAT + CUT + at_lat] = pick[:, :, edge]
    return pick.astype(BF), back.astype(BF), place.astype(BF)


def dot(a, b, dims):
    return lax.dot_general(a, b, ((dims[:1], dims[1:]), ((), ())), preferred_element_type=F32)


def nn(a, b):
    return dot(a, b, (1, 0))


def nt(a, b):
    return dot(a, b, (1, 1))


def eye(n):
    return (lax.broadcasted_iota(jnp.int32, (n, n), 0) == lax.broadcasted_iota(jnp.int32, (n, n), 1)).astype(F32).astype(BF)


def spread():
    lane = lax.broadcasted_iota(jnp.int32, (256, WIN), 0)
    query = lax.broadcasted_iota(jnp.int32, (256, WIN), 1)
    held = jnp.where(lane < MAIN, lane, MAIN + lax.bitwise_and(lane, REST - 1))
    return ((held == query) & (lane < MAIN + HEADS * REST)).astype(F32).astype(BF)


def fold(a, b):
    return jnp.concatenate([a[:, :128], b[:, :128], jnp.concatenate([a[:, 128:], b[:, 128:]], axis=1)], axis=0)


def unfold(both, n):
    return [
        jnp.concatenate([both[n * i : n * (i + 1)], both[2 * n : 3 * n, 64 * i : 64 * (i + 1)]], axis=1) for i in range(2)
    ]


def core_is(core, rows):
    return lax.broadcasted_iota(jnp.int32, (rows, 128), 0) * 0 + lax.axis_index("c") == core


def band_is(first, rows):
    at = lax.axis_index("zl") * lax.axis_size("y") + lax.axis_index("y")
    want = 0 if first else lax.axis_size("zl") * lax.axis_size("y") - 1
    return lax.broadcasted_iota(jnp.int32, (rows, 128), 0) * 0 + at == want


def cut_kernel(tokens, d_out, to_core, lat, edge, to_diag):
    both = (tokens[...].astype(F32), d_out[...].astype(F32))
    top = fold(*(a[:, :HALF_LAT].reshape(N_LAT, C) for a in both))
    corner = fold(*(a[:, :HALF_LAT, :EDGE].reshape(N_EDGE, C) for a in both))
    lon = fold(*(a[:, HALF_LAT:, :EDGE].reshape(N_EDGE, C) for a in both))
    side = jnp.concatenate([corner, lon], axis=0)
    lat[...] = top.astype(BF)
    edge[...] = side.astype(BF)
    to_diag[...] = corner.astype(BF)
    spare = jnp.zeros((LAT_ROWS - SIDE_ROWS, 128), F32)
    to_core[...] = jnp.where(core_is(1, LAT_ROWS), jnp.concatenate([side, spare], axis=0), top).astype(BF)


def join_kernel(lat, corner, sibling, to_lat, to_line):
    to_lat[:LAT_ROWS, :] = lat[...]
    to_lat[LAT_ROWS:, :] = sibling[:CORNER_ROWS, :]
    to_line[:LAT_ROWS, :] = lat[...]
    to_line[LAT_ROWS : 2 * LAT_ROWS, :] = sibling[...]
    to_line[2 * LAT_ROWS :, :] = corner[...]


def tables_kernel(pos, table, bias, hi_out, lo_out, scr):
    one = eye(WIN)
    idx = pos[...]
    hi = lax.shift_right_logical(idx, 7)
    lo = lax.bitwise_and(idx, 127)
    sp = spread()
    hi2 = nt(nt(one, hi.astype(F32).astype(BF)).astype(BF), sp)
    lo2 = nt(nt(one, lo.astype(F32).astype(BF)).astype(BF), sp)
    hi2 = hi2.astype(jnp.int32)
    lo2 = lo2.astype(jnp.int32)
    hi_out[...] = hi2
    lo_out[...] = lo2

    steps = []
    for pair in range(HEADS // 2):
        words = []
        for head in (2 * pair, 2 * pair + 1):
            row = table[head]
            unit = jnp.maximum(jnp.max(jnp.abs(row), axis=1, keepdims=True), 1e-20) * (1.0 / 32767.0)
            fixed = row * (1.0 / unit)
            fixed = jnp.floor(jnp.clip(fixed + 0.5, -32767.0, 32767.0)).astype(jnp.int32)
            steps.append(unit)
            words.append(fixed)
        scr[pair : pair + 1, :NPOS] = lax.shift_left(words[0], 16) | lax.bitwise_and(words[1], 65535)
    scr[:, NPOS:] = jnp.zeros((HEADS // 2, HI * 128 - NPOS), jnp.int32)

    def look(h_idx, l_idx):
        acc = [[jnp.zeros((8, 128), jnp.int32) for _ in h_idx] for _ in range(HEADS // 2)]
        for part in range(HI):
            hit = [h == part for h in h_idx]
            for pair in range(HEADS // 2):
                row = jnp.broadcast_to(scr[pair : pair + 1, part * 128 : part * 128 + 128], (8, 128))
                for i, l in enumerate(l_idx):
                    got = jnp.take_along_axis(row, l, axis=1, mode="promise_in_bounds")
                    acc[pair][i] = jnp.where(hit[i], got, acc[pair][i])
        out = []
        for pair in range(HEADS // 2):
            high = [lax.shift_right_arithmetic(v, 16) for v in acc[pair]]
            low = [lax.shift_right_arithmetic(lax.shift_left(v, 16), 16) for v in acc[pair]]
            out.append([v.astype(F32) * steps[2 * pair] for v in high])
            out.append([v.astype(F32) * steps[2 * pair + 1] for v in low])
        return out

    def step(block, carry):
        rows = [pl.ds(pl.multiple_of(block * 24 + 8 * i, 8), 8) for i in range(3)]
        acc = look([hi_out[r, :128] for r in rows], [lo_out[r, :128] for r in rows])
        for head in range(HEADS):
            for i, r in enumerate(rows):
                bias[r, MAIN * head : MAIN * (head + 1)] = acc[head][i]
        return carry

    lax.fori_loop(0, WIN // 24, step, 0)
    pad = jnp.zeros((REST, 256 - WIN), jnp.int32)
    h_rest = jnp.concatenate([hi[MAIN:], pad], axis=1)
    l_rest = jnp.concatenate([lo[MAIN:], pad], axis=1)
    tiles = [(slice(8 * i, 8 * i + 8), slice(128 * j, 128 * j + 128)) for i in range(2) for j in range(2)]
    acc = look([h_rest[t] for t in tiles], [l_rest[t] for t in tiles])
    rest = [jnp.concatenate([jnp.concatenate(a[2 * i : 2 * i + 2], axis=1) for i in range(2)], axis=0) for a in acc]
    rest = jnp.concatenate(rest + [jnp.zeros((128 - HEADS * REST, 256), F32)], axis=0)
    bias[:, HEADS * MAIN :] = rest.T[:WIN]


def by_head(x):
    lane = lax.broadcasted_iota(jnp.int32, (1, C), 1)
    keep = [((lane >= HEAD * h) & (lane < HEAD * (h + 1))).astype(F32).astype(BF) for h in range(HEADS)]
    parts = [x[:MAIN] * keep[h] for h in range(HEADS)]
    parts += [x[MAIN:] * keep[h] for h in range(HEADS)]
    parts.append(jnp.zeros((PAIRS - HEADS * WIN, C), BF))
    return jnp.concatenate(parts, axis=0)


def heads_apart(left, right, scale):
    main = [
        nn(left[HEAD * h : HEAD * (h + 1)], right[:, MAIN * h : MAIN * (h + 1)]) for h in range(HEADS)
    ]
    main = (jnp.concatenate(main, axis=0) * scale).astype(BF)
    rest = nn(left, right[:, HEADS * MAIN :]) * scale
    row = lax.broadcasted_iota(jnp.int32, (C, 128), 0)
    lane = lax.broadcasted_iota(jnp.int32, (C, 128), 1)
    rest = jnp.where(lax.div(row, HEAD) == lax.div(lane, REST), rest, 0.0).astype(BF)
    fold_l = lax.broadcasted_iota(jnp.int32, (128, REST), 0)
    fold_a = lax.broadcasted_iota(jnp.int32, (128, REST), 1)
    fold = (lax.rem(fold_l, REST) == fold_a).astype(F32).astype(BF)
    rest = nn(rest, fold).astype(BF)
    return jnp.concatenate([main, rest], axis=1)


def regions(mask):
    sp = spread()
    out = []
    lab = [mask[row, level : level + 1, :].astype(F32) for level in range(WPL) for row in range(ROWS)]
    lab = jnp.concatenate(lab, axis=0).astype(BF)
    for w in range(WINDOWS):
        lane = lax.broadcasted_iota(jnp.int32, (COLS, WIN), 1)
        col = lax.broadcasted_iota(jnp.int32, (COLS, WIN), 0)
        across = (lax.rem(lane, WLON) + w * WLON == col).astype(F32).astype(BF)
        wide = nn(lab, across)
        r = lax.broadcasted_iota(jnp.int32, (WPL * ROWS, WIN), 0)
        a = lax.broadcasted_iota(jnp.int32, (WPL * ROWS, WIN), 1)
        row = jnp.sum(jnp.where(lax.div(a, WLON) == r, wide, 0.0), axis=0, keepdims=True)
        row = jnp.broadcast_to(row, (WIN, WIN)).astype(BF)
        down = nt(eye(WIN), row)
        over = nt(row, sp)
        out.append(jnp.where(over == jnp.broadcast_to(down[:, :1], (WIN, 256)), 0.0, NEG))
    return out


def block_kernel(
    own_x, own_d, sibling, from_lon, from_lat, from_line, from_side, from_diag, pick, back, gain, w_qkv, wp, mask, bias,
    base_x, base_d, out_lat, out_corner, out_edge, grads, d_bias,
):
    f32 = lambda ref, start, size: ref[start : start + size, :].astype(F32)
    over = f32(from_line, 0, LAT_ROWS) + f32(from_side, LAT_ROWS, LAT_ROWS)
    lat = unfold(jnp.where(band_is(False, LAT_ROWS), over, f32(from_lat, 0, LAT_ROWS)), N_LAT)
    lon = f32(sibling, CORNER_ROWS, CORNER_ROWS), f32(from_lon, CORNER_ROWS, CORNER_ROWS)
    lon = unfold(jnp.where(core_is(0, CORNER_ROWS), *lon), N_EDGE)
    inner = jnp.where(
        band_is(False, CORNER_ROWS), f32(from_side, 2 * LAT_ROWS, CORNER_ROWS), f32(from_lat, LAT_ROWS, CORNER_ROWS)
    )
    diag = unfold(jnp.where(core_is(0, CORNER_ROWS), inner, f32(from_diag, 0, CORNER_ROWS)), N_EDGE)
    x_all, d_all = (
        jnp.concatenate([own[...], lat[i].astype(BF), lon[i].astype(BF), diag[i].astype(BF)], axis=0)
        for i, own in enumerate((own_x, own_d))
    )
    eye_c = eye(C)
    eye_w = eye(WIN)
    g = jnp.sum(eye_c.astype(F32) * gain[...], axis=1, keepdims=True)
    w3 = [w_qkv[:, C * i : C * (i + 1)] for i in range(3)]
    w3t = [None] + [nt(eye_c, w).astype(BF) for w in w3[1:]]
    wpt = nt(eye_c, wp[...]).astype(BF)
    blocked = regions(mask)
    sums = [jnp.zeros((C, C), F32) for _ in range(4)]
    d_gain = jnp.zeros((C, 1), F32)
    x_back = jnp.zeros((N_BACK, C), F32)
    d_back = jnp.zeros((N_BACK, C), F32)
    for w in range(WINDOWS):
        x = nn(pick[w], x_all).astype(BF)
        d_proj = nn(pick[w], d_all).astype(BF)
        xt = nt(eye_c, x)
        mean = jnp.sum(xt, axis=0, keepdims=True) * (1.0 / C)
        centered = xt - mean
        var = jnp.sum(centered * centered, axis=0, keepdims=True) * (1.0 / C)
        rstd = lax.rsqrt(var + EPS)
        xhat = centered * rstd
        nt_w = (xhat * g).astype(BF)
        n_w = nt(eye_w, nt_w).astype(BF)
        q = nn(n_w, w3[0]).astype(BF)
        k = nn(n_w, w3[1]).astype(BF)
        v = nn(n_w, w3[2]).astype(BF)
        kt = nn(w3t[1], nt_w).astype(BF)
        vt = nn(w3t[2], nt_w).astype(BF)
        qm = by_head(q)
        dm = by_head(nt(d_proj, wp[...]).astype(BF))
        far = jnp.concatenate([blocked[w][:, :MAIN]] * HEADS + [blocked[w][:, MAIN:]], axis=1)
        s = nt(k, qm) * SCALE + bias[...] + far
        e = jnp.exp(s - jnp.max(s, axis=0, keepdims=True))
        p = e * (1.0 / jnp.sum(e, axis=0, keepdims=True))
        attn = p.astype(BF)
        d_attn = nt(v, dm)
        pd = p * d_attn
        ds = pd - p * jnp.sum(pd, axis=0, keepdims=True)
        dsb = ds.astype(BF)
        if w == 0:
            d_bias[...] = ds
        else:
            d_bias[...] += ds
        mixed_t = heads_apart(vt, attn, 1.0)
        dq_t = heads_apart(kt, dsb, SCALE)
        dk = (nn(dsb, qm) * SCALE).astype(BF)
        dv = nn(attn, dm).astype(BF)
        proj_t = nn(wpt, mixed_t).astype(BF)
        x_back = x_back + nt(back[w], proj_t)
        sums[0] = sums[0] + nt(nt_w, dq_t)
        sums[1] = sums[1] + nn(nt_w, dk)
        sums[2] = sums[2] + nn(nt_w, dv)
        sums[3] = sums[3] + nn(mixed_t, d_proj)
        dn = nn(w3[0], dq_t) + nt(w3[1], dk) + nt(w3[2], dv)
        dn = dn.astype(BF).astype(F32)
        d_gain = d_gain + jnp.sum(dn * xhat, axis=1, keepdims=True)
        dy = dn * g
        m1 = jnp.sum(dy, axis=0, keepdims=True) * (1.0 / C)
        m2 = jnp.sum(dy * xhat, axis=0, keepdims=True) * (1.0 / C)
        dx = (rstd * (dy - m1 - xhat * m2)).astype(BF)
        d_back = d_back + nt(back[w], dx)
    for i in range(4):
        grads[C * i : C * (i + 1), :] = sums[i][:, :128].astype(BF)
    for i in range(2):
        pair = jnp.concatenate([sums[2 * i][:, 128:], sums[2 * i + 1][:, 128:]], axis=1)
        grads[C * (4 + i) : C * (5 + i), :] = pair.astype(BF)
    row = jnp.sum(eye_c.astype(F32) * d_gain, axis=0, keepdims=True)
    tail = jnp.concatenate([row[:, 128:], jnp.zeros((1, 256 - C), F32)], axis=1)
    grads[6 * C :, :] = jnp.concatenate([row[:, :128], tail, jnp.zeros((126, 128), F32)], axis=0).astype(BF)
    for i, (total, own, base) in enumerate(((x_back, own_x, base_x), (d_back, own_d, base_d))):
        base[...] = (own[...].astype(F32) + total[:N_OWN]).astype(BF)
    parts = ((out_lat, N_OWN, N_LAT), (out_edge, N_OWN + N_LAT, CUT), (out_corner, N_OWN + N_LAT + CUT, N_LAT))
    for out, start, size in parts:
        both = fold(x_back[start : start + size], d_back[start : start + size])
        spare = out.shape[0] - both.shape[0]
        if spare:
            both = jnp.concatenate([both, jnp.zeros((spare, 128), F32)], axis=0)
        out[...] = both.astype(BF)


def scatter_kernel(d_bias, hi, lo, edge, lat, out, acc):
    acc[...] = jnp.zeros_like(acc)

    def step(block, carry):
        rows = pl.ds(pl.multiple_of(block * 8, 8), 8)
        h_all = hi[rows, :]
        l_all = lo[rows, :]
        d_all = d_bias[rows, :]
        part = lax.broadcasted_iota(jnp.int32, (HIP, 256), 0)
        group = lax.shift_right_logical(lax.broadcasted_iota(jnp.int32, (HIP, 128), 1), 4)
        place = lax.broadcasted_iota(jnp.int32, (128, 256), 0)
        total = acc[...]
        for i in range(8):
            hit = jnp.broadcast_to(h_all[i : i + 1], (HIP, 256)) == part
            rest = jnp.broadcast_to(d_all[i : i + 1, HEADS * MAIN :], (HIP, 128))
            rest = jnp.where(hit[:, 128:], rest, 0.0)
            many = []
            for head in range(HEADS):
                main = jnp.broadcast_to(d_all[i : i + 1, MAIN * head : MAIN * (head + 1)], (HIP, 128))
                main = jnp.where(hit[:, :128], main, 0.0)
                many.append(jnp.concatenate([main, jnp.where(group == head, rest, 0.0)], axis=1))
            many = jnp.concatenate(many, axis=0).astype(BF)
            spot = (jnp.broadcast_to(l_all[i : i + 1], (128, 256)) == place).astype(F32).astype(BF)
            total = total + nt(many, spot)
        acc[...] = total
        return carry

    lax.fori_loop(0, WIN // 8, step, 0)
    out[:EDGE_ROWS, :] = edge[...]
    rows = [acc[HIP * h : HIP * h + HI] for h in range(HEADS)] + [jnp.zeros((TAB_ROWS - HEADS * HI, 128), F32)]
    out[EDGE_ROWS:MSG, :] = jnp.concatenate(rows, axis=0).astype(BF)
    out[MSG:, :] = lat[...]


def pair_kernel(own, near, out):
    out[:EDGE_ROWS, :] = own[:EDGE_ROWS, :]
    out[EDGE_ROWS:, :] = (own[EDGE_ROWS:MSG, :].astype(F32) + near[EDGE_ROWS:MSG, :].astype(F32)).astype(BF)


def line_kernel(near, lat, corner, across):
    across[:LAT_ROWS, :] = lat[...]
    across[LAT_ROWS:, :] = (near[MSG:, :].astype(F32) + corner[...].astype(F32)).astype(BF)


def beside_kernel(across, out):
    out[...] = across[LAT_ROWS:, :]


def total_kernel(parts, out):
    total = parts[0].astype(F32)
    for i in range(1, parts.shape[0]):
        total = total + parts[i].astype(F32)
    total = total.astype(BF)
    for i in range(out.shape[0]):
        out[i] = total


def middle_kernel(pair, near, far, base_x, base_d, lat, corner, place, out_x, out_d, out_lat, out_near):
    edge = jnp.where(core_is(1, 3 * CUT), near[: 3 * CUT, :].astype(F32), far[: 3 * CUT, :].astype(F32))
    adds = [nn(place[...], e.astype(BF)) for e in unfold(edge, CUT)]
    for add, base, out in ((adds[0], base_x, out_x), (adds[1], base_d, out_d)):
        out[...] = (base[...].astype(F32) + add[:N_OWN]).astype(BF)
    whole = lat[...].astype(F32) + fold(adds[0][N_OWN:], adds[1][N_OWN:])
    out_lat[LAT_ROWS:, :] = jnp.zeros((16, 128), BF)
    out_lat[:LAT_ROWS, :] = jnp.where(band_is(False, LAT_ROWS), corner[...].astype(F32), whole).astype(BF)
    out_near[...] = (pair[EDGE_ROWS:, :].astype(F32) + far[EDGE_ROWS:, :].astype(F32)).astype(BF)


def finish_kernel(base_x, base_d, lat, across, beside, near, own, out_x, out_d, out_t):
    got = lat[:LAT_ROWS, :].astype(F32) + across[:LAT_ROWS, :].astype(F32) + beside[...].astype(F32)
    for add, base, out in zip(unfold(got, N_LAT), (base_x, base_d), (out_x, out_d)):
        out[:, HALF_LAT:] = base[:, HALF_LAT:]
        add = add.reshape(WPL, HALF_LAT, COLS, C)
        out[:, :HALF_LAT] = (base[:, :HALF_LAT].astype(F32) + add).astype(BF)
    t = jnp.where(core_is(1, TAB_ROWS), near[...].astype(F32), own[...].astype(F32))
    for part in range(HI):
        width = min(128, NPOS - part * 128)
        for head in range(HEADS):
            row = head * HI + part
            out_t[head, :, part * 128 : part * 128 + width] = t[row : row + 1, :width]


def unpack_kernel(g, scale, qkv, proj, gain):
    k = scale
    full = [g[C * i : C * (i + 1), :].astype(F32) * k for i in range(6)]
    qkv[:, 0:128] = full[0]
    qkv[:, 128:256] = jnp.concatenate([full[4][:, :64], full[1][:, :64]], axis=1)
    qkv[:, 256:384] = jnp.concatenate([full[1][:, 64:], full[4][:, 64:]], axis=1)
    qkv[:, 384:512] = full[2]
    qkv[:, 512:576] = full[5][:, :64]
    proj[:, 0:128] = full[3]
    proj[:, 128:192] = full[5][:, 64:]
    tail = g[6 * C : 6 * C + 16, :].astype(F32) * k
    gain[:, :128] = tail[0:1]
    gain[:, 128:] = tail[1:2, : C - 128]


def call(kernel, out_shape, *args, scratch=(), cost=(0, 0), vmem=8):
    return pl.pallas_call(
        kernel,
        out_shape=out_shape,
        scratch_shapes=list(scratch),
        compiler_params=pltpu.CompilerParams(vmem_limit_bytes=vmem * 2**20),
        cost_estimate=pl.CostEstimate(flops=cost[0], bytes_accessed=cost[1], transcendentals=0),
    )(*args)


def sds(shape, dtype):
    return jax.ShapeDtypeStruct(shape, dtype)


def make(sizes):
    n_lat = sizes[0] * sizes[1] * sizes[2]
    n_lon = sizes[3] * sizes[4]
    n_plane = sizes[0] * sizes[2] * sizes[4]
    n_line = sizes[1] * sizes[3]
    piece = G_ROWS // n_plane
    band = sizes[1] * sizes[2]

    def route(d_lat, d_lon):
        return [
            (a * n_lon + b, (a + d_lat) % n_lat * n_lon + (b + d_lon) % n_lon)
            for a in range(n_lat)
            for b in range(n_lon)
        ]

    def first(pair):
        return pair[0] // n_lon % band == 0

    def last(pair):
        return pair[0] // n_lon % band == band - 1

    def hop(to, cores):
        return [
            (a * n_lon + zh * sizes[4] + c, a * n_lon + to(zh, c)[0] * sizes[4] + to(zh, c)[1])
            for a in range(n_lat)
            for zh in range(sizes[3])
            for c in cores
        ]

    def per_device(tokens, mask_ids, pos_index, norm_gain, w_qkv, w_proj, earth_bias, d_out):
        pick, back, place = (jnp.asarray(c) for c in constants())
        to_core, lat, edge, to_diag = call(
            cut_kernel,
            (
                sds((LAT_ROWS, 128), BF),
                sds((LAT_ROWS, 128), BF),
                sds((SIDE_ROWS, 128), BF),
                sds((CORNER_ROWS, 128), BF),
            ),
            tokens,
            d_out,
        )
        sibling = lax.ppermute(to_core, AXES, hop(lambda zh, c: (zh, 1 - c), (0, 1)))
        from_lon = lax.ppermute(edge, AXES, hop(lambda zh, c: (1 - zh, 1), (0,)))
        from_diag = lax.ppermute(to_diag, AXES, [r for r in route(-1, -1) if r[0] % sizes[4] == 0])
        to_lat, to_line = call(
            join_kernel,
            (sds((LAT_ROWS + CORNER_ROWS, 128), BF), sds((LINE_ROWS, 128), BF)),
            lat,
            to_diag,
            sibling,
        )
        south = route(-1, 0)
        from_lat = lax.ppermute(to_lat, AXES, [r for r in south if not first(r)])
        from_line = lax.ppermute(to_line, AXES, [r for r in south if first(r) and r[0] % sizes[4] == 1])
        bias, hi, lo = call(
            tables_kernel,
            (sds((WIN, PAIRS), F32), sds((WIN, 256), jnp.int32), sds((WIN, 256), jnp.int32)),
            pos_index,
            earth_bias.transpose(1, 0, 2),
            scratch=[pltpu.VMEM((HEADS // 2, HI * 128), jnp.int32)],
            cost=(6 * 10**9, 10**6),
        )
        received = (from_line, from_lon, from_diag, from_lat, bias)
        from_line, from_lon, from_diag, from_lat, bias = lax.optimization_barrier(received)
        from_side = lax.ppermute(from_line, AXES, [r for r in hop(lambda zh, c: (zh, 0), (1,)) if last(r)])
        base_x, base_d, out_lat, out_corner, out_edge, grads, d_bias = call(
            block_kernel,
            (
                sds((N_OWN, C), BF),
                sds((N_OWN, C), BF),
                sds((LAT_ROWS, 128), BF),
                sds((LAT_ROWS, 128), BF),
                sds((EDGE_ROWS, 128), BF),
                sds((G_ROWS, 128), BF),
                sds((WIN, PAIRS), F32),
            ),
            tokens.reshape(N_OWN, C),
            d_out.reshape(N_OWN, C),
            sibling,
            from_lon,
            from_lat,
            from_line,
            from_side,
            from_diag,
            pick,
            back,
            norm_gain.reshape(1, C),
            w_qkv,
            w_proj,
            mask_ids.transpose(1, 0, 2),
            bias,
            vmem=20,
            cost=(6 * 10**9, 10**6),
        )
        parts = lax.all_to_all(grads.reshape(n_plane, piece, 128), PLANE, 0, 0)
        own = call(
            scatter_kernel,
            sds((MSG + LAT_ROWS, 128), BF),
            d_bias,
            hi,
            lo,
            out_edge,
            out_lat,
            scratch=[pltpu.VMEM((HEADS * HIP, 128), F32)],
            cost=(8 * 10**9, 10**6),
        )
        parts, own = lax.optimization_barrier((parts, own))
        near = lax.ppermute(own, AXES, hop(lambda zh, c: (zh, 1 - c), (0, 1)))
        part = call(total_kernel, sds((n_line, piece, 128), BF), parts, cost=(10**9, 10**6))
        line = lax.all_to_all(part, LINE, 0, 0)
        pair = call(pair_kernel, sds((MSG, 128), BF), own, near, cost=(10**9, 10**6))
        far = lax.ppermute(pair, AXES, hop(lambda zh, c: (1 - zh, 0), (1,)))
        across = call(line_kernel, sds((2 * LAT_ROWS, 128), BF), near, out_lat, out_corner, cost=(10**9, 10**6))
        across = lax.ppermute(across, AXES, [r for r in route(1, 0) if last(r) and r[0] % sizes[4] == 0])
        line, pair = lax.optimization_barrier((line, pair))
        total = call(total_kernel, sds((n_plane, piece, 128), BF), line, cost=(10**9, 10**6))
        whole = lax.all_to_all(total, PLANE, 0, 0)
        base_x, base_d, to_lat, to_near = call(
            middle_kernel,
            (
                sds((N_OWN, C), BF),
                sds((N_OWN, C), BF),
                sds((LAT_ROWS + 16, 128), BF),
                sds((TAB_ROWS, 128), BF),
            ),
            pair,
            near,
            far,
            base_x,
            base_d,
            out_lat,
            out_corner,
            place,
            cost=(20 * 10**9, 10**6),
        )
        corners = [r for r in route(1, 1) if last(r) and r[0] % sizes[4] == 1]
        from_lat = lax.ppermute(to_lat, AXES, [r for r in route(1, 0) if not last(r)] + corners)
        from_near = lax.ppermute(to_near, AXES, hop(lambda zh, c: (zh, 1), (0,)))
        across, from_near = lax.optimization_barrier((across, from_near))
        beside = call(beside_kernel, sds((LAT_ROWS, 128), BF), across, cost=(10**9, 10**6))
        beside = lax.ppermute(beside, AXES, [r for r in hop(lambda zh, c: (zh, 1), (0,)) if first(r)])
        scale = float(n_lat * n_lon * N_OWN) ** -0.5
        qkv, proj, gain = call(
            lambda g, a, b, c: unpack_kernel(g, scale, a, b, c),
            (sds((C, 3 * C), F32), sds((C, C), F32), sds((1, C), F32)),
            whole.reshape(G_ROWS, 128),
        )
        base_x, qkv = lax.optimization_barrier((base_x, qkv))
        updated, d_tokens, d_table = call(
            finish_kernel,
            (
                sds((WPL, ROWS, COLS, C), BF),
                sds((WPL, ROWS, COLS, C), BF),
                sds((HEADS, 1, NPOS), F32),
            ),
            base_x.reshape(WPL, ROWS, COLS, C),
            base_d.reshape(WPL, ROWS, COLS, C),
            from_lat,
            across,
            beside,
            from_near,
            to_near,
            cost=(20 * 10**9, 10**6),
        )
        return updated, d_tokens, qkv, proj, gain.reshape(C), d_table.transpose(1, 0, 2)

    return per_device


def solution(mesh):
    fine = jax.sharding.Mesh(mesh.devices.reshape(SPLIT), AXES)
    placed = (
        P(None, LAT_AXES, LON_AXES, None),
        P(None, LAT_AXES, LON_AXES),
        P(),
        P(),
        P(),
        P(),
        P(LAT_AXES, None, None),
        P(None, LAT_AXES, LON_AXES, None),
    )
    return jax.shard_map(
        make(SPLIT),
        mesh=fine,
        in_specs=placed,
        out_specs=(
            P(None, LAT_AXES, LON_AXES, None),
            P(None, LAT_AXES, LON_AXES, None),
            P(),
            P(),
            P(),
            P(LAT_AXES, None, None),
        ),
        check_vma=False,
    )
```

```python
import jax
import jax.numpy as jnp
import numpy as np
from jax import lax
from jax.experimental import pallas as pl
from jax.experimental.pallas import tpu as pltpu
from jax.sharding import PartitionSpec as P

BF = jnp.bfloat16
F32 = jnp.float32

WPL, WLAT, WLON = 2, 6, 12
HALF_LAT, HALF_LON = WLAT // 2, WLON // 2
ROWS, COLS = 6, 24
C = 192
HEADS = 6
HEAD = C // HEADS
WIN = WPL * WLAT * WLON
WINDOWS = COLS // WLON
NPOS = 3312
HI = -(-NPOS // 128)
HIP = 32
EDGE = 8
N_OWN = WPL * ROWS * COLS
N_LAT = WPL * HALF_LAT * COLS
N_EDGE = WPL * HALF_LAT * EDGE
N_ALL = N_OWN + N_LAT + 2 * N_EDGE
MAIN = 128
REST = WIN - MAIN
PAIRS = HEADS * MAIN + 128
EPS = 1e-05
SCALE = HEAD**-0.5
NEG = -1000000000.0
G_ROWS = 1280
CUT = WPL * ROWS * HALF_LON
EDGE_ROWS = 3 * CUT + 8
TAB_ROWS = 160
MSG = EDGE_ROWS + TAB_ROWS
LAT_ROWS = 3 * N_LAT
CORNER_ROWS = 3 * N_EDGE
SIDE_ROWS = 2 * CORNER_ROWS

SPLIT = (4, 8, 4, 2, 2)
AXES = ("x", "zl", "y", "zh", "c")
LAT_AXES = ("x", "zl", "y")
LON_AXES = ("zh", "c")
PLANE = ("x", "y", "c")
LINE = ("zh", "zl")


N_BACK = N_OWN + 2 * N_LAT + CUT


def source_rows():
    at = np.zeros((WINDOWS, WIN), np.int32)
    for level in range(WPL):
        for row in range(ROWS):
            for col in range(COLS):
                from_level = (level + WPL // 2) % WPL
                r, c = row + HALF_LAT, col + HALF_LON
                if r < ROWS and c < COLS:
                    src = from_level * ROWS * COLS + r * COLS + c
                elif c < COLS:
                    src = N_OWN + from_level * HALF_LAT * COLS + (r - ROWS) * COLS + c
                elif r < ROWS:
                    src = N_OWN + N_LAT + from_level * HALF_LAT * EDGE + (r - HALF_LAT) * EDGE + c - COLS
                else:
                    src = N_OWN + N_LAT + N_EDGE + from_level * HALF_LAT * EDGE + (r - ROWS) * EDGE + c - COLS
                at[col // WLON, level * WLAT * WLON + row * WLON + col % WLON] = src
    return at


def constants():
    at = source_rows()
    pick = np.zeros((WINDOWS, WIN, N_ALL), np.float32)
    for w in range(WINDOWS):
        pick[w, np.arange(WIN), at[w]] = 1.0
    back = np.zeros((WINDOWS, N_BACK, WIN), np.float32)
    back[:, : N_OWN + N_LAT] = pick.transpose(0, 2, 1)[:, : N_OWN + N_LAT]
    place = np.zeros((N_OWN + N_LAT, CUT), np.float32)
    for level in range(WPL):
        for row in range(ROWS):
            for col in range(HALF_LON):
                edge = N_OWN + N_LAT + level * HALF_LAT * EDGE + (row % HALF_LAT) * EDGE + col
                edge += 0 if row >= HALF_LAT else N_EDGE
                to = level * ROWS * HALF_LON + row * HALF_LON + col
                back[:, N_OWN + N_LAT + to] = pick[:, :, edge]
                if row >= HALF_LAT:
                    place[level * ROWS * COLS + row * COLS + col, to] = 1.0
                else:
                    at_lat = level * HALF_LAT * COLS + row * COLS + col
                    place[N_OWN + at_lat, to] = 1.0
                    back[:, N_OWN + N_LAT + CUT + at_lat] = pick[:, :, edge]
    return pick.astype(BF), back.astype(BF), place.astype(BF)


def dot(a, b, dims):
    return lax.dot_general(a, b, ((dims[:1], dims[1:]), ((), ())), preferred_element_type=F32)


def nn(a, b):
    return dot(a, b, (1, 0))


def nt(a, b):
    return dot(a, b, (1, 1))


def eye(n):
    return (lax.broadcasted_iota(jnp.int32, (n, n), 0) == lax.broadcasted_iota(jnp.int32, (n, n), 1)).astype(F32).astype(BF)


def spread():
    lane = lax.broadcasted_iota(jnp.int32, (256, WIN), 0)
    query = lax.broadcasted_iota(jnp.int32, (256, WIN), 1)
    held = jnp.where(lane < MAIN, lane, MAIN + lax.bitwise_and(lane, REST - 1))
    return ((held == query) & (lane < MAIN + HEADS * REST)).astype(F32).astype(BF)


def fold(a, b):
    return jnp.concatenate([a[:, :128], b[:, :128], jnp.concatenate([a[:, 128:], b[:, 128:]], axis=1)], axis=0)


def unfold(both, n):
    return [
        jnp.concatenate([both[n * i : n * (i + 1)], both[2 * n : 3 * n, 64 * i : 64 * (i + 1)]], axis=1) for i in range(2)
    ]


def core_is(core, rows):
    return lax.broadcasted_iota(jnp.int32, (rows, 128), 0) * 0 + lax.axis_index("c") == core


def band_is(first, rows):
    at = lax.axis_index("zl") * lax.axis_size("y") + lax.axis_index("y")
    want = 0 if first else lax.axis_size("zl") * lax.axis_size("y") - 1
    return lax.broadcasted_iota(jnp.int32, (rows, 128), 0) * 0 + at == want


def cut_kernel(tokens, d_out, to_core, lat, to_lon, to_diag):
    both = (tokens[...].astype(F32), d_out[...].astype(F32))
    top = fold(*(a[:, :HALF_LAT].reshape(N_LAT, C) for a in both))
    corner = fold(*(a[:, :HALF_LAT, :EDGE].reshape(N_EDGE, C) for a in both))
    lon = fold(*(a[:, HALF_LAT:, :EDGE].reshape(N_EDGE, C) for a in both))
    side = jnp.concatenate([corner, lon], axis=0)
    lat[...] = top.astype(BF)
    to_lon[...] = lon.astype(BF)
    to_diag[...] = corner.astype(BF)
    spare = jnp.zeros((LAT_ROWS - SIDE_ROWS, 128), F32)
    to_core[...] = jnp.where(core_is(1, LAT_ROWS), jnp.concatenate([side, spare], axis=0), top).astype(BF)


def join_kernel(lat, sibling, to_lat):
    to_lat[:LAT_ROWS, :] = lat[...]
    to_lat[LAT_ROWS:, :] = sibling[:CORNER_ROWS, :]


def border_kernel(lon, diag, to_lon, to_diag):
    to_lon[...] = lon[...]
    to_diag[...] = diag[...]


def tables_kernel(pos, table, bias, hi_out, lo_out, scr):
    one = eye(WIN)
    idx = pos[...]
    hi = lax.shift_right_logical(idx, 7)
    lo = lax.bitwise_and(idx, 127)
    sp = spread()
    hi2 = nt(nt(one, hi.astype(F32).astype(BF)).astype(BF), sp)
    lo2 = nt(nt(one, lo.astype(F32).astype(BF)).astype(BF), sp)
    hi2 = hi2.astype(jnp.int32)
    lo2 = lo2.astype(jnp.int32)
    hi_out[...] = hi2
    lo_out[...] = lo2

    steps = []
    for pair in range(HEADS // 2):
        words = []
        for head in (2 * pair, 2 * pair + 1):
            row = table[head]
            unit = jnp.maximum(jnp.max(jnp.abs(row), axis=1, keepdims=True), 1e-20) * (1.0 / 32767.0)
            fixed = row * (1.0 / unit)
            fixed = jnp.floor(jnp.clip(fixed + 0.5, -32767.0, 32767.0)).astype(jnp.int32)
            steps.append(unit)
            words.append(fixed)
        scr[pair : pair + 1, :NPOS] = lax.shift_left(words[0], 16) | lax.bitwise_and(words[1], 65535)
    scr[:, NPOS:] = jnp.zeros((HEADS // 2, HI * 128 - NPOS), jnp.int32)

    def look(h_idx, l_idx):
        acc = [[jnp.zeros((8, 128), jnp.int32) for _ in h_idx] for _ in range(HEADS // 2)]
        for part in range(HI):
            hit = [h == part for h in h_idx]
            for pair in range(HEADS // 2):
                row = jnp.broadcast_to(scr[pair : pair + 1, part * 128 : part * 128 + 128], (8, 128))
                for i, l in enumerate(l_idx):
                    got = jnp.take_along_axis(row, l, axis=1, mode="promise_in_bounds")
                    acc[pair][i] = jnp.where(hit[i], got, acc[pair][i])
        out = []
        for pair in range(HEADS // 2):
            high = [lax.shift_right_arithmetic(v, 16) for v in acc[pair]]
            low = [lax.shift_right_arithmetic(lax.shift_left(v, 16), 16) for v in acc[pair]]
            out.append([v.astype(F32) * steps[2 * pair] for v in high])
            out.append([v.astype(F32) * steps[2 * pair + 1] for v in low])
        return out

    def step(block, carry):
        rows = [pl.ds(pl.multiple_of(block * 24 + 8 * i, 8), 8) for i in range(3)]
        acc = look([hi_out[r, :128] for r in rows], [lo_out[r, :128] for r in rows])
        for head in range(HEADS):
            for i, r in enumerate(rows):
                bias[r, MAIN * head : MAIN * (head + 1)] = acc[head][i]
        return carry

    lax.fori_loop(0, WIN // 24, step, 0)
    pad = jnp.zeros((REST, 256 - WIN), jnp.int32)
    h_rest = jnp.concatenate([hi[MAIN:], pad], axis=1)
    l_rest = jnp.concatenate([lo[MAIN:], pad], axis=1)
    tiles = [(slice(8 * i, 8 * i + 8), slice(128 * j, 128 * j + 128)) for i in range(2) for j in range(2)]
    acc = look([h_rest[t] for t in tiles], [l_rest[t] for t in tiles])
    rest = [jnp.concatenate([jnp.concatenate(a[2 * i : 2 * i + 2], axis=1) for i in range(2)], axis=0) for a in acc]
    rest = jnp.concatenate(rest + [jnp.zeros((128 - HEADS * REST, 256), F32)], axis=0)
    bias[:, HEADS * MAIN :] = rest.T[:WIN]


def by_head(x):
    lane = lax.broadcasted_iota(jnp.int32, (1, C), 1)
    keep = [((lane >= HEAD * h) & (lane < HEAD * (h + 1))).astype(F32).astype(BF) for h in range(HEADS)]
    parts = [x[:MAIN] * keep[h] for h in range(HEADS)]
    parts += [x[MAIN:] * keep[h] for h in range(HEADS)]
    parts.append(jnp.zeros((PAIRS - HEADS * WIN, C), BF))
    return jnp.concatenate(parts, axis=0)


def heads_apart(left, right, scale):
    main = [
        nn(left[HEAD * h : HEAD * (h + 1)], right[:, MAIN * h : MAIN * (h + 1)]) for h in range(HEADS)
    ]
    main = (jnp.concatenate(main, axis=0) * scale).astype(BF)
    rest = nn(left, right[:, HEADS * MAIN :]) * scale
    row = lax.broadcasted_iota(jnp.int32, (C, 128), 0)
    lane = lax.broadcasted_iota(jnp.int32, (C, 128), 1)
    rest = jnp.where(lax.div(row, HEAD) == lax.div(lane, REST), rest, 0.0).astype(BF)
    fold_l = lax.broadcasted_iota(jnp.int32, (128, REST), 0)
    fold_a = lax.broadcasted_iota(jnp.int32, (128, REST), 1)
    fold = (lax.rem(fold_l, REST) == fold_a).astype(F32).astype(BF)
    rest = nn(rest, fold).astype(BF)
    return jnp.concatenate([main, rest], axis=1)


def regions(mask):
    sp = spread()
    out = []
    lab = [mask[row, level : level + 1, :].astype(F32) for level in range(WPL) for row in range(ROWS)]
    lab = jnp.concatenate(lab, axis=0).astype(BF)
    for w in range(WINDOWS):
        lane = lax.broadcasted_iota(jnp.int32, (COLS, WIN), 1)
        col = lax.broadcasted_iota(jnp.int32, (COLS, WIN), 0)
        across = (lax.rem(lane, WLON) + w * WLON == col).astype(F32).astype(BF)
        wide = nn(lab, across)
        r = lax.broadcasted_iota(jnp.int32, (WPL * ROWS, WIN), 0)
        a = lax.broadcasted_iota(jnp.int32, (WPL * ROWS, WIN), 1)
        row = jnp.sum(jnp.where(lax.div(a, WLON) == r, wide, 0.0), axis=0, keepdims=True)
        row = jnp.broadcast_to(row, (WIN, WIN)).astype(BF)
        down = nt(eye(WIN), row)
        over = nt(row, sp)
        out.append(jnp.where(over == jnp.broadcast_to(down[:, :1], (WIN, 256)), 0.0, NEG))
    return out


def block_kernel(
    own_x, own_d, sibling, from_lon, from_lat, from_diag, pick, back, gain, w_qkv, wp, mask, bias,
    base_x, base_d, out_lat, out_corner, out_edge, grads, d_bias,
):
    f32 = lambda ref, start, size: ref[start : start + size, :].astype(F32)
    lat = unfold(f32(from_lat, 0, LAT_ROWS), N_LAT)
    lon = f32(sibling, CORNER_ROWS, CORNER_ROWS), f32(from_lon, 0, CORNER_ROWS)
    lon = unfold(jnp.where(core_is(0, CORNER_ROWS), *lon), N_EDGE)
    diag = f32(from_lat, LAT_ROWS, CORNER_ROWS), f32(from_diag, 0, CORNER_ROWS)
    diag = unfold(jnp.where(core_is(0, CORNER_ROWS), *diag), N_EDGE)
    x_all, d_all = (
        jnp.concatenate([own[...], lat[i].astype(BF), lon[i].astype(BF), diag[i].astype(BF)], axis=0)
        for i, own in enumerate((own_x, own_d))
    )
    eye_c = eye(C)
    eye_w = eye(WIN)
    g = jnp.sum(eye_c.astype(F32) * gain[...], axis=1, keepdims=True)
    w3 = [w_qkv[:, C * i : C * (i + 1)] for i in range(3)]
    w3t = [None] + [nt(eye_c, w).astype(BF) for w in w3[1:]]
    wpt = nt(eye_c, wp[...]).astype(BF)
    blocked = regions(mask)
    sums = [jnp.zeros((C, C), F32) for _ in range(4)]
    d_gain = jnp.zeros((C, 1), F32)
    x_back = jnp.zeros((N_BACK, C), F32)
    d_back = jnp.zeros((N_BACK, C), F32)
    for w in range(WINDOWS):
        x = nn(pick[w], x_all).astype(BF)
        d_proj = nn(pick[w], d_all).astype(BF)
        xt = nt(eye_c, x)
        mean = jnp.sum(xt, axis=0, keepdims=True) * (1.0 / C)
        centered = xt - mean
        var = jnp.sum(centered * centered, axis=0, keepdims=True) * (1.0 / C)
        rstd = lax.rsqrt(var + EPS)
        xhat = centered * rstd
        nt_w = (xhat * g).astype(BF)
        n_w = nt(eye_w, nt_w).astype(BF)
        q = nn(n_w, w3[0]).astype(BF)
        k = nn(n_w, w3[1]).astype(BF)
        v = nn(n_w, w3[2]).astype(BF)
        kt = nn(w3t[1], nt_w).astype(BF)
        vt = nn(w3t[2], nt_w).astype(BF)
        qm = by_head(q)
        dm = by_head(nt(d_proj, wp[...]).astype(BF))
        far = jnp.concatenate([blocked[w][:, :MAIN]] * HEADS + [blocked[w][:, MAIN:]], axis=1)
        s = nt(k, qm) * SCALE + bias[...] + far
        e = jnp.exp(s - jnp.max(s, axis=0, keepdims=True))
        p = e * (1.0 / jnp.sum(e, axis=0, keepdims=True))
        attn = p.astype(BF)
        d_attn = nt(v, dm)
        pd = p * d_attn
        ds = pd - p * jnp.sum(pd, axis=0, keepdims=True)
        dsb = ds.astype(BF)
        if w == 0:
            d_bias[...] = ds
        else:
            d_bias[...] += ds
        mixed_t = heads_apart(vt, attn, 1.0)
        dq_t = heads_apart(kt, dsb, SCALE)
        dk = (nn(dsb, qm) * SCALE).astype(BF)
        dv = nn(attn, dm).astype(BF)
        proj_t = nn(wpt, mixed_t).astype(BF)
        x_back = x_back + nt(back[w], proj_t)
        sums[0] = sums[0] + nt(nt_w, dq_t)
        sums[1] = sums[1] + nn(nt_w, dk)
        sums[2] = sums[2] + nn(nt_w, dv)
        sums[3] = sums[3] + nn(mixed_t, d_proj)
        dn = nn(w3[0], dq_t) + nt(w3[1], dk) + nt(w3[2], dv)
        dn = dn.astype(BF).astype(F32)
        d_gain = d_gain + jnp.sum(dn * xhat, axis=1, keepdims=True)
        dy = dn * g
        m1 = jnp.sum(dy, axis=0, keepdims=True) * (1.0 / C)
        m2 = jnp.sum(dy * xhat, axis=0, keepdims=True) * (1.0 / C)
        dx = (rstd * (dy - m1 - xhat * m2)).astype(BF)
        d_back = d_back + nt(back[w], dx)
    for i in range(4):
        grads[C * i : C * (i + 1), :] = sums[i][:, :128].astype(BF)
    for i in range(2):
        pair = jnp.concatenate([sums[2 * i][:, 128:], sums[2 * i + 1][:, 128:]], axis=1)
        grads[C * (4 + i) : C * (5 + i), :] = pair.astype(BF)
    row = jnp.sum(eye_c.astype(F32) * d_gain, axis=0, keepdims=True)
    tail = jnp.concatenate([row[:, 128:], jnp.zeros((1, 256 - C), F32)], axis=1)
    grads[6 * C :, :] = jnp.concatenate([row[:, :128], tail, jnp.zeros((126, 128), F32)], axis=0).astype(BF)
    for i, (total, own, base) in enumerate(((x_back, own_x, base_x), (d_back, own_d, base_d))):
        base[...] = (own[...].astype(F32) + total[:N_OWN]).astype(BF)
    parts = ((out_lat, N_OWN, N_LAT), (out_edge, N_OWN + N_LAT, CUT), (out_corner, N_OWN + N_LAT + CUT, N_LAT))
    for out, start, size in parts:
        both = fold(x_back[start : start + size], d_back[start : start + size])
        spare = out.shape[0] - both.shape[0]
        if spare:
            both = jnp.concatenate([both, jnp.zeros((spare, 128), F32)], axis=0)
        out[...] = both.astype(BF)


def scatter_kernel(d_bias, hi, lo, edge, lat, out, acc):
    acc[...] = jnp.zeros_like(acc)

    def step(block, carry):
        rows = pl.ds(pl.multiple_of(block * 8, 8), 8)
        h_all = hi[rows, :]
        l_all = lo[rows, :]
        d_all = d_bias[rows, :]
        part = lax.broadcasted_iota(jnp.int32, (HIP, 256), 0)
        group = lax.shift_right_logical(lax.broadcasted_iota(jnp.int32, (HIP, 128), 1), 4)
        place = lax.broadcasted_iota(jnp.int32, (128, 256), 0)
        total = acc[...]
        for i in range(8):
            hit = jnp.broadcast_to(h_all[i : i + 1], (HIP, 256)) == part
            rest = jnp.broadcast_to(d_all[i : i + 1, HEADS * MAIN :], (HIP, 128))
            rest = jnp.where(hit[:, 128:], rest, 0.0)
            many = []
            for head in range(HEADS):
                main = jnp.broadcast_to(d_all[i : i + 1, MAIN * head : MAIN * (head + 1)], (HIP, 128))
                main = jnp.where(hit[:, :128], main, 0.0)
                many.append(jnp.concatenate([main, jnp.where(group == head, rest, 0.0)], axis=1))
            many = jnp.concatenate(many, axis=0).astype(BF)
            spot = (jnp.broadcast_to(l_all[i : i + 1], (128, 256)) == place).astype(F32).astype(BF)
            total = total + nt(many, spot)
        acc[...] = total
        return carry

    lax.fori_loop(0, WIN // 8, step, 0)
    out[:EDGE_ROWS, :] = edge[...]
    rows = [acc[HIP * h : HIP * h + HI] for h in range(HEADS)] + [jnp.zeros((TAB_ROWS - HEADS * HI, 128), F32)]
    out[EDGE_ROWS:MSG, :] = jnp.concatenate(rows, axis=0).astype(BF)
    out[MSG:, :] = lat[...]


def pair_kernel(own, near, out):
    out[:EDGE_ROWS, :] = own[:EDGE_ROWS, :]
    out[EDGE_ROWS:, :] = (own[EDGE_ROWS:MSG, :].astype(F32) + near[EDGE_ROWS:MSG, :].astype(F32)).astype(BF)


def line_kernel(near, lat, corner, across):
    across[:LAT_ROWS, :] = lat[...]
    across[LAT_ROWS:, :] = (near[MSG:, :].astype(F32) + corner[...].astype(F32)).astype(BF)


def beside_kernel(across, out):
    out[...] = across[LAT_ROWS:, :]


def total_kernel(parts, out):
    total = parts[0].astype(F32)
    for i in range(1, parts.shape[0]):
        total = total + parts[i].astype(F32)
    total = total.astype(BF)
    for i in range(out.shape[0]):
        out[i] = total


def middle_kernel(pair, near, far, base_x, base_d, lat, corner, place, out_x, out_d, out_lat, out_near):
    edge = jnp.where(core_is(1, 3 * CUT), near[: 3 * CUT, :].astype(F32), far[: 3 * CUT, :].astype(F32))
    adds = [nn(place[...], e.astype(BF)) for e in unfold(edge, CUT)]
    for add, base, out in ((adds[0], base_x, out_x), (adds[1], base_d, out_d)):
        out[...] = (base[...].astype(F32) + add[:N_OWN]).astype(BF)
    whole = lat[...].astype(F32) + fold(adds[0][N_OWN:], adds[1][N_OWN:])
    out_lat[LAT_ROWS:, :] = jnp.zeros((16, 128), BF)
    out_lat[:LAT_ROWS, :] = jnp.where(band_is(False, LAT_ROWS), corner[...].astype(F32), whole).astype(BF)
    out_near[...] = (pair[EDGE_ROWS:, :].astype(F32) + far[EDGE_ROWS:, :].astype(F32)).astype(BF)


def finish_kernel(base_x, base_d, lat, across, beside, near, own, out_x, out_d, out_t):
    got = lat[:LAT_ROWS, :].astype(F32) + across[:LAT_ROWS, :].astype(F32) + beside[...].astype(F32)
    for add, base, out in zip(unfold(got, N_LAT), (base_x, base_d), (out_x, out_d)):
        out[:, HALF_LAT:] = base[:, HALF_LAT:]
        add = add.reshape(WPL, HALF_LAT, COLS, C)
        out[:, :HALF_LAT] = (base[:, :HALF_LAT].astype(F32) + add).astype(BF)
    t = jnp.where(core_is(1, TAB_ROWS), near[...].astype(F32), own[...].astype(F32))
    for part in range(HI):
        width = min(128, NPOS - part * 128)
        for head in range(HEADS):
            row = head * HI + part
            out_t[head, :, part * 128 : part * 128 + width] = t[row : row + 1, :width]


def unpack_kernel(g, scale, qkv, proj, gain):
    k = scale
    full = [g[C * i : C * (i + 1), :].astype(F32) * k for i in range(6)]
    qkv[:, 0:128] = full[0]
    qkv[:, 128:256] = jnp.concatenate([full[4][:, :64], full[1][:, :64]], axis=1)
    qkv[:, 256:384] = jnp.concatenate([full[1][:, 64:], full[4][:, 64:]], axis=1)
    qkv[:, 384:512] = full[2]
    qkv[:, 512:576] = full[5][:, :64]
    proj[:, 0:128] = full[3]
    proj[:, 128:192] = full[5][:, 64:]
    tail = g[6 * C : 6 * C + 16, :].astype(F32) * k
    gain[:, :128] = tail[0:1]
    gain[:, 128:] = tail[1:2, : C - 128]


def call(kernel, out_shape, *args, scratch=(), cost=(0, 0), vmem=8):
    return pl.pallas_call(
        kernel,
        out_shape=out_shape,
        scratch_shapes=list(scratch),
        compiler_params=pltpu.CompilerParams(vmem_limit_bytes=vmem * 2**20),
        cost_estimate=pl.CostEstimate(flops=cost[0], bytes_accessed=cost[1], transcendentals=0),
    )(*args)


def sds(shape, dtype):
    return jax.ShapeDtypeStruct(shape, dtype)


def make(sizes):
    n_lat = sizes[0] * sizes[1] * sizes[2]
    n_lon = sizes[3] * sizes[4]
    n_plane = sizes[0] * sizes[2] * sizes[4]
    n_line = sizes[1] * sizes[3]
    piece = G_ROWS // n_plane
    band = sizes[1] * sizes[2]

    def route(d_lat, d_lon):
        return [
            (a * n_lon + b, (a + d_lat) % n_lat * n_lon + (b + d_lon) % n_lon)
            for a in range(n_lat)
            for b in range(n_lon)
        ]

    def first(pair):
        return pair[0] // n_lon % band == 0

    def last(pair):
        return pair[0] // n_lon % band == band - 1

    def hop(to, cores):
        return [
            (a * n_lon + zh * sizes[4] + c, a * n_lon + to(zh, c)[0] * sizes[4] + to(zh, c)[1])
            for a in range(n_lat)
            for zh in range(sizes[3])
            for c in cores
        ]

    def per_device(tokens, mask_ids, pos_index, norm_gain, w_qkv, w_proj, earth_bias, d_out):
        pick, back, place = (jnp.asarray(c) for c in constants())
        to_core, lat, to_lon, to_diag = call(
            cut_kernel,
            (
                sds((LAT_ROWS, 128), BF),
                sds((LAT_ROWS, 128), BF),
                sds((CORNER_ROWS, 128), BF),
                sds((CORNER_ROWS, 128), BF),
            ),
            tokens,
            d_out,
        )
        sibling = lax.ppermute(to_core, AXES, hop(lambda zh, c: (zh, 1 - c), (0, 1)))
        to_lat = call(join_kernel, sds((LAT_ROWS + CORNER_ROWS, 128), BF), lat, sibling)
        from_lat = lax.ppermute(to_lat, AXES, route(-1, 0))
        to_lat, to_lon, to_diag = lax.optimization_barrier((to_lat, to_lon, to_diag))
        to_lon, to_diag = call(border_kernel, (sds((CORNER_ROWS, 128), BF), sds((CORNER_ROWS, 128), BF)), to_lon, to_diag, cost=(10**10, 10**6))
        from_lon = lax.ppermute(to_lon, AXES, hop(lambda zh, c: (1 - zh, 1), (0,)))
        from_diag = lax.ppermute(to_diag, AXES, [r for r in route(-1, -1) if r[0] % sizes[4] == 0])
        bias, hi, lo = call(
            tables_kernel,
            (sds((WIN, PAIRS), F32), sds((WIN, 256), jnp.int32), sds((WIN, 256), jnp.int32)),
            pos_index,
            earth_bias.transpose(1, 0, 2),
            scratch=[pltpu.VMEM((HEADS // 2, HI * 128), jnp.int32)],
            cost=(6 * 10**9, 10**6),
        )
        from_lat, bias = lax.optimization_barrier((from_lat, bias))
        from_lon, from_diag, bias = lax.optimization_barrier((from_lon, from_diag, bias))
        base_x, base_d, out_lat, out_corner, out_edge, grads, d_bias = call(
            block_kernel,
            (
                sds((N_OWN, C), BF),
                sds((N_OWN, C), BF),
                sds((LAT_ROWS, 128), BF),
                sds((LAT_ROWS, 128), BF),
                sds((EDGE_ROWS, 128), BF),
                sds((G_ROWS, 128), BF),
                sds((WIN, PAIRS), F32),
            ),
            tokens.reshape(N_OWN, C),
            d_out.reshape(N_OWN, C),
            sibling,
            from_lon,
            from_lat,
            from_diag,
            pick,
            back,
            norm_gain.reshape(1, C),
            w_qkv,
            w_proj,
            mask_ids.transpose(1, 0, 2),
            bias,
            vmem=20,
            cost=(6 * 10**9, 10**6),
        )
        parts = lax.all_to_all(grads.reshape(n_plane, piece, 128), PLANE, 0, 0)
        own = call(
            scatter_kernel,
            sds((MSG + LAT_ROWS, 128), BF),
            d_bias,
            hi,
            lo,
            out_edge,
            out_lat,
            scratch=[pltpu.VMEM((HEADS * HIP, 128), F32)],
            cost=(8 * 10**9, 10**6),
        )
        parts, own = lax.optimization_barrier((parts, own))
        near = lax.ppermute(own, AXES, hop(lambda zh, c: (zh, 1 - c), (0, 1)))
        part = call(total_kernel, sds((n_line, piece, 128), BF), parts, cost=(10**9, 10**6))
        line = lax.all_to_all(part, LINE, 0, 0)
        pair = call(pair_kernel, sds((MSG, 128), BF), own, near, cost=(10**9, 10**6))
        far = lax.ppermute(pair, AXES, hop(lambda zh, c: (1 - zh, 0), (1,)))
        across = call(line_kernel, sds((2 * LAT_ROWS, 128), BF), near, out_lat, out_corner, cost=(10**9, 10**6))
        across = lax.ppermute(across, AXES, [r for r in route(1, 0) if last(r) and r[0] % sizes[4] == 0])
        line, pair = lax.optimization_barrier((line, pair))
        total = call(total_kernel, sds((n_plane, piece, 128), BF), line, cost=(10**9, 10**6))
        whole = lax.all_to_all(total, PLANE, 0, 0)
        base_x, base_d, to_lat, to_near = call(
            middle_kernel,
            (
                sds((N_OWN, C), BF),
                sds((N_OWN, C), BF),
                sds((LAT_ROWS + 16, 128), BF),
                sds((TAB_ROWS, 128), BF),
            ),
            pair,
            near,
            far,
            base_x,
            base_d,
            out_lat,
            out_corner,
            place,
            cost=(20 * 10**9, 10**6),
        )
        corners = [r for r in route(1, 1) if last(r) and r[0] % sizes[4] == 1]
        from_lat = lax.ppermute(to_lat, AXES, [r for r in route(1, 0) if not last(r)] + corners)
        from_near = lax.ppermute(to_near, AXES, hop(lambda zh, c: (zh, 1), (0,)))
        across, from_near = lax.optimization_barrier((across, from_near))
        beside = call(beside_kernel, sds((LAT_ROWS, 128), BF), across, cost=(10**9, 10**6))
        beside = lax.ppermute(beside, AXES, [r for r in hop(lambda zh, c: (zh, 1), (0,)) if first(r)])
        scale = float(n_lat * n_lon * N_OWN) ** -0.5
        qkv, proj, gain = call(
            lambda g, a, b, c: unpack_kernel(g, scale, a, b, c),
            (sds((C, 3 * C), F32), sds((C, C), F32), sds((1, C), F32)),
            whole.reshape(G_ROWS, 128),
        )
        base_x, qkv = lax.optimization_barrier((base_x, qkv))
        updated, d_tokens, d_table = call(
            finish_kernel,
            (
                sds((WPL, ROWS, COLS, C), BF),
                sds((WPL, ROWS, COLS, C), BF),
                sds((HEADS, 1, NPOS), F32),
            ),
            base_x.reshape(WPL, ROWS, COLS, C),
            base_d.reshape(WPL, ROWS, COLS, C),
            from_lat,
            across,
            beside,
            from_near,
            to_near,
            cost=(20 * 10**9, 10**6),
        )
        return updated, d_tokens, qkv, proj, gain.reshape(C), d_table.transpose(1, 0, 2)

    return per_device


def solution(mesh):
    fine = jax.sharding.Mesh(mesh.devices.reshape(SPLIT), AXES)
    placed = (
        P(None, LAT_AXES, LON_AXES, None),
        P(None, LAT_AXES, LON_AXES),
        P(),
        P(),
        P(),
        P(),
        P(LAT_AXES, None, None),
        P(None, LAT_AXES, LON_AXES, None),
    )
    return jax.shard_map(
        make(SPLIT),
        mesh=fine,
        in_specs=placed,
        out_specs=(
            P(None, LAT_AXES, LON_AXES, None),
            P(None, LAT_AXES, LON_AXES, None),
            P(),
            P(),
            P(),
            P(LAT_AXES, None, None),
        ),
        check_vma=False,
    )
```

```python
import jax
import jax.numpy as jnp
import numpy as np
from jax import lax
from jax.experimental import pallas as pl
from jax.experimental.pallas import tpu as pltpu
from jax.sharding import PartitionSpec as P

BF = jnp.bfloat16
F32 = jnp.float32

WPL, WLAT, WLON = 2, 6, 12
HALF_LAT, HALF_LON = WLAT // 2, WLON // 2
ROWS, COLS = 6, 24
C = 192
HEADS = 6
HEAD = C // HEADS
WIN = WPL * WLAT * WLON
WINDOWS = COLS // WLON
NPOS = 3312
HI = -(-NPOS // 128)
HIP = 32
EDGE = 8
N_OWN = WPL * ROWS * COLS
N_LAT = WPL * HALF_LAT * COLS
N_EDGE = WPL * HALF_LAT * EDGE
N_ALL = N_OWN + N_LAT + 2 * N_EDGE
MAIN = 128
REST = WIN - MAIN
PAIRS = HEADS * MAIN + 128
EPS = 1e-05
SCALE = HEAD**-0.5
NEG = -1000000000.0
G_ROWS = 1280
CUT = WPL * ROWS * HALF_LON
EDGE_ROWS = 3 * CUT + 8
TAB_ROWS = 160
MSG = EDGE_ROWS + TAB_ROWS
LAT_ROWS = 3 * N_LAT
CORNER_ROWS = 3 * N_EDGE
SIDE_ROWS = 2 * CORNER_ROWS

SPLIT = (4, 8, 4, 2, 2)
AXES = ("x", "zl", "y", "zh", "c")
LAT_AXES = ("x", "zl", "y")
LON_AXES = ("zh", "c")
PLANE = ("x", "y", "c")
LINE = ("zh", "zl")


N_BACK = N_OWN + 2 * N_LAT + CUT


def source_rows():
    at = np.zeros((WINDOWS, WIN), np.int32)
    for level in range(WPL):
        for row in range(ROWS):
            for col in range(COLS):
                from_level = (level + WPL // 2) % WPL
                r, c = row + HALF_LAT, col + HALF_LON
                if r < ROWS and c < COLS:
                    src = from_level * ROWS * COLS + r * COLS + c
                elif c < COLS:
                    src = N_OWN + from_level * HALF_LAT * COLS + (r - ROWS) * COLS + c
                elif r < ROWS:
                    src = N_OWN + N_LAT + from_level * HALF_LAT * EDGE + (r - HALF_LAT) * EDGE + c - COLS
                else:
                    src = N_OWN + N_LAT + N_EDGE + from_level * HALF_LAT * EDGE + (r - ROWS) * EDGE + c - COLS
                at[col // WLON, level * WLAT * WLON + row * WLON + col % WLON] = src
    return at


def constants():
    at = source_rows()
    pick = np.zeros((WINDOWS, WIN, N_ALL), np.float32)
    for w in range(WINDOWS):
        pick[w, np.arange(WIN), at[w]] = 1.0
    back = np.zeros((WINDOWS, N_BACK, WIN), np.float32)
    back[:, : N_OWN + N_LAT] = pick.transpose(0, 2, 1)[:, : N_OWN + N_LAT]
    place = np.zeros((N_OWN + N_LAT, CUT), np.float32)
    for level in range(WPL):
        for row in range(ROWS):
            for col in range(HALF_LON):
                edge = N_OWN + N_LAT + level * HALF_LAT * EDGE + (row % HALF_LAT) * EDGE + col
                edge += 0 if row >= HALF_LAT else N_EDGE
                to = level * ROWS * HALF_LON + row * HALF_LON + col
                back[:, N_OWN + N_LAT + to] = pick[:, :, edge]
                if row >= HALF_LAT:
                    place[level * ROWS * COLS + row * COLS + col, to] = 1.0
                else:
                    at_lat = level * HALF_LAT * COLS + row * COLS + col
                    place[N_OWN + at_lat, to] = 1.0
                    back[:, N_OWN + N_LAT + CUT + at_lat] = pick[:, :, edge]
    return pick.astype(BF), back.astype(BF), place.astype(BF)


def dot(a, b, dims):
    return lax.dot_general(a, b, ((dims[:1], dims[1:]), ((), ())), preferred_element_type=F32)


def nn(a, b):
    return dot(a, b, (1, 0))


def nt(a, b):
    return dot(a, b, (1, 1))


def eye(n):
    return (lax.broadcasted_iota(jnp.int32, (n, n), 0) == lax.broadcasted_iota(jnp.int32, (n, n), 1)).astype(F32).astype(BF)


def spread():
    lane = lax.broadcasted_iota(jnp.int32, (256, WIN), 0)
    query = lax.broadcasted_iota(jnp.int32, (256, WIN), 1)
    held = jnp.where(lane < MAIN, lane, MAIN + lax.bitwise_and(lane, REST - 1))
    return ((held == query) & (lane < MAIN + HEADS * REST)).astype(F32).astype(BF)


def fold(a, b):
    return jnp.concatenate([a[:, :128], b[:, :128], jnp.concatenate([a[:, 128:], b[:, 128:]], axis=1)], axis=0)


def unfold(both, n):
    return [
        jnp.concatenate([both[n * i : n * (i + 1)], both[2 * n : 3 * n, 64 * i : 64 * (i + 1)]], axis=1) for i in range(2)
    ]


def core_is(core, rows):
    return lax.broadcasted_iota(jnp.int32, (rows, 128), 0) * 0 + lax.axis_index("c") == core


def band_is(first, rows):
    at = lax.axis_index("zl") * lax.axis_size("y") + lax.axis_index("y")
    want = 0 if first else lax.axis_size("zl") * lax.axis_size("y") - 1
    return lax.broadcasted_iota(jnp.int32, (rows, 128), 0) * 0 + at == want


def cut_kernel(tokens, d_out, to_core, lat, to_lon, to_diag):
    both = (tokens[...].astype(F32), d_out[...].astype(F32))
    top = fold(*(a[:, :HALF_LAT].reshape(N_LAT, C) for a in both))
    corner = fold(*(a[:, :HALF_LAT, :EDGE].reshape(N_EDGE, C) for a in both))
    lon = fold(*(a[:, HALF_LAT:, :EDGE].reshape(N_EDGE, C) for a in both))
    side = jnp.concatenate([corner, lon], axis=0)
    lat[...] = top.astype(BF)
    to_lon[...] = lon.astype(BF)
    to_diag[...] = corner.astype(BF)
    spare = jnp.zeros((LAT_ROWS - SIDE_ROWS, 128), F32)
    to_core[...] = jnp.where(core_is(1, LAT_ROWS), jnp.concatenate([side, spare], axis=0), top).astype(BF)


def join_kernel(lat, sibling, to_lat):
    to_lat[:LAT_ROWS, :] = lat[...]
    to_lat[LAT_ROWS:, :] = sibling[:CORNER_ROWS, :]


def border_kernel(lon, diag, to_lon, to_diag):
    to_lon[...] = lon[...]
    to_diag[...] = diag[...]


def tables_kernel(pos, table, bias, hi_out, lo_out, scr):
    one = eye(WIN)
    idx = pos[...]
    hi = lax.shift_right_logical(idx, 7)
    lo = lax.bitwise_and(idx, 127)
    sp = spread()
    hi2 = nt(nt(one, hi.astype(F32).astype(BF)).astype(BF), sp)
    lo2 = nt(nt(one, lo.astype(F32).astype(BF)).astype(BF), sp)
    hi2 = hi2.astype(jnp.int32)
    lo2 = lo2.astype(jnp.int32)
    hi_out[...] = hi2
    lo_out[...] = lo2

    steps = []
    for pair in range(HEADS // 2):
        words = []
        for head in (2 * pair, 2 * pair + 1):
            row = table[head]
            unit = jnp.maximum(jnp.max(jnp.abs(row), axis=1, keepdims=True), 1e-20) * (1.0 / 32767.0)
            fixed = row * (1.0 / unit)
            fixed = jnp.floor(jnp.clip(fixed + 0.5, -32767.0, 32767.0)).astype(jnp.int32)
            steps.append(unit)
            words.append(fixed)
        scr[pair : pair + 1, :NPOS] = lax.shift_left(words[0], 16) | lax.bitwise_and(words[1], 65535)
    scr[:, NPOS:] = jnp.zeros((HEADS // 2, HI * 128 - NPOS), jnp.int32)

    def look(h_idx, l_idx):
        acc = [[jnp.zeros((8, 128), jnp.int32) for _ in h_idx] for _ in range(HEADS // 2)]
        for part in range(HI):
            hit = [h == part for h in h_idx]
            for pair in range(HEADS // 2):
                row = jnp.broadcast_to(scr[pair : pair + 1, part * 128 : part * 128 + 128], (8, 128))
                for i, l in enumerate(l_idx):
                    got = jnp.take_along_axis(row, l, axis=1, mode="promise_in_bounds")
                    acc[pair][i] = jnp.where(hit[i], got, acc[pair][i])
        out = []
        for pair in range(HEADS // 2):
            high = [lax.shift_right_arithmetic(v, 16) for v in acc[pair]]
            low = [lax.shift_right_arithmetic(lax.shift_left(v, 16), 16) for v in acc[pair]]
            out.append([v.astype(F32) * steps[2 * pair] for v in high])
            out.append([v.astype(F32) * steps[2 * pair + 1] for v in low])
        return out

    def step(block, carry):
        rows = [pl.ds(pl.multiple_of(block * 24 + 8 * i, 8), 8) for i in range(3)]
        acc = look([hi_out[r, :128] for r in rows], [lo_out[r, :128] for r in rows])
        for head in range(HEADS):
            for i, r in enumerate(rows):
                bias[r, MAIN * head : MAIN * (head + 1)] = acc[head][i]
        return carry

    lax.fori_loop(0, WIN // 24, step, 0)
    pad = jnp.zeros((REST, 256 - WIN), jnp.int32)
    h_rest = jnp.concatenate([hi[MAIN:], pad], axis=1)
    l_rest = jnp.concatenate([lo[MAIN:], pad], axis=1)
    tiles = [(slice(8 * i, 8 * i + 8), slice(128 * j, 128 * j + 128)) for i in range(2) for j in range(2)]
    acc = look([h_rest[t] for t in tiles], [l_rest[t] for t in tiles])
    rest = [jnp.concatenate([jnp.concatenate(a[2 * i : 2 * i + 2], axis=1) for i in range(2)], axis=0) for a in acc]
    rest = jnp.concatenate(rest + [jnp.zeros((128 - HEADS * REST, 256), F32)], axis=0)
    bias[:, HEADS * MAIN :] = rest.T[:WIN]


def by_head(x):
    lane = lax.broadcasted_iota(jnp.int32, (1, C), 1)
    keep = [((lane >= HEAD * h) & (lane < HEAD * (h + 1))).astype(F32).astype(BF) for h in range(HEADS)]
    parts = [x[:MAIN] * keep[h] for h in range(HEADS)]
    parts += [x[MAIN:] * keep[h] for h in range(HEADS)]
    parts.append(jnp.zeros((PAIRS - HEADS * WIN, C), BF))
    return jnp.concatenate(parts, axis=0)


def heads_apart(left, right, scale):
    main = [
        nn(left[HEAD * h : HEAD * (h + 1)], right[:, MAIN * h : MAIN * (h + 1)]) for h in range(HEADS)
    ]
    main = (jnp.concatenate(main, axis=0) * scale).astype(BF)
    rest = nn(left, right[:, HEADS * MAIN :]) * scale
    row = lax.broadcasted_iota(jnp.int32, (C, 128), 0)
    lane = lax.broadcasted_iota(jnp.int32, (C, 128), 1)
    rest = jnp.where(lax.div(row, HEAD) == lax.div(lane, REST), rest, 0.0).astype(BF)
    fold_l = lax.broadcasted_iota(jnp.int32, (128, REST), 0)
    fold_a = lax.broadcasted_iota(jnp.int32, (128, REST), 1)
    fold = (lax.rem(fold_l, REST) == fold_a).astype(F32).astype(BF)
    rest = nn(rest, fold).astype(BF)
    return jnp.concatenate([main, rest], axis=1)


def regions(mask):
    sp = spread()
    out = []
    lab = [mask[row, level : level + 1, :].astype(F32) for level in range(WPL) for row in range(ROWS)]
    lab = jnp.concatenate(lab, axis=0).astype(BF)
    for w in range(WINDOWS):
        lane = lax.broadcasted_iota(jnp.int32, (COLS, WIN), 1)
        col = lax.broadcasted_iota(jnp.int32, (COLS, WIN), 0)
        across = (lax.rem(lane, WLON) + w * WLON == col).astype(F32).astype(BF)
        wide = nn(lab, across)
        r = lax.broadcasted_iota(jnp.int32, (WPL * ROWS, WIN), 0)
        a = lax.broadcasted_iota(jnp.int32, (WPL * ROWS, WIN), 1)
        row = jnp.sum(jnp.where(lax.div(a, WLON) == r, wide, 0.0), axis=0, keepdims=True)
        row = jnp.broadcast_to(row, (WIN, WIN)).astype(BF)
        down = nt(eye(WIN), row)
        over = nt(row, sp)
        out.append(jnp.where(over == jnp.broadcast_to(down[:, :1], (WIN, 256)), 0.0, NEG))
    return out


def block_kernel(
    own_x, own_d, sibling, from_lon, from_lat, from_diag, pick, back, gain, w_qkv, wp, mask, bias,
    base_x, base_d, out_lat, out_corner, out_edge, grads, d_bias,
):
    f32 = lambda ref, start, size: ref[start : start + size, :].astype(F32)
    lat = unfold(f32(from_lat, 0, LAT_ROWS), N_LAT)
    lon = f32(sibling, CORNER_ROWS, CORNER_ROWS), f32(from_lon, 0, CORNER_ROWS)
    lon = unfold(jnp.where(core_is(0, CORNER_ROWS), *lon), N_EDGE)
    diag = f32(from_lat, LAT_ROWS, CORNER_ROWS), f32(from_diag, 0, CORNER_ROWS)
    diag = unfold(jnp.where(core_is(0, CORNER_ROWS), *diag), N_EDGE)
    x_all, d_all = (
        jnp.concatenate([own[...], lat[i].astype(BF), lon[i].astype(BF), diag[i].astype(BF)], axis=0)
        for i, own in enumerate((own_x, own_d))
    )
    eye_c = eye(C)
    eye_w = eye(WIN)
    g = jnp.sum(eye_c.astype(F32) * gain[...], axis=1, keepdims=True)
    w3 = [w_qkv[:, C * i : C * (i + 1)] for i in range(3)]
    w3t = [None] + [nt(eye_c, w).astype(BF) for w in w3[1:]]
    wpt = nt(eye_c, wp[...]).astype(BF)
    blocked = regions(mask)
    sums = [jnp.zeros((C, C), F32) for _ in range(4)]
    d_gain = jnp.zeros((C, 1), F32)
    x_back = jnp.zeros((N_BACK, C), F32)
    d_back = jnp.zeros((N_BACK, C), F32)
    for w in range(WINDOWS):
        x = nn(pick[w], x_all).astype(BF)
        d_proj = nn(pick[w], d_all).astype(BF)
        xt = nt(eye_c, x)
        mean = jnp.sum(xt, axis=0, keepdims=True) * (1.0 / C)
        centered = xt - mean
        var = jnp.sum(centered * centered, axis=0, keepdims=True) * (1.0 / C)
        rstd = lax.rsqrt(var + EPS)
        xhat = centered * rstd
        nt_w = (xhat * g).astype(BF)
        n_w = nt(eye_w, nt_w).astype(BF)
        q = nn(n_w, w3[0]).astype(BF)
        k = nn(n_w, w3[1]).astype(BF)
        v = nn(n_w, w3[2]).astype(BF)
        kt = nn(w3t[1], nt_w).astype(BF)
        vt = nn(w3t[2], nt_w).astype(BF)
        qm = by_head(q)
        dm = by_head(nt(d_proj, wp[...]).astype(BF))
        far = jnp.concatenate([blocked[w][:, :MAIN]] * HEADS + [blocked[w][:, MAIN:]], axis=1)
        s = nt(k, qm) * SCALE + bias[...] + far
        e = jnp.exp(s - jnp.max(s, axis=0, keepdims=True))
        p = e * (1.0 / jnp.sum(e, axis=0, keepdims=True))
        attn = p.astype(BF)
        d_attn = nt(v, dm)
        pd = p * d_attn
        ds = pd - p * jnp.sum(pd, axis=0, keepdims=True)
        dsb = ds.astype(BF)
        if w == 0:
            d_bias[...] = ds
        else:
            d_bias[...] += ds
        mixed_t = heads_apart(vt, attn, 1.0)
        dq_t = heads_apart(kt, dsb, SCALE)
        dk = (nn(dsb, qm) * SCALE).astype(BF)
        dv = nn(attn, dm).astype(BF)
        proj_t = nn(wpt, mixed_t).astype(BF)
        x_back = x_back + nt(back[w], proj_t)
        sums[0] = sums[0] + nt(nt_w, dq_t)
        sums[1] = sums[1] + nn(nt_w, dk)
        sums[2] = sums[2] + nn(nt_w, dv)
        sums[3] = sums[3] + nn(mixed_t, d_proj)
        dn = nn(w3[0], dq_t) + nt(w3[1], dk) + nt(w3[2], dv)
        dn = dn.astype(BF).astype(F32)
        d_gain = d_gain + jnp.sum(dn * xhat, axis=1, keepdims=True)
        dy = dn * g
        m1 = jnp.sum(dy, axis=0, keepdims=True) * (1.0 / C)
        m2 = jnp.sum(dy * xhat, axis=0, keepdims=True) * (1.0 / C)
        dx = (rstd * (dy - m1 - xhat * m2)).astype(BF)
        d_back = d_back + nt(back[w], dx)
    for i in range(4):
        grads[C * i : C * (i + 1), :] = sums[i][:, :128].astype(BF)
    for i in range(2):
        pair = jnp.concatenate([sums[2 * i][:, 128:], sums[2 * i + 1][:, 128:]], axis=1)
        grads[C * (4 + i) : C * (5 + i), :] = pair.astype(BF)
    row = jnp.sum(eye_c.astype(F32) * d_gain, axis=0, keepdims=True)
    tail = jnp.concatenate([row[:, 128:], jnp.zeros((1, 256 - C), F32)], axis=1)
    grads[6 * C :, :] = jnp.concatenate([row[:, :128], tail, jnp.zeros((126, 128), F32)], axis=0).astype(BF)
    for i, (total, own, base) in enumerate(((x_back, own_x, base_x), (d_back, own_d, base_d))):
        base[...] = (own[...].astype(F32) + total[:N_OWN]).astype(BF)
    parts = ((out_lat, N_OWN, N_LAT), (out_edge, N_OWN + N_LAT, CUT), (out_corner, N_OWN + N_LAT + CUT, N_LAT))
    for out, start, size in parts:
        both = fold(x_back[start : start + size], d_back[start : start + size])
        spare = out.shape[0] - both.shape[0]
        if spare:
            both = jnp.concatenate([both, jnp.zeros((spare, 128), F32)], axis=0)
        out[...] = both.astype(BF)


def scatter_kernel(d_bias, hi, lo, edge, lat, out, acc):
    acc[...] = jnp.zeros_like(acc)

    def step(block, carry):
        rows = pl.ds(pl.multiple_of(block * 8, 8), 8)
        h_all = hi[rows, :]
        l_all = lo[rows, :]
        d_all = d_bias[rows, :]
        part = lax.broadcasted_iota(jnp.int32, (HIP, 256), 0)
        group = lax.shift_right_logical(lax.broadcasted_iota(jnp.int32, (HIP, 128), 1), 4)
        place = lax.broadcasted_iota(jnp.int32, (128, 256), 0)
        total = acc[...]
        for i in range(8):
            hit = jnp.broadcast_to(h_all[i : i + 1], (HIP, 256)) == part
            rest = jnp.broadcast_to(d_all[i : i + 1, HEADS * MAIN :], (HIP, 128))
            rest = jnp.where(hit[:, 128:], rest, 0.0)
            many = []
            for head in range(HEADS):
                main = jnp.broadcast_to(d_all[i : i + 1, MAIN * head : MAIN * (head + 1)], (HIP, 128))
                main = jnp.where(hit[:, :128], main, 0.0)
                many.append(jnp.concatenate([main, jnp.where(group == head, rest, 0.0)], axis=1))
            many = jnp.concatenate(many, axis=0).astype(BF)
            spot = (jnp.broadcast_to(l_all[i : i + 1], (128, 256)) == place).astype(F32).astype(BF)
            total = total + nt(many, spot)
        acc[...] = total
        return carry

    lax.fori_loop(0, WIN // 8, step, 0)
    out[:EDGE_ROWS, :] = edge[...]
    rows = [acc[HIP * h : HIP * h + HI] for h in range(HEADS)] + [jnp.zeros((TAB_ROWS - HEADS * HI, 128), F32)]
    out[EDGE_ROWS:MSG, :] = jnp.concatenate(rows, axis=0).astype(BF)
    out[MSG:, :] = lat[...]


def pair_kernel(own, near, out):
    out[:EDGE_ROWS, :] = own[:EDGE_ROWS, :]
    out[EDGE_ROWS:, :] = (own[EDGE_ROWS:MSG, :].astype(F32) + near[EDGE_ROWS:MSG, :].astype(F32)).astype(BF)


def line_kernel(near, lat, corner, across):
    across[:LAT_ROWS, :] = lat[...]
    across[LAT_ROWS:, :] = (near[MSG:, :].astype(F32) + corner[...].astype(F32)).astype(BF)


def beside_kernel(across, out):
    out[...] = across[LAT_ROWS:, :]


def total_kernel(parts, out):
    total = parts[0].astype(F32)
    for i in range(1, parts.shape[0]):
        total = total + parts[i].astype(F32)
    total = total.astype(BF)
    for i in range(out.shape[0]):
        out[i] = total


def middle_kernel(pair, near, far, base_x, base_d, lat, corner, place, out_x, out_d, out_lat, out_near):
    edge = jnp.where(core_is(1, 3 * CUT), near[: 3 * CUT, :].astype(F32), far[: 3 * CUT, :].astype(F32))
    adds = [nn(place[...], e.astype(BF)) for e in unfold(edge, CUT)]
    for add, base, out in ((adds[0], base_x, out_x), (adds[1], base_d, out_d)):
        out[...] = (base[...].astype(F32) + add[:N_OWN]).astype(BF)
    whole = lat[...].astype(F32) + fold(adds[0][N_OWN:], adds[1][N_OWN:])
    out_lat[LAT_ROWS:, :] = jnp.zeros((16, 128), BF)
    out_lat[:LAT_ROWS, :] = jnp.where(band_is(False, LAT_ROWS), corner[...].astype(F32), whole).astype(BF)
    out_near[...] = (pair[EDGE_ROWS:, :].astype(F32) + far[EDGE_ROWS:, :].astype(F32)).astype(BF)


def finish_kernel(base_x, base_d, lat, across, beside, near, own, out_x, out_d, out_t):
    got = lat[:LAT_ROWS, :].astype(F32) + across[:LAT_ROWS, :].astype(F32) + beside[...].astype(F32)
    for add, base, out in zip(unfold(got, N_LAT), (base_x, base_d), (out_x, out_d)):
        out[:, HALF_LAT:] = base[:, HALF_LAT:]
        add = add.reshape(WPL, HALF_LAT, COLS, C)
        out[:, :HALF_LAT] = (base[:, :HALF_LAT].astype(F32) + add).astype(BF)
    t = jnp.where(core_is(1, TAB_ROWS), near[...].astype(F32), own[...].astype(F32))
    for part in range(HI):
        width = min(128, NPOS - part * 128)
        for head in range(HEADS):
            row = head * HI + part
            out_t[head, :, part * 128 : part * 128 + width] = t[row : row + 1, :width]


def unpack_kernel(g, scale, qkv, proj, gain):
    k = scale
    full = [g[C * i : C * (i + 1), :].astype(F32) * k for i in range(6)]
    qkv[:, 0:128] = full[0]
    qkv[:, 128:256] = jnp.concatenate([full[4][:, :64], full[1][:, :64]], axis=1)
    qkv[:, 256:384] = jnp.concatenate([full[1][:, 64:], full[4][:, 64:]], axis=1)
    qkv[:, 384:512] = full[2]
    qkv[:, 512:576] = full[5][:, :64]
    proj[:, 0:128] = full[3]
    proj[:, 128:192] = full[5][:, 64:]
    tail = g[6 * C : 6 * C + 16, :].astype(F32) * k
    gain[:, :128] = tail[0:1]
    gain[:, 128:] = tail[1:2, : C - 128]


def call(kernel, out_shape, *args, scratch=(), cost=(0, 0), vmem=8):
    return pl.pallas_call(
        kernel,
        out_shape=out_shape,
        scratch_shapes=list(scratch),
        compiler_params=pltpu.CompilerParams(vmem_limit_bytes=vmem * 2**20),
        cost_estimate=pl.CostEstimate(flops=cost[0], bytes_accessed=cost[1], transcendentals=0),
    )(*args)


def sds(shape, dtype):
    return jax.ShapeDtypeStruct(shape, dtype)


def make(sizes):
    n_lat = sizes[0] * sizes[1] * sizes[2]
    n_lon = sizes[3] * sizes[4]
    n_plane = sizes[0] * sizes[2] * sizes[4]
    n_line = sizes[1] * sizes[3]
    piece = G_ROWS // n_plane
    band = sizes[1] * sizes[2]

    def route(d_lat, d_lon):
        return [
            (a * n_lon + b, (a + d_lat) % n_lat * n_lon + (b + d_lon) % n_lon)
            for a in range(n_lat)
            for b in range(n_lon)
        ]

    def first(pair):
        return pair[0] // n_lon % band == 0

    def last(pair):
        return pair[0] // n_lon % band == band - 1

    def hop(to, cores):
        return [
            (a * n_lon + zh * sizes[4] + c, a * n_lon + to(zh, c)[0] * sizes[4] + to(zh, c)[1])
            for a in range(n_lat)
            for zh in range(sizes[3])
            for c in cores
        ]

    def per_device(tokens, mask_ids, pos_index, norm_gain, w_qkv, w_proj, earth_bias, d_out):
        pick, back, place = (jnp.asarray(c) for c in constants())
        to_core, lat, to_lon, to_diag = call(
            cut_kernel,
            (
                sds((LAT_ROWS, 128), BF),
                sds((LAT_ROWS, 128), BF),
                sds((CORNER_ROWS, 128), BF),
                sds((CORNER_ROWS, 128), BF),
            ),
            tokens,
            d_out,
        )
        sibling = lax.ppermute(to_core, AXES, hop(lambda zh, c: (zh, 1 - c), (0, 1)))
        to_lat = call(join_kernel, sds((LAT_ROWS + CORNER_ROWS, 128), BF), lat, sibling)
        from_lat = lax.ppermute(to_lat, AXES, route(-1, 0))
        to_lat, to_lon, to_diag = lax.optimization_barrier((to_lat, to_lon, to_diag))
        to_lon, to_diag = call(border_kernel, (sds((CORNER_ROWS, 128), BF), sds((CORNER_ROWS, 128), BF)), to_lon, to_diag, cost=(10**10, 10**6))
        from_lon = lax.ppermute(to_lon, AXES, hop(lambda zh, c: (1 - zh, 1), (0,)))
        from_diag = lax.ppermute(to_diag, AXES, [r for r in route(-1, -1) if r[0] % sizes[4] == 0])
        bias, hi, lo = call(
            tables_kernel,
            (sds((WIN, PAIRS), F32), sds((WIN, 256), jnp.int32), sds((WIN, 256), jnp.int32)),
            pos_index,
            earth_bias.transpose(1, 0, 2),
            scratch=[pltpu.VMEM((HEADS // 2, HI * 128), jnp.int32)],
            cost=(6 * 10**9, 10**6),
        )
        from_lat, bias = lax.optimization_barrier((from_lat, bias))
        from_lon, from_diag, bias = lax.optimization_barrier((from_lon, from_diag, bias))
        base_x, base_d, out_lat, out_corner, out_edge, grads, d_bias = call(
            block_kernel,
            (
                sds((N_OWN, C), BF),
                sds((N_OWN, C), BF),
                sds((LAT_ROWS, 128), BF),
                sds((LAT_ROWS, 128), BF),
                sds((EDGE_ROWS, 128), BF),
                sds((G_ROWS, 128), BF),
                sds((WIN, PAIRS), F32),
            ),
            tokens.reshape(N_OWN, C),
            d_out.reshape(N_OWN, C),
            sibling,
            from_lon,
            from_lat,
            from_diag,
            pick,
            back,
            norm_gain.reshape(1, C),
            w_qkv,
            w_proj,
            mask_ids.transpose(1, 0, 2),
            bias,
            vmem=20,
            cost=(6 * 10**9, 10**6),
        )
        parts = lax.all_to_all(grads.reshape(n_plane, piece, 128), PLANE, 0, 0)
        own = call(
            scatter_kernel,
            sds((MSG + LAT_ROWS, 128), BF),
            d_bias,
            hi,
            lo,
            out_edge,
            out_lat,
            scratch=[pltpu.VMEM((HEADS * HIP, 128), F32)],
            cost=(8 * 10**9, 10**6),
        )
        parts, own = lax.optimization_barrier((parts, own))
        near = lax.ppermute(own, AXES, hop(lambda zh, c: (zh, 1 - c), (0, 1)))
        part = call(total_kernel, sds((n_line, piece, 128), BF), parts, cost=(10**9, 10**6))
        line = lax.all_to_all(part, LINE, 0, 0)
        pair = call(pair_kernel, sds((MSG, 128), BF), own, near, cost=(10**9, 10**6))
        far = lax.ppermute(pair, AXES, hop(lambda zh, c: (1 - zh, 0), (1,)))
        across = call(line_kernel, sds((2 * LAT_ROWS, 128), BF), near, out_lat, out_corner, cost=(10**9, 10**6))
        across = lax.ppermute(across, AXES, [r for r in route(1, 0) if last(r) and r[0] % sizes[4] == 0])
        line, pair = lax.optimization_barrier((line, pair))
        total = call(total_kernel, sds((n_plane, piece, 128), BF), line, cost=(10**9, 10**6))
        whole = lax.all_to_all(total, PLANE, 0, 0)
        base_x, base_d, to_lat, to_near = call(
            middle_kernel,
            (
                sds((N_OWN, C), BF),
                sds((N_OWN, C), BF),
                sds((LAT_ROWS + 16, 128), BF),
                sds((TAB_ROWS, 128), BF),
            ),
            pair,
            near,
            far,
            base_x,
            base_d,
            out_lat,
            out_corner,
            place,
            cost=(20 * 10**9, 10**6),
        )
        corners = [r for r in route(1, 1) if last(r) and r[0] % sizes[4] == 1]
        from_lat = lax.ppermute(to_lat, AXES, [r for r in route(1, 0) if not last(r)] + corners)
        from_near = lax.ppermute(to_near, AXES, hop(lambda zh, c: (zh, 1), (0,)))
        across, from_near = lax.optimization_barrier((across, from_near))
        beside = call(beside_kernel, sds((LAT_ROWS, 128), BF), across, cost=(10**9, 10**6))
        beside = lax.ppermute(beside, AXES, [r for r in hop(lambda zh, c: (zh, 1), (0,)) if first(r)])
        updated, d_tokens, d_table = call(
            finish_kernel,
            (
                sds((WPL, ROWS, COLS, C), BF),
                sds((WPL, ROWS, COLS, C), BF),
                sds((HEADS, 1, NPOS), F32),
            ),
            base_x.reshape(WPL, ROWS, COLS, C),
            base_d.reshape(WPL, ROWS, COLS, C),
            from_lat,
            across,
            beside,
            from_near,
            to_near,
            cost=(10**8, 10**5),
        )
        whole, updated = lax.optimization_barrier((whole, updated))
        scale = float(n_lat * n_lon * N_OWN) ** -0.5
        qkv, proj, gain = call(
            lambda g, a, b, c: unpack_kernel(g, scale, a, b, c),
            (sds((C, 3 * C), F32), sds((C, C), F32), sds((1, C), F32)),
            whole.reshape(G_ROWS, 128),
        )
        return updated, d_tokens, qkv, proj, gain.reshape(C), d_table.transpose(1, 0, 2)

    return per_device


def solution(mesh):
    fine = jax.sharding.Mesh(mesh.devices.reshape(SPLIT), AXES)
    placed = (
        P(None, LAT_AXES, LON_AXES, None),
        P(None, LAT_AXES, LON_AXES),
        P(),
        P(),
        P(),
        P(),
        P(LAT_AXES, None, None),
        P(None, LAT_AXES, LON_AXES, None),
    )
    return jax.shard_map(
        make(SPLIT),
        mesh=fine,
        in_specs=placed,
        out_specs=(
            P(None, LAT_AXES, LON_AXES, None),
            P(None, LAT_AXES, LON_AXES, None),
            P(),
            P(),
            P(),
            P(LAT_AXES, None, None),
        ),
        check_vma=False,
    )
```

```python
import jax
import jax.numpy as jnp
import numpy as np
from jax import lax
from jax.experimental import pallas as pl
from jax.experimental.pallas import tpu as pltpu
from jax.sharding import PartitionSpec as P

BF = jnp.bfloat16
F32 = jnp.float32

WPL, WLAT, WLON = 2, 6, 12
HALF_LAT, HALF_LON = WLAT // 2, WLON // 2
ROWS, COLS = 6, 24
C = 192
HEADS = 6
HEAD = C // HEADS
WIN = WPL * WLAT * WLON
WINDOWS = COLS // WLON
NPOS = 3312
HI = -(-NPOS // 128)
HIP = 32
EDGE = 8
N_OWN = WPL * ROWS * COLS
N_LAT = WPL * HALF_LAT * COLS
N_EDGE = WPL * HALF_LAT * EDGE
N_ALL = N_OWN + N_LAT + 2 * N_EDGE
MAIN = 128
REST = WIN - MAIN
PAIRS = HEADS * MAIN + 128
EPS = 1e-05
SCALE = HEAD**-0.5
NEG = -1000000000.0
G_ROWS = 1280
CUT = WPL * ROWS * HALF_LON
EDGE_ROWS = 3 * CUT + 8
TAB_ROWS = 160
MSG = EDGE_ROWS + TAB_ROWS
LAT_ROWS = 3 * N_LAT
CORNER_ROWS = 3 * N_EDGE
SIDE_ROWS = 2 * CORNER_ROWS
LINE_ROWS = 2 * LAT_ROWS + CORNER_ROWS

SPLIT = (4, 8, 4, 2, 2)
AXES = ("x", "zl", "y", "zh", "c")
LAT_AXES = ("x", "zl", "y")
LON_AXES = ("zh", "c")
PLANE = ("x", "y", "c")
LINE = ("zh", "zl")


N_BACK = N_OWN + 2 * N_LAT + CUT


def source_rows():
    at = np.zeros((WINDOWS, WIN), np.int32)
    for level in range(WPL):
        for row in range(ROWS):
            for col in range(COLS):
                from_level = (level + WPL // 2) % WPL
                r, c = row + HALF_LAT, col + HALF_LON
                if r < ROWS and c < COLS:
                    src = from_level * ROWS * COLS + r * COLS + c
                elif c < COLS:
                    src = N_OWN + from_level * HALF_LAT * COLS + (r - ROWS) * COLS + c
                elif r < ROWS:
                    src = N_OWN + N_LAT + from_level * HALF_LAT * EDGE + (r - HALF_LAT) * EDGE + c - COLS
                else:
                    src = N_OWN + N_LAT + N_EDGE + from_level * HALF_LAT * EDGE + (r - ROWS) * EDGE + c - COLS
                at[col // WLON, level * WLAT * WLON + row * WLON + col % WLON] = src
    return at


def constants():
    at = source_rows()
    pick = np.zeros((WINDOWS, WIN, N_ALL), np.float32)
    for w in range(WINDOWS):
        pick[w, np.arange(WIN), at[w]] = 1.0
    back = np.zeros((WINDOWS, N_BACK, WIN), np.float32)
    back[:, : N_OWN + N_LAT] = pick.transpose(0, 2, 1)[:, : N_OWN + N_LAT]
    place = np.zeros((N_OWN + N_LAT, CUT), np.float32)
    for level in range(WPL):
        for row in range(ROWS):
            for col in range(HALF_LON):
                edge = N_OWN + N_LAT + level * HALF_LAT * EDGE + (row % HALF_LAT) * EDGE + col
                edge += 0 if row >= HALF_LAT else N_EDGE
                to = level * ROWS * HALF_LON + row * HALF_LON + col
                back[:, N_OWN + N_LAT + to] = pick[:, :, edge]
                if row >= HALF_LAT:
                    place[level * ROWS * COLS + row * COLS + col, to] = 1.0
                else:
                    at_lat = level * HALF_LAT * COLS + row * COLS + col
                    place[N_OWN + at_lat, to] = 1.0
                    back[:, N_OWN + N_LAT + CUT + at_lat] = pick[:, :, edge]
    return pick.astype(BF), back.astype(BF), place.astype(BF)


def dot(a, b, dims):
    return lax.dot_general(a, b, ((dims[:1], dims[1:]), ((), ())), preferred_element_type=F32)


def nn(a, b):
    return dot(a, b, (1, 0))


def nt(a, b):
    return dot(a, b, (1, 1))


def eye(n):
    return (lax.broadcasted_iota(jnp.int32, (n, n), 0) == lax.broadcasted_iota(jnp.int32, (n, n), 1)).astype(F32).astype(BF)


def spread():
    lane = lax.broadcasted_iota(jnp.int32, (256, WIN), 0)
    query = lax.broadcasted_iota(jnp.int32, (256, WIN), 1)
    held = jnp.where(lane < MAIN, lane, MAIN + lax.bitwise_and(lane, REST - 1))
    return ((held == query) & (lane < MAIN + HEADS * REST)).astype(F32).astype(BF)


def fold(a, b):
    return jnp.concatenate([a[:, :128], b[:, :128], jnp.concatenate([a[:, 128:], b[:, 128:]], axis=1)], axis=0)


def unfold(both, n):
    return [
        jnp.concatenate([both[n * i : n * (i + 1)], both[2 * n : 3 * n, 64 * i : 64 * (i + 1)]], axis=1) for i in range(2)
    ]


def core_is(core, rows):
    return lax.broadcasted_iota(jnp.int32, (rows, 128), 0) * 0 + lax.axis_index("c") == core


def band_is(first, rows):
    at = lax.axis_index("zl") * lax.axis_size("y") + lax.axis_index("y")
    want = 0 if first else lax.axis_size("zl") * lax.axis_size("y") - 1
    return lax.broadcasted_iota(jnp.int32, (rows, 128), 0) * 0 + at == want


def cut_kernel(tokens, d_out, to_core, lat, to_lon, to_diag):
    both = (tokens[...].astype(F32), d_out[...].astype(F32))
    top = fold(*(a[:, :HALF_LAT].reshape(N_LAT, C) for a in both))
    corner = fold(*(a[:, :HALF_LAT, :EDGE].reshape(N_EDGE, C) for a in both))
    lon = fold(*(a[:, HALF_LAT:, :EDGE].reshape(N_EDGE, C) for a in both))
    side = jnp.concatenate([corner, lon], axis=0)
    lat[...] = top.astype(BF)
    to_lon[...] = lon.astype(BF)
    to_diag[...] = corner.astype(BF)
    spare = jnp.zeros((LAT_ROWS - SIDE_ROWS, 128), F32)
    to_core[...] = jnp.where(core_is(1, LAT_ROWS), jnp.concatenate([side, spare], axis=0), top).astype(BF)


def join_kernel(lat, corner, sibling, to_lat, to_line):
    to_lat[:LAT_ROWS, :] = lat[...]
    to_lat[LAT_ROWS:, :] = sibling[:CORNER_ROWS, :]
    to_line[:LAT_ROWS, :] = lat[...]
    to_line[LAT_ROWS : 2 * LAT_ROWS, :] = sibling[...]
    to_line[2 * LAT_ROWS :, :] = corner[...]


def tables_kernel(pos, table, bias, hi_out, lo_out, scr):
    one = eye(WIN)
    idx = pos[...]
    hi = lax.shift_right_logical(idx, 7)
    lo = lax.bitwise_and(idx, 127)
    sp = spread()
    hi2 = nt(nt(one, hi.astype(F32).astype(BF)).astype(BF), sp)
    lo2 = nt(nt(one, lo.astype(F32).astype(BF)).astype(BF), sp)
    hi2 = hi2.astype(jnp.int32)
    lo2 = lo2.astype(jnp.int32)
    hi_out[...] = hi2
    lo_out[...] = lo2

    steps = []
    for pair in range(HEADS // 2):
        words = []
        for head in (2 * pair, 2 * pair + 1):
            row = table[head]
            unit = jnp.maximum(jnp.max(jnp.abs(row), axis=1, keepdims=True), 1e-20) * (1.0 / 32767.0)
            fixed = row * (1.0 / unit)
            fixed = jnp.floor(jnp.clip(fixed + 0.5, -32767.0, 32767.0)).astype(jnp.int32)
            steps.append(unit)
            words.append(fixed)
        scr[pair : pair + 1, :NPOS] = lax.shift_left(words[0], 16) | lax.bitwise_and(words[1], 65535)
    scr[:, NPOS:] = jnp.zeros((HEADS // 2, HI * 128 - NPOS), jnp.int32)

    def look(h_idx, l_idx):
        acc = [[jnp.zeros((8, 128), jnp.int32) for _ in h_idx] for _ in range(HEADS // 2)]
        for part in range(HI):
            hit = [h == part for h in h_idx]
            for pair in range(HEADS // 2):
                row = jnp.broadcast_to(scr[pair : pair + 1, part * 128 : part * 128 + 128], (8, 128))
                for i, l in enumerate(l_idx):
                    got = jnp.take_along_axis(row, l, axis=1, mode="promise_in_bounds")
                    acc[pair][i] = jnp.where(hit[i], got, acc[pair][i])
        out = []
        for pair in range(HEADS // 2):
            high = [lax.shift_right_arithmetic(v, 16) for v in acc[pair]]
            low = [lax.shift_right_arithmetic(lax.shift_left(v, 16), 16) for v in acc[pair]]
            out.append([v.astype(F32) * steps[2 * pair] for v in high])
            out.append([v.astype(F32) * steps[2 * pair + 1] for v in low])
        return out

    def step(block, carry):
        rows = [pl.ds(pl.multiple_of(block * 24 + 8 * i, 8), 8) for i in range(3)]
        acc = look([hi_out[r, :128] for r in rows], [lo_out[r, :128] for r in rows])
        for head in range(HEADS):
            for i, r in enumerate(rows):
                bias[r, MAIN * head : MAIN * (head + 1)] = acc[head][i]
        return carry

    lax.fori_loop(0, WIN // 24, step, 0)
    pad = jnp.zeros((REST, 256 - WIN), jnp.int32)
    h_rest = jnp.concatenate([hi[MAIN:], pad], axis=1)
    l_rest = jnp.concatenate([lo[MAIN:], pad], axis=1)
    tiles = [(slice(8 * i, 8 * i + 8), slice(128 * j, 128 * j + 128)) for i in range(2) for j in range(2)]
    acc = look([h_rest[t] for t in tiles], [l_rest[t] for t in tiles])
    rest = [jnp.concatenate([jnp.concatenate(a[2 * i : 2 * i + 2], axis=1) for i in range(2)], axis=0) for a in acc]
    rest = jnp.concatenate(rest + [jnp.zeros((128 - HEADS * REST, 256), F32)], axis=0)
    bias[:, HEADS * MAIN :] = rest.T[:WIN]


def by_head(x):
    lane = lax.broadcasted_iota(jnp.int32, (1, C), 1)
    keep = [((lane >= HEAD * h) & (lane < HEAD * (h + 1))).astype(F32).astype(BF) for h in range(HEADS)]
    parts = [x[:MAIN] * keep[h] for h in range(HEADS)]
    parts += [x[MAIN:] * keep[h] for h in range(HEADS)]
    parts.append(jnp.zeros((PAIRS - HEADS * WIN, C), BF))
    return jnp.concatenate(parts, axis=0)


def heads_apart(left, right, scale):
    main = [
        nn(left[HEAD * h : HEAD * (h + 1)], right[:, MAIN * h : MAIN * (h + 1)]) for h in range(HEADS)
    ]
    main = (jnp.concatenate(main, axis=0) * scale).astype(BF)
    rest = nn(left, right[:, HEADS * MAIN :]) * scale
    row = lax.broadcasted_iota(jnp.int32, (C, 128), 0)
    lane = lax.broadcasted_iota(jnp.int32, (C, 128), 1)
    rest = jnp.where(lax.div(row, HEAD) == lax.div(lane, REST), rest, 0.0).astype(BF)
    fold_l = lax.broadcasted_iota(jnp.int32, (128, REST), 0)
    fold_a = lax.broadcasted_iota(jnp.int32, (128, REST), 1)
    fold = (lax.rem(fold_l, REST) == fold_a).astype(F32).astype(BF)
    rest = nn(rest, fold).astype(BF)
    return jnp.concatenate([main, rest], axis=1)


def regions(mask):
    sp = spread()
    out = []
    lab = [mask[row, level : level + 1, :].astype(F32) for level in range(WPL) for row in range(ROWS)]
    lab = jnp.concatenate(lab, axis=0).astype(BF)
    for w in range(WINDOWS):
        lane = lax.broadcasted_iota(jnp.int32, (COLS, WIN), 1)
        col = lax.broadcasted_iota(jnp.int32, (COLS, WIN), 0)
        across = (lax.rem(lane, WLON) + w * WLON == col).astype(F32).astype(BF)
        wide = nn(lab, across)
        r = lax.broadcasted_iota(jnp.int32, (WPL * ROWS, WIN), 0)
        a = lax.broadcasted_iota(jnp.int32, (WPL * ROWS, WIN), 1)
        row = jnp.sum(jnp.where(lax.div(a, WLON) == r, wide, 0.0), axis=0, keepdims=True)
        row = jnp.broadcast_to(row, (WIN, WIN)).astype(BF)
        down = nt(eye(WIN), row)
        over = nt(row, sp)
        out.append(jnp.where(over == jnp.broadcast_to(down[:, :1], (WIN, 256)), 0.0, NEG))
    return out


def block_kernel(
    own_x, own_d, sibling, from_lon, from_lat, from_line, from_side, from_diag, pick, back, gain, w_qkv, wp, mask, bias,
    base_x, base_d, out_lat, out_corner, out_edge, grads, d_bias,
):
    f32 = lambda ref, start, size: ref[start : start + size, :].astype(F32)
    over = f32(from_line, 0, LAT_ROWS) + f32(from_side, LAT_ROWS, LAT_ROWS)
    lat = unfold(jnp.where(band_is(False, LAT_ROWS), over, f32(from_lat, 0, LAT_ROWS)), N_LAT)
    lon = f32(sibling, CORNER_ROWS, CORNER_ROWS), f32(from_lon, 0, CORNER_ROWS)
    lon = unfold(jnp.where(core_is(0, CORNER_ROWS), *lon), N_EDGE)
    inner = jnp.where(
        band_is(False, CORNER_ROWS), f32(from_side, 2 * LAT_ROWS, CORNER_ROWS), f32(from_lat, LAT_ROWS, CORNER_ROWS)
    )
    diag = unfold(jnp.where(core_is(0, CORNER_ROWS), inner, f32(from_diag, 0, CORNER_ROWS)), N_EDGE)
    x_all, d_all = (
        jnp.concatenate([own[...], lat[i].astype(BF), lon[i].astype(BF), diag[i].astype(BF)], axis=0)
        for i, own in enumerate((own_x, own_d))
    )
    eye_c = eye(C)
    eye_w = eye(WIN)
    g = jnp.sum(eye_c.astype(F32) * gain[...], axis=1, keepdims=True)
    w3 = [w_qkv[:, C * i : C * (i + 1)] for i in range(3)]
    w3t = [None] + [nt(eye_c, w).astype(BF) for w in w3[1:]]
    wpt = nt(eye_c, wp[...]).astype(BF)
    blocked = regions(mask)
    sums = [jnp.zeros((C, C), F32) for _ in range(4)]
    d_gain = jnp.zeros((C, 1), F32)
    x_back = jnp.zeros((N_BACK, C), F32)
    d_back = jnp.zeros((N_BACK, C), F32)
    for w in range(WINDOWS):
        x = nn(pick[w], x_all).astype(BF)
        d_proj = nn(pick[w], d_all).astype(BF)
        xt = nt(eye_c, x)
        mean = jnp.sum(xt, axis=0, keepdims=True) * (1.0 / C)
        centered = xt - mean
        var = jnp.sum(centered * centered, axis=0, keepdims=True) * (1.0 / C)
        rstd = lax.rsqrt(var + EPS)
        xhat = centered * rstd
        nt_w = (xhat * g).astype(BF)
        n_w = nt(eye_w, nt_w).astype(BF)
        q = nn(n_w, w3[0]).astype(BF)
        k = nn(n_w, w3[1]).astype(BF)
        v = nn(n_w, w3[2]).astype(BF)
        kt = nn(w3t[1], nt_w).astype(BF)
        vt = nn(w3t[2], nt_w).astype(BF)
        qm = by_head(q)
        dm = by_head(nt(d_proj, wp[...]).astype(BF))
        far = jnp.concatenate([blocked[w][:, :MAIN]] * HEADS + [blocked[w][:, MAIN:]], axis=1)
        s = nt(k, qm) * SCALE + bias[...] + far
        e = jnp.exp(s - jnp.max(s, axis=0, keepdims=True))
        p = e * (1.0 / jnp.sum(e, axis=0, keepdims=True))
        attn = p.astype(BF)
        d_attn = nt(v, dm)
        pd = p * d_attn
        ds = pd - p * jnp.sum(pd, axis=0, keepdims=True)
        dsb = ds.astype(BF)
        if w == 0:
            d_bias[...] = ds
        else:
            d_bias[...] += ds
        mixed_t = heads_apart(vt, attn, 1.0)
        dq_t = heads_apart(kt, dsb, SCALE)
        dk = (nn(dsb, qm) * SCALE).astype(BF)
        dv = nn(attn, dm).astype(BF)
        proj_t = nn(wpt, mixed_t).astype(BF)
        x_back = x_back + nt(back[w], proj_t)
        sums[0] = sums[0] + nt(nt_w, dq_t)
        sums[1] = sums[1] + nn(nt_w, dk)
        sums[2] = sums[2] + nn(nt_w, dv)
        sums[3] = sums[3] + nn(mixed_t, d_proj)
        dn = nn(w3[0], dq_t) + nt(w3[1], dk) + nt(w3[2], dv)
        dn = dn.astype(BF).astype(F32)
        d_gain = d_gain + jnp.sum(dn * xhat, axis=1, keepdims=True)
        dy = dn * g
        m1 = jnp.sum(dy, axis=0, keepdims=True) * (1.0 / C)
        m2 = jnp.sum(dy * xhat, axis=0, keepdims=True) * (1.0 / C)
        dx = (rstd * (dy - m1 - xhat * m2)).astype(BF)
        d_back = d_back + nt(back[w], dx)
    for i in range(4):
        grads[C * i : C * (i + 1), :] = sums[i][:, :128].astype(BF)
    for i in range(2):
        pair = jnp.concatenate([sums[2 * i][:, 128:], sums[2 * i + 1][:, 128:]], axis=1)
        grads[C * (4 + i) : C * (5 + i), :] = pair.astype(BF)
    row = jnp.sum(eye_c.astype(F32) * d_gain, axis=0, keepdims=True)
    tail = jnp.concatenate([row[:, 128:], jnp.zeros((1, 256 - C), F32)], axis=1)
    grads[6 * C :, :] = jnp.concatenate([row[:, :128], tail, jnp.zeros((126, 128), F32)], axis=0).astype(BF)
    for i, (total, own, base) in enumerate(((x_back, own_x, base_x), (d_back, own_d, base_d))):
        base[...] = (own[...].astype(F32) + total[:N_OWN]).astype(BF)
    parts = ((out_lat, N_OWN, N_LAT), (out_edge, N_OWN + N_LAT, CUT), (out_corner, N_OWN + N_LAT + CUT, N_LAT))
    for out, start, size in parts:
        both = fold(x_back[start : start + size], d_back[start : start + size])
        spare = out.shape[0] - both.shape[0]
        if spare:
            both = jnp.concatenate([both, jnp.zeros((spare, 128), F32)], axis=0)
        out[...] = both.astype(BF)


def scatter_kernel(d_bias, hi, lo, edge, lat, out, acc):
    acc[...] = jnp.zeros_like(acc)

    def step(block, carry):
        rows = pl.ds(pl.multiple_of(block * 8, 8), 8)
        h_all = hi[rows, :]
        l_all = lo[rows, :]
        d_all = d_bias[rows, :]
        part = lax.broadcasted_iota(jnp.int32, (HIP, 256), 0)
        group = lax.shift_right_logical(lax.broadcasted_iota(jnp.int32, (HIP, 128), 1), 4)
        place = lax.broadcasted_iota(jnp.int32, (128, 256), 0)
        total = acc[...]
        for i in range(8):
            hit = jnp.broadcast_to(h_all[i : i + 1], (HIP, 256)) == part
            rest = jnp.broadcast_to(d_all[i : i + 1, HEADS * MAIN :], (HIP, 128))
            rest = jnp.where(hit[:, 128:], rest, 0.0)
            many = []
            for head in range(HEADS):
                main = jnp.broadcast_to(d_all[i : i + 1, MAIN * head : MAIN * (head + 1)], (HIP, 128))
                main = jnp.where(hit[:, :128], main, 0.0)
                many.append(jnp.concatenate([main, jnp.where(group == head, rest, 0.0)], axis=1))
            many = jnp.concatenate(many, axis=0).astype(BF)
            spot = (jnp.broadcast_to(l_all[i : i + 1], (128, 256)) == place).astype(F32).astype(BF)
            total = total + nt(many, spot)
        acc[...] = total
        return carry

    lax.fori_loop(0, WIN // 8, step, 0)
    out[:EDGE_ROWS, :] = edge[...]
    rows = [acc[HIP * h : HIP * h + HI] for h in range(HEADS)] + [jnp.zeros((TAB_ROWS - HEADS * HI, 128), F32)]
    out[EDGE_ROWS:MSG, :] = jnp.concatenate(rows, axis=0).astype(BF)
    out[MSG:, :] = lat[...]


def pair_kernel(own, near, out):
    out[:EDGE_ROWS, :] = own[:EDGE_ROWS, :]
    out[EDGE_ROWS:, :] = (own[EDGE_ROWS:MSG, :].astype(F32) + near[EDGE_ROWS:MSG, :].astype(F32)).astype(BF)


def line_kernel(near, lat, corner, across):
    across[:LAT_ROWS, :] = lat[...]
    across[LAT_ROWS:, :] = (near[MSG:, :].astype(F32) + corner[...].astype(F32)).astype(BF)


def beside_kernel(across, out):
    out[...] = across[LAT_ROWS:, :]


def total_kernel(parts, out):
    total = parts[0].astype(F32)
    for i in range(1, parts.shape[0]):
        total = total + parts[i].astype(F32)
    total = total.astype(BF)
    for i in range(out.shape[0]):
        out[i] = total


def middle_kernel(pair, near, far, base_x, base_d, lat, corner, place, out_x, out_d, out_lat, out_near):
    edge = jnp.where(core_is(1, 3 * CUT), near[: 3 * CUT, :].astype(F32), far[: 3 * CUT, :].astype(F32))
    adds = [nn(place[...], e.astype(BF)) for e in unfold(edge, CUT)]
    for add, base, out in ((adds[0], base_x, out_x), (adds[1], base_d, out_d)):
        out[...] = (base[...].astype(F32) + add[:N_OWN]).astype(BF)
    whole = lat[...].astype(F32) + fold(adds[0][N_OWN:], adds[1][N_OWN:])
    out_lat[LAT_ROWS:, :] = jnp.zeros((16, 128), BF)
    out_lat[:LAT_ROWS, :] = jnp.where(band_is(False, LAT_ROWS), corner[...].astype(F32), whole).astype(BF)
    out_near[...] = (pair[EDGE_ROWS:, :].astype(F32) + far[EDGE_ROWS:, :].astype(F32)).astype(BF)


def finish_kernel(base_x, base_d, lat, across, beside, near, own, out_x, out_d, out_t):
    got = lat[:LAT_ROWS, :].astype(F32) + across[:LAT_ROWS, :].astype(F32) + beside[...].astype(F32)
    for add, base, out in zip(unfold(got, N_LAT), (base_x, base_d), (out_x, out_d)):
        out[:, HALF_LAT:] = base[:, HALF_LAT:]
        add = add.reshape(WPL, HALF_LAT, COLS, C)
        out[:, :HALF_LAT] = (base[:, :HALF_LAT].astype(F32) + add).astype(BF)
    t = jnp.where(core_is(1, TAB_ROWS), near[...].astype(F32), own[...].astype(F32))
    for part in range(HI):
        width = min(128, NPOS - part * 128)
        for head in range(HEADS):
            row = head * HI + part
            out_t[head, :, part * 128 : part * 128 + width] = t[row : row + 1, :width]


def unpack_kernel(g, scale, qkv, proj, gain):
    k = scale
    full = [g[C * i : C * (i + 1), :].astype(F32) * k for i in range(6)]
    qkv[:, 0:128] = full[0]
    qkv[:, 128:256] = jnp.concatenate([full[4][:, :64], full[1][:, :64]], axis=1)
    qkv[:, 256:384] = jnp.concatenate([full[1][:, 64:], full[4][:, 64:]], axis=1)
    qkv[:, 384:512] = full[2]
    qkv[:, 512:576] = full[5][:, :64]
    proj[:, 0:128] = full[3]
    proj[:, 128:192] = full[5][:, 64:]
    tail = g[6 * C : 6 * C + 16, :].astype(F32) * k
    gain[:, :128] = tail[0:1]
    gain[:, 128:] = tail[1:2, : C - 128]


def call(kernel, out_shape, *args, scratch=(), cost=(0, 0), vmem=8):
    return pl.pallas_call(
        kernel,
        out_shape=out_shape,
        scratch_shapes=list(scratch),
        compiler_params=pltpu.CompilerParams(vmem_limit_bytes=vmem * 2**20),
        cost_estimate=pl.CostEstimate(flops=cost[0], bytes_accessed=cost[1], transcendentals=0),
    )(*args)


def sds(shape, dtype):
    return jax.ShapeDtypeStruct(shape, dtype)


def make(sizes):
    n_lat = sizes[0] * sizes[1] * sizes[2]
    n_lon = sizes[3] * sizes[4]
    n_plane = sizes[0] * sizes[2] * sizes[4]
    n_line = sizes[1] * sizes[3]
    piece = G_ROWS // n_plane
    band = sizes[1] * sizes[2]

    def route(d_lat, d_lon):
        return [
            (a * n_lon + b, (a + d_lat) % n_lat * n_lon + (b + d_lon) % n_lon)
            for a in range(n_lat)
            for b in range(n_lon)
        ]

    def first(pair):
        return pair[0] // n_lon % band == 0

    def last(pair):
        return pair[0] // n_lon % band == band - 1

    def hop(to, cores):
        return [
            (a * n_lon + zh * sizes[4] + c, a * n_lon + to(zh, c)[0] * sizes[4] + to(zh, c)[1])
            for a in range(n_lat)
            for zh in range(sizes[3])
            for c in cores
        ]

    def per_device(tokens, mask_ids, pos_index, norm_gain, w_qkv, w_proj, earth_bias, d_out):
        pick, back, place = (jnp.asarray(c) for c in constants())
        to_core, lat, to_lon, to_diag = call(
            cut_kernel,
            (
                sds((LAT_ROWS, 128), BF),
                sds((LAT_ROWS, 128), BF),
                sds((CORNER_ROWS, 128), BF),
                sds((CORNER_ROWS, 128), BF),
            ),
            tokens,
            d_out,
        )
        sibling = lax.ppermute(to_core, AXES, hop(lambda zh, c: (zh, 1 - c), (0, 1)))
        from_lon = lax.ppermute(to_lon, AXES, hop(lambda zh, c: (1 - zh, 1), (0,)))
        from_diag = lax.ppermute(to_diag, AXES, [r for r in route(-1, -1) if r[0] % sizes[4] == 0])
        to_lat, to_line = call(
            join_kernel,
            (sds((LAT_ROWS + CORNER_ROWS, 128), BF), sds((LINE_ROWS, 128), BF)),
            lat,
            to_diag,
            sibling,
        )
        south = route(-1, 0)
        from_lat = lax.ppermute(to_lat, AXES, [r for r in south if not first(r)])
        from_line = lax.ppermute(to_line, AXES, [r for r in south if first(r) and r[0] % sizes[4] == 1])
        bias, hi, lo = call(
            tables_kernel,
            (sds((WIN, PAIRS), F32), sds((WIN, 256), jnp.int32), sds((WIN, 256), jnp.int32)),
            pos_index,
            earth_bias.transpose(1, 0, 2),
            scratch=[pltpu.VMEM((HEADS // 2, HI * 128), jnp.int32)],
            cost=(6 * 10**9, 10**6),
        )
        received = (from_line, from_lon, from_diag, from_lat, bias)
        from_line, from_lon, from_diag, from_lat, bias = lax.optimization_barrier(received)
        from_side = lax.ppermute(from_line, AXES, [r for r in hop(lambda zh, c: (zh, 0), (1,)) if last(r)])
        base_x, base_d, out_lat, out_corner, out_edge, grads, d_bias = call(
            block_kernel,
            (
                sds((N_OWN, C), BF),
                sds((N_OWN, C), BF),
                sds((LAT_ROWS, 128), BF),
                sds((LAT_ROWS, 128), BF),
                sds((EDGE_ROWS, 128), BF),
                sds((G_ROWS, 128), BF),
                sds((WIN, PAIRS), F32),
            ),
            tokens.reshape(N_OWN, C),
            d_out.reshape(N_OWN, C),
            sibling,
            from_lon,
            from_lat,
            from_line,
            from_side,
            from_diag,
            pick,
            back,
            norm_gain.reshape(1, C),
            w_qkv,
            w_proj,
            mask_ids.transpose(1, 0, 2),
            bias,
            vmem=20,
            cost=(6 * 10**9, 10**6),
        )
        parts = lax.all_to_all(grads.reshape(n_plane, piece, 128), PLANE, 0, 0)
        own = call(
            scatter_kernel,
            sds((MSG + LAT_ROWS, 128), BF),
            d_bias,
            hi,
            lo,
            out_edge,
            out_lat,
            scratch=[pltpu.VMEM((HEADS * HIP, 128), F32)],
            cost=(8 * 10**9, 10**6),
        )
        parts, own = lax.optimization_barrier((parts, own))
        near = lax.ppermute(own, AXES, hop(lambda zh, c: (zh, 1 - c), (0, 1)))
        part = call(total_kernel, sds((n_line, piece, 128), BF), parts, cost=(10**9, 10**6))
        line = lax.all_to_all(part, LINE, 0, 0)
        pair = call(pair_kernel, sds((MSG, 128), BF), own, near, cost=(10**9, 10**6))
        far = lax.ppermute(pair, AXES, hop(lambda zh, c: (1 - zh, 0), (1,)))
        across = call(line_kernel, sds((2 * LAT_ROWS, 128), BF), near, out_lat, out_corner, cost=(10**9, 10**6))
        across = lax.ppermute(across, AXES, [r for r in route(1, 0) if last(r) and r[0] % sizes[4] == 0])
        line, pair = lax.optimization_barrier((line, pair))
        total = call(total_kernel, sds((n_plane, piece, 128), BF), line, cost=(10**9, 10**6))
        whole = lax.all_to_all(total, PLANE, 0, 0)
        base_x, base_d, to_lat, to_near = call(
            middle_kernel,
            (
                sds((N_OWN, C), BF),
                sds((N_OWN, C), BF),
                sds((LAT_ROWS + 16, 128), BF),
                sds((TAB_ROWS, 128), BF),
            ),
            pair,
            near,
            far,
            base_x,
            base_d,
            out_lat,
            out_corner,
            place,
            cost=(20 * 10**9, 10**6),
        )
        corners = [r for r in route(1, 1) if last(r) and r[0] % sizes[4] == 1]
        from_lat = lax.ppermute(to_lat, AXES, [r for r in route(1, 0) if not last(r)] + corners)
        from_near = lax.ppermute(to_near, AXES, hop(lambda zh, c: (zh, 1), (0,)))
        across, from_near = lax.optimization_barrier((across, from_near))
        beside = call(beside_kernel, sds((LAT_ROWS, 128), BF), across, cost=(10**9, 10**6))
        beside = lax.ppermute(beside, AXES, [r for r in hop(lambda zh, c: (zh, 1), (0,)) if first(r)])
        scale = float(n_lat * n_lon * N_OWN) ** -0.5
        qkv, proj, gain = call(
            lambda g, a, b, c: unpack_kernel(g, scale, a, b, c),
            (sds((C, 3 * C), F32), sds((C, C), F32), sds((1, C), F32)),
            whole.reshape(G_ROWS, 128),
        )
        base_x, qkv = lax.optimization_barrier((base_x, qkv))
        updated, d_tokens, d_table = call(
            finish_kernel,
            (
                sds((WPL, ROWS, COLS, C), BF),
                sds((WPL, ROWS, COLS, C), BF),
                sds((HEADS, 1, NPOS), F32),
            ),
            base_x.reshape(WPL, ROWS, COLS, C),
            base_d.reshape(WPL, ROWS, COLS, C),
            from_lat,
            across,
            beside,
            from_near,
            to_near,
            cost=(20 * 10**9, 10**6),
        )
        return updated, d_tokens, qkv, proj, gain.reshape(C), d_table.transpose(1, 0, 2)

    return per_device


def solution(mesh):
    fine = jax.sharding.Mesh(mesh.devices.reshape(SPLIT), AXES)
    placed = (
        P(None, LAT_AXES, LON_AXES, None),
        P(None, LAT_AXES, LON_AXES),
        P(),
        P(),
        P(),
        P(),
        P(LAT_AXES, None, None),
        P(None, LAT_AXES, LON_AXES, None),
    )
    return jax.shard_map(
        make(SPLIT),
        mesh=fine,
        in_specs=placed,
        out_specs=(
            P(None, LAT_AXES, LON_AXES, None),
            P(None, LAT_AXES, LON_AXES, None),
            P(),
            P(),
            P(),
            P(LAT_AXES, None, None),
        ),
        check_vma=False,
    )
```
